32 devices in a mesh: dp: 8 (over y, x, core), tensor: 4 (over z).
Axes of the slice: x: 2, y: 2, z: 4, core: 2. Of those that a mesh axis runs over, the one named last changes fastest.
Arguments:
- block_input: bfloat16 [16384, 1536], P('dp'), may hold values from -6 to 6
- segment_ids: int32 [16384], P('dp'), may hold values from 0 to 16383, as said below
- norm_gain: float32 [1536], replicated, may hold values from 0.1 to 1.9
- gate_weight: bfloat16 [1536, 3072], P(None, 'tensor'), may hold values from -0.15625 to 0.15625
- input_weight: bfloat16 [1536, 3072], P(None, 'tensor'), may hold values from -0.15625 to 0.15625
- state_weight: bfloat16 [1536, 256], replicated, may hold values from -0.15625 to 0.15625
- step_weight: bfloat16 [1536, 48], P(None, 'tensor'), may hold values from -0.15625 to 0.15625
- mixer_conv: float32 [4, 3072], P(None, 'tensor'), may hold values from -3 to 3
- mixer_shift: float32 [3072], P('tensor'), may hold values from -3 to 3
- state_conv: float32 [4, 256], replicated, may hold values from -3 to 3
- state_shift: float32 [256], replicated, may hold values from -3 to 3
- step_bias: float32 [48], P('tensor'), may hold values from -6.9 to -2.3
- decay_log: float32 [48], P('tensor'), may hold values from 0 to 2.77
- skip_gain: float32 [48], P('tensor'), may hold values from -4 to 4
- gate_gain: float32 [3072], P('tensor'), may hold values from 0.1 to 1.9
- out_weight: bfloat16 [3072, 1536], P('tensor'), may hold values from -0.109375 to 0.109375
- out_grad: bfloat16 [16384, 1536], P('dp'), may hold values from -6 to 6
Outputs:
- block_output: bfloat16 [16384, 1536], P('dp')
- input_grad: bfloat16 [16384, 1536], P('dp')
- norm_gain_grad: float32 [1536], P('tensor')
- gate_weight_grad: float32 [1536, 3072], P(None, 'tensor')
- input_weight_grad: float32 [1536, 3072], P(None, 'tensor')
- state_weight_grad: float32 [1536, 256], P('tensor')
- step_weight_grad: float32 [1536, 48], P(None, 'tensor')
- mixer_conv_grad: float32 [4, 3072], P(None, 'tensor')
- mixer_shift_grad: float32 [3072], P('tensor')
- state_conv_grad: float32 [4, 256], replicated
- state_shift_grad: float32 [256], replicated
- step_bias_grad: float32 [48], P('tensor')
- decay_log_grad: float32 [48], P('tensor')
- skip_gain_grad: float32 [48], P('tensor')
- gate_gain_grad: float32 [3072], P('tensor')
- out_weight_grad: float32 [3072, 1536], P('tensor')
The draws below stay inside these ranges and needn't reach their ends.
Inputs may be any that keep to these rules, and one draw needn't show every extreme that they name: `segment_ids`: each token's number is the position, in the whole array, of the first token of its document; documents are 200 to 2000 tokens long unless cut at the end of a packed sequence of 2048 tokens, and none crosses such an end.
All inputs are finite; a program needn't handle non-finite values.
Results may differ from the reference program's by a relative error of at most 0.024.
Values may be sent and summed in bfloat16 or wider, within the bound.
No kernel may reach another device: no remote copies, remote signals or barrier semaphores. Data moves between devices by JAX's collectives and lax.ppermute only.
A program may use at most 256 MiB of HBM per device.

```python
import jax
import jax.numpy as jnp
from jax import lax

D = 1536
H = 48
N = 128
KCONV = 4
SEQ_LEN = 2048
DOC_MIN = 200
DOC_MAX = 2000
DI = 3072
TOKENS = 16384


def draw_segment_ids(key, part):
    key = jax.random.fold_in(key, 7)
    sequences = TOKENS // SEQ_LEN
    pieces = SEQ_LEN // DOC_MIN + 1
    lengths = jax.random.randint(key, (sequences, pieces), DOC_MIN, DOC_MAX + 1).astype(jnp.int32)
    ends = jnp.cumsum(lengths, axis=1).astype(jnp.int32)
    place = jnp.arange(SEQ_LEN, dtype=jnp.int32)
    which = jnp.sum((ends[:, None, :] <= place[None, :, None]).astype(jnp.int32), axis=2).astype(jnp.int32)
    starts = jnp.concatenate([jnp.zeros((sequences, 1), jnp.int32), ends[:, :-1]], axis=1).astype(jnp.int32)
    first = jnp.take_along_axis(starts, which, axis=1)
    offset = (jnp.arange(sequences, dtype=jnp.int32) * SEQ_LEN)[:, None]
    return (first + offset).astype(jnp.int32).reshape(-1)


def draw_step_bias(key, part):
    key = jax.random.fold_in(key, 11)
    upper = -2.3
    return jax.random.uniform(key, (H,), jnp.float32, -6.9, upper)


def draw_decay_log(key, part):
    key = jax.random.fold_in(key, 13)
    upper = 2.77
    return jax.random.uniform(key, (H,), jnp.float32, 0.0, upper)


def shard_levels(key, shape, cuts, least, high):
    def one(axis_at, parts):
        heights = jax.random.uniform(jax.random.fold_in(jax.random.fold_in(key, 6), axis_at), (parts,), jnp.float32, least / len(cuts), high / len(cuts))
        return jnp.repeat(jnp.exp(heights), shape[axis_at] // parts).reshape((-1,) + (1,) * (len(shape) - axis_at - 1))

    factor_of = one(*cuts[0])
    for cut in cuts[1:]:
        factor_of = factor_of * one(*cut)
    return factor_of


def gaussian(key, dims, deviation, bound, cuts=(), held_as=jnp.bfloat16):
    gain = shard_levels(key, dims, cuts, -0.22, 0.18) if cuts else 1.0
    drawn = jax.random.normal(key, dims, jnp.float32) * deviation * gain
    return jnp.minimum(jnp.maximum(drawn, -bound), bound).astype(held_as)


def setup_inputs(seed: int = 0) -> dict:
    arg_keys = jax.random.split(jax.random.key(seed), 18)
    return {
        "block_input": gaussian(arg_keys[0], (TOKENS, D), 1.0, 6.0, ((0, 8),)),
        "segment_ids": draw_segment_ids(jax.random.fold_in(arg_keys[17], 71), 0),
        "norm_gain": jnp.clip(1.0 + 0.18 * jax.random.normal(arg_keys[2], (D,), jnp.float32), 0.1, 1.9),
        "gate_weight": gaussian(arg_keys[3], (D, DI), D ** -0.5, 0.15625, ((1, 4),)),
        "input_weight": gaussian(arg_keys[4], (D, DI), D ** -0.5, 0.15625, ((1, 4),)),
        "state_weight": gaussian(arg_keys[5], (D, 2 * N), D ** -0.5, 0.15625),
        "step_weight": gaussian(arg_keys[6], (D, H), D ** -0.5, 0.15625, ((1, 4),)),
        "mixer_conv": gaussian(arg_keys[7], (KCONV, DI), KCONV ** -0.5, 3.0, ((1, 4),), jnp.float32),
        "mixer_shift": gaussian(arg_keys[8], (DI,), 0.5, 3.0, ((0, 4),), jnp.float32),
        "state_conv": gaussian(arg_keys[9], (KCONV, 2 * N), KCONV ** -0.5, 3.0, (), jnp.float32),
        "state_shift": gaussian(arg_keys[10], (2 * N,), 0.5, 3.0, (), jnp.float32),
        "step_bias": draw_step_bias(jax.random.fold_in(arg_keys[17], 71), 0),
        "decay_log": draw_decay_log(jax.random.fold_in(arg_keys[17], 71), 0),
        "skip_gain": gaussian(arg_keys[13], (H,), 1.5, 4.0, ((0, 4),), jnp.float32),
        "gate_gain": jnp.clip(1.0 + 0.18 * jax.random.normal(arg_keys[14], (DI,), jnp.float32), 0.1, 1.9),
        "out_weight": gaussian(arg_keys[15], (DI, D), DI ** -0.5, 0.109375, ((0, 4),)),
        "out_grad": gaussian(arg_keys[16], (TOKENS, D), 1.0, 6.0, ((0, 8),)),
    }


epsilon = 1e-05
highest = lax.Precision.HIGHEST

@jax.custom_vjp
def low(v):
    return lax.optimization_barrier(v.astype(jnp.bfloat16)).astype(jnp.float32)

@jax.custom_vjp
def low_back(v):
    return v

def low_keep(v):
    return (low(v), None)

def low_pass(kept, grad):
    return (grad,)

def back_keep(v):
    return (v, None)

def back_low(kept, grad):
    return (low(grad),)
low.defvjp(low_keep, low_pass)
low_back.defvjp(back_keep, back_low)

def product(left, right):
    return jnp.dot(left, right, precision=highest, preferred_element_type=jnp.float32)

def shift_rows(values, offset):
    return jnp.pad(values, ((offset, 0), (0, 0)))[:values.shape[0]]

def shift_segments(segments, offset):
    filler = jnp.full((offset,), -1, jnp.int32)
    return jnp.concatenate([filler, segments[:segments.shape[0] - offset].astype(jnp.int32)])

def causal_conv(values, weight, shift, segments):
    total = shift[None, :] + weight[0][None, :] * values
    for offset in range(1, weight.shape[0]):
        same = (shift_segments(segments, offset) == segments.astype(jnp.int32)).astype(values.dtype)
        total = total + weight[offset][None, :] * shift_rows(values, offset) * same[:, None]
    return total

def state_mix(mixer_in, state_b, state_c, step_size, decay_log, skip_gain, segments):
    length, heads = step_size.shape
    scores = product(state_c, state_b.T)
    place = jnp.arange(length)
    mask = ((place[:, None] >= place[None, :]) & (segments[:, None] == segments[None, :])).astype(scores.dtype)
    rates = -jnp.exp(decay_log)
    levels = jnp.cumsum(step_size * rates[None, :], axis=0)
    values = mixer_in.reshape(length, heads, -1)

    def one_head(item):
        head_values, head_step, head_level = item
        spread = jnp.where(mask > 0, head_level[:, None] - head_level[None, :], 0.0)
        weights = low(scores * jnp.exp(spread) * mask * head_step[None, :])
        return product(weights, head_values)
    mixed = lax.map(jax.checkpoint(one_head), (jnp.moveaxis(values, 1, 0), step_size.T, levels.T))
    mixed = jnp.moveaxis(mixed, 0, 1) + skip_gain[None, :, None] * values
    return mixed.reshape(length, -1)

def block(params, residual, segments):
    norm_gain, gate_weight, input_weight, state_weight, step_weight, mixer_conv, mixer_shift, state_conv, state_shift, step_bias, decay_log, skip_gain, gate_gain, out_weight = params
    inverse_rms = lax.rsqrt(lax.optimization_barrier(jnp.mean(residual * residual, axis=-1, keepdims=True)) + epsilon)
    normed = low(residual * inverse_rms * norm_gain)
    gate_raw = low_back(low(product(normed, gate_weight)))
    mixer_raw = low_back(low(product(normed, input_weight)))
    state_raw = low_back(low(product(normed, state_weight)))
    step_raw = low_back(low(product(normed, step_weight)))
    mixer_in = low(jax.nn.silu(causal_conv(mixer_raw, mixer_conv, mixer_shift, segments)))
    states = low(jax.nn.silu(causal_conv(state_raw, state_conv, state_shift, segments)))
    step_size = jax.nn.softplus(step_raw + step_bias)
    half = states.shape[1] // 2
    mixed = low_back(state_mix(mixer_in, states[:, :half], states[:, half:], step_size, decay_log, skip_gain, segments))
    gated = mixed * jax.nn.silu(gate_raw)
    gate_rms = lax.rsqrt(lax.optimization_barrier(jnp.mean(gated * gated, axis=-1, keepdims=True)) + epsilon)
    gate_out = low(gated * gate_rms * gate_gain)
    return product(gate_out, out_weight) + residual

def reference(block_input, segment_ids, norm_gain, gate_weight, input_weight, state_weight, step_weight, mixer_conv, mixer_shift, state_conv, state_shift, step_bias, decay_log, skip_gain, gate_gain, out_weight, out_grad):
    params = tuple((item.astype(jnp.float32) for item in (norm_gain, gate_weight, input_weight, state_weight, step_weight, mixer_conv, mixer_shift, state_conv, state_shift, step_bias, decay_log, skip_gain, gate_gain, out_weight)))
    width = block_input.shape[1]
    inputs = block_input.astype(jnp.float32).reshape(-1, SEQ_LEN, width)
    cotangent = out_grad.astype(jnp.float32).reshape(-1, SEQ_LEN, width)
    segments = segment_ids.astype(jnp.int32).reshape(-1, SEQ_LEN)

    def forward(weights, rows):

        def per_sequence(item):
            return block(weights, item[0], item[1])
        return lax.map(per_sequence, (rows, segments))
    outputs, pull = jax.vjp(forward, params, inputs)
    grads, input_grads = pull(cotangent)
    return (outputs.reshape(-1, width).astype(jnp.bfloat16), input_grads.reshape(-1, width).astype(jnp.bfloat16), grads[0], grads[1], grads[2], grads[3], grads[4], grads[5], grads[6], grads[7], grads[8], grads[9], grads[10], grads[11], grads[12], grads[13])
```

```python
import functools

import jax
import jax.numpy as jnp
from jax import lax
from jax.experimental import pallas as pl
from jax.experimental.pallas import tpu as pltpu
from jax.sharding import PartitionSpec as P

epsilon = 1e-05
highest = lax.Precision.HIGHEST
f32 = jnp.float32
bf16 = jnp.bfloat16
LOG2E = 1.4426950408889634
CHUNK = 128
LANES = 128
ROWS = 512
VMEM_BYTES = 60 * 1024 * 1024
BRIEF = pl.CostEstimate(flops=1000, bytes_accessed=1000, transcendentals=0)


def dot(left, right, precision=None):
    return lax.dot_general(
        left, right, (((1,), (0,)), ((), ())), precision=precision, preferred_element_type=f32
    )


def dot_nt(left, right):
    return lax.dot_general(left, right, (((1,), (1,)), ((), ())), preferred_element_type=f32)


def dot_tn(left, right):
    return lax.dot_general(left, right, (((0,), (0,)), ((), ())), preferred_element_type=f32)


def sigmoid(values):
    return 0.5 * jnp.tanh(0.5 * values) + 0.5


def softplus(values):
    power = jnp.exp(-jnp.abs(values))
    above = 1.0 + power
    exact = above == 1.0
    tail = jnp.log(above) * (power / jnp.where(exact, 1.0, above - 1.0))
    return jnp.maximum(values, 0.0) + jnp.where(exact, power, tail)


def spread(column):
    return jnp.broadcast_to(column, (column.shape[0], LANES))


def stand(row):
    return jnp.transpose(jnp.broadcast_to(row, (CHUNK, CHUNK)))


def fold(values):
    return jnp.sum(values.reshape(values.shape[0] // 8, 8, values.shape[1]), axis=0)


def halves(values):
    upper = values.astype(bf16)
    lower = (values - upper.astype(f32)).astype(bf16)
    return jnp.concatenate([upper, lower], axis=1)


def place(axis):
    return lax.broadcasted_iota(jnp.int32, (CHUNK, CHUNK), axis)


def low_lanes():
    return place(1) < LANES // 2


def column_step(width):
    return 256 if width % 256 == 0 else 128


def conv_pre(window, taps, lanes, kept):
    total = taps[4:5, lanes] + taps[0:1, lanes] * window[8:]
    for offset in range(1, 4):
        moved = window[8 - offset : 8 - offset + CHUNK]
        total = total + taps[offset : offset + 1, lanes] * (kept[offset - 1] * moved)
    return total


def step_levels(step_raw, heads):
    field = step_raw + heads[0:1, :]
    step = softplus(field)
    tri = (place(0) >= place(1)).astype(f32)
    levels = dot(tri, step * heads[1:2, :], highest)
    return field, step, levels


HBM = pl.BlockSpec(memory_space=pl.ANY)
SMEM = pl.BlockSpec(memory_space=pltpu.SMEM)
ANY = pl.BlockSpec(memory_space=pl.ANY)


def whole(shape):
    return pl.BlockSpec(shape, lambda i: (0,) * len(shape), pipeline_mode=pl.Buffered(1))


def held(shape):
    return pl.BlockSpec(shape, lambda i: (0,) * len(shape))


def wholes(items):
    return [whole(item.shape) for item in items]


def started(pairs, semaphores, first=0):
    copies = []
    for k, (source, target) in enumerate(pairs):
        copy = pltpu.make_async_copy(source, target, semaphores.at[first + k])
        copy.start()
        copies.append(copy)
    return copies


def settle(copies):
    for copy in copies:
        copy.wait()


def line_of(values):
    return values[...].reshape(1, values.shape[0])


def prepare_kernel(
    segments,
    norm_gain,
    mixer_conv,
    mixer_shift,
    state_conv,
    state_shift,
    step_bias,
    decay_log,
    skip_gain,
    gate_gain,
    state_weight,
    step_weight,
    gain,
    marks,
    chan,
    state_chan,
    heads,
    small_weight,
):
    length = segments.shape[0]
    inner = gate_gain.shape[0]
    count = step_bias.shape[0]
    gain[...] = line_of(norm_gain)
    place_line = lax.broadcasted_iota(jnp.int32, (8, length), 1)
    first = lax.axis_index("dp") * length
    start = jnp.broadcast_to(line_of(segments), (8, length)) - first
    left = jnp.zeros((8, length), f32)
    for k in range(1, 4):
        later = pltpu.roll(start, length - k, 1)
        same = (later <= place_line) & (place_line < length - k)
        left += same.astype(f32)
    marks[0:1, :] = start[0:1].astype(f32)
    marks[1:2, :] = left[0:1]
    heads[...] = jnp.zeros_like(heads)
    rates = -jnp.exp(line_of(decay_log))
    heads[0:1, :count] = line_of(step_bias)
    heads[1:2, :count] = rates * LOG2E
    heads[2:3, :count] = rates
    heads[3:4, :count] = line_of(skip_gain)
    chan[...] = jnp.zeros_like(chan)
    chan[0:4, :] = mixer_conv[...]
    chan[4:5, :] = line_of(mixer_shift)
    owner = lax.broadcasted_iota(jnp.int32, (LANES, inner), 0)
    channel = lax.broadcasted_iota(jnp.int32, (LANES, inner), 1)
    owns = (channel // (inner // count) == owner).astype(f32)
    chan[5:6, :] = dot(heads[...], owns, highest)[3:4]
    chan[6:7, :] = line_of(gate_gain)
    state_chan[...] = jnp.zeros_like(state_chan)
    state_chan[0:4, :] = state_conv[...]
    state_chan[4:5, :] = line_of(state_shift)
    small_weight[:, :256] = state_weight[...]
    small_weight[:, 256:] = jnp.zeros((small_weight.shape[0], LANES), bf16)
    small_weight[:, 256 : 256 + count] = step_weight[...]


def prepare(length, width, inner, values):
    shapes = [
        ((1, width), f32),
        ((2, length), f32),
        ((8, inner), f32),
        ((8, 256), f32),
        ((8, LANES), f32),
        ((width, 384), bf16),
    ]
    return pl.pallas_call(
        prepare_kernel,
        grid=(1,),
        in_specs=wholes(values),
        out_specs=[whole(shape) for shape, _ in shapes],
        out_shape=[jax.ShapeDtypeStruct(shape, kind) for shape, kind in shapes],
        compiler_params=pltpu.CompilerParams(vmem_limit_bytes=VMEM_BYTES),
        cost_estimate=BRIEF,
        name="prepare",
    )(*values)


def forward_kernel(
    starts,
    marks,
    tokens_home,
    grads_home,
    input_home,
    gate_home,
    small_home,
    out_home,
    gain,
    chan,
    state_chan,
    heads,
    *rest,
    block,
    first,
    unread,
    project,
):
    if not first:
        state_in, halo_in = rest[:2]
        rest = rest[2:]
    rest = rest[unread:]
    homes, rest = rest[:11], rest[11:]
    (
        partial,
        sums,
        state,
        halo_out,
        tokens,
        grads,
        normed,
        gate_raw,
        mixer_raw,
        small_raw,
        mixer_in,
        slope,
        states,
        state_slope,
        mixed,
        back,
        kept_states,
        raw,
        state_raw,
        gated_low,
        wide_back,
        input_weight,
        gate_weight,
        state_weight,
        out_weight,
        damped,
        carried_out,
        load_sems,
        store_sems,
    ) = rest
    rows, width = tokens.shape
    inner = gate_weight.shape[1]
    wide = column_step(inner)
    here = pl.ds(block * rows, rows)
    sequence = lax.axis_index("dp") * starts.shape[0]
    loads = started(
        [
            (tokens_home.at[here, :], tokens),
            (small_home, state_weight),
            (input_home, input_weight),
            (gate_home, gate_weight),
            (grads_home.at[here, :], grads),
            (out_home, out_weight),
        ],
        load_sems,
    )
    if first:
        state[...] = jnp.zeros_like(state)
        raw[0:8, :] = jnp.zeros((8, inner), f32)
        state_raw[0:8, :] = jnp.zeros((8, 256), f32)
    else:
        state[...] = state_in[...]
        raw[0:8, :] = halo_in[:, :inner]
        state_raw[0:8, :] = halo_in[:, inner:]

    def norm_rows(index, carry):
        at = pl.ds(pl.multiple_of(index * 16, 16), 16)
        values = tokens[at, :].astype(f32)
        inverse = lax.rsqrt(jnp.mean(values * values, axis=-1, keepdims=True) + epsilon)
        normed[at, :] = (values * inverse * gain[...]).astype(bf16)
        return carry

    settle(loads[:1])
    lax.fori_loop(0, rows // 16, norm_rows, 0, unroll=4)
    stores = started([(normed, homes[0].at[here, :])], store_sems, 0)
    settle(loads[1:2])
    small = dot(normed[...], state_weight[...]).astype(bf16)
    small_raw[...] = small
    state_raw[8 : 8 + rows, :] = small[:, :256].astype(f32)
    settle(loads[2:4])
    for start in range(0, inner, wide):
        lanes = slice(start, start + wide)
        low = dot(normed[...], input_weight[:, lanes]).astype(bf16)
        mixer_raw[:, lanes] = low
        raw[8 : 8 + rows, lanes] = low.astype(f32)
        gate_raw[:, lanes] = dot(normed[...], gate_weight[:, lanes]).astype(bf16)
    settle(loads[4:])
    for start in range(0, inner, wide):
        lanes = slice(start, start + wide)
        wide_back[:, lanes] = dot_nt(grads[...], out_weight[lanes, :])

    stores += started(
        [
            (gate_raw, homes[1].at[here, :]),
            (mixer_raw, homes[2].at[here, :]),
            (small_raw, homes[3].at[here, :]),
        ],
        store_sems,
        1,
    )

    def chunk(index, carry):
        first_row = pl.multiple_of(index * CHUNK, CHUNK)
        at = pl.ds(first_row, CHUNK)
        first_token = block * rows + index * CHUNK
        chunk_first = first_token.astype(f32)
        row_place = place(0).astype(f32) + chunk_first
        lane_place = place(1).astype(f32) + chunk_first
        start_column = stand(marks[0:1, pl.ds(pl.multiple_of(block * rows + index * CHUNK, CHUNK), CHUNK)])
        age = row_place - start_column
        kept = [(age >= k).astype(f32) for k in range(1, 4)]
        for j in range(2):
            lanes = slice(j * LANES, (j + 1) * LANES)
            pre = conv_pre(
                state_raw[pl.ds(first_row, CHUNK + 8), lanes], state_chan, lanes, kept
            )
            sigma = sigmoid(pre)
            act = pre * sigma
            states[at, lanes] = act.astype(bf16)
            state_slope[at, lanes] = (sigma + act * (1.0 - sigma)).astype(bf16)
        state_b = states[at, :LANES]
        state_c = states[at, LANES:]
        scores = jnp.where(
            (lane_place <= row_place) & (lane_place >= start_column),
            dot_nt(state_c, state_b),
            0.0,
        )
        _, step_size, levels = step_levels(small_raw[at, 256:].astype(f32), heads)
        levels_row = jnp.transpose(levels)
        last_start = (starts[first_token + CHUNK - 1] - sequence).astype(f32)
        carried = (last_start < chunk_first).astype(f32)
        ends = (row_place >= last_start).astype(f32)
        begins = (start_column < chunk_first).astype(f32)
        state_low = state[...].astype(bf16)
        kept_states[index] = state_low
        carried_out[...] = dot(state_c, state_low)
        low = low_lanes()
        squares = jnp.zeros((CHUNK, LANES), f32)
        crosses = jnp.zeros((CHUNK, LANES), f32)
        for j in range(inner // LANES):
            lanes = slice(j * LANES, (j + 1) * LANES)
            pre = conv_pre(raw[pl.ds(first_row, CHUNK + 8), lanes], chan, lanes, kept)
            sigma = sigmoid(pre)
            act = pre * sigma
            value = act.astype(bf16)
            mixer_in[at, lanes] = value
            slope[at, lanes] = (sigma + act * (1.0 - sigma)).astype(bf16)
            value = value.astype(f32)
            level_pair = []
            weights = []
            for h in (2 * j, 2 * j + 1):
                level = spread(levels[:, h : h + 1])
                level_pair.append(level)
                damping = jnp.exp2(jnp.minimum(level - levels_row[h : h + 1, :], 0.0))
                weights.append((scores * damping).astype(bf16))
            level = jnp.where(low, level_pair[0], level_pair[1])
            step_pair = jnp.where(
                low,
                spread(step_size[:, 2 * j : 2 * j + 1]),
                spread(step_size[:, 2 * j + 1 : 2 * j + 2]),
            )
            stepped = value * step_pair
            stacked = jnp.concatenate(
                [jnp.where(low, stepped, 0.0), jnp.where(low, 0.0, stepped)], axis=0
            ).astype(bf16)
            end_level = level[CHUNK - 1 : CHUNK, :]
            result = dot(jnp.concatenate(weights, axis=1), stacked)
            result += (begins * jnp.exp2(level)) * carried_out[:, lanes]
            damped[:, lanes] = (stepped * (ends * jnp.exp2(end_level - level))).astype(bf16)
            state[:, lanes] = state[:, lanes] * (carried * jnp.exp2(end_level))
            result += chan[5:6, lanes] * value
            mixed[at, lanes] = result
            gate = gate_raw[at, lanes].astype(f32)
            gated = result * (gate * sigmoid(gate))
            squares += gated * gated
            gained = gated * chan[6:7, lanes]
            gated_low[at, lanes] = gained.astype(bf16)
            out_back = wide_back[at, lanes]
            back[at, lanes] = out_back.astype(bf16)
            crosses += out_back * gained
        state[...] += dot_tn(state_b, damped[...])
        sums[0:1, at] = jnp.sum(jnp.transpose(squares), axis=0, keepdims=True)
        sums[1:2, at] = jnp.sum(jnp.transpose(crosses), axis=0, keepdims=True)
        return carry

    lax.fori_loop(0, rows // CHUNK, chunk, 0)
    stores += started(
        [
            (mixer_in, homes[4].at[here, :]),
            (slope, homes[5].at[here, :]),
            (states, homes[6].at[here, :]),
            (state_slope, homes[7].at[here, :]),
            (mixed, homes[8].at[here, :]),
            (back, homes[9].at[here, :]),
            (kept_states, homes[10].at[pl.ds(block * (rows // CHUNK), rows // CHUNK)]),
        ],
        store_sems,
        4,
    )
    if project:
        for start in range(0, width, 512):
            lanes = slice(start, start + 512)
            partial[:, lanes] = dot(gated_low[...], out_weight[:, lanes]).astype(bf16)
    else:
        partial[...] = gated_low[...]
    halo_out[:, :inner] = raw[rows : rows + 8, :]
    halo_out[:, inner:] = state_raw[rows : rows + 8, :]
    settle(stores)


def forward(block, starts, marks, tokens, grads, params, carry, earlier, after, project):
    gain, gate_weight, input_weight, small_weight, chan, state_chan, heads, out_weight = params
    tables = [gain, chan, state_chan, heads]
    weights = [input_weight, gate_weight, small_weight, out_weight]
    length, width = tokens.shape
    inner = gate_weight.shape[1]
    chunks = ROWS // CHUNK
    stored = [
        (width, bf16),
        (inner, bf16),
        (inner, bf16),
        (384, bf16),
        (inner, bf16),
        (inner, bf16),
        (256, bf16),
        (256, bf16),
        (inner, f32),
        (inner, bf16),
    ]
    out_shape = [jax.ShapeDtypeStruct((length, columns), kind) for columns, kind in stored]
    out_shape += [jax.ShapeDtypeStruct((length // CHUNK, LANES, inner), bf16)]
    shared = len(out_shape)
    own = [
        ((ROWS, width if project else inner), bf16),
        ((2, ROWS), f32),
        ((LANES, inner), f32),
        ((8, inner + 256), f32),
    ]
    out_shape += [jax.ShapeDtypeStruct(shape, kind) for shape, kind in own]
    in_specs = [SMEM, whole(marks.shape)] + [HBM] * 6 + wholes(tables) + wholes(carry)
    operands = [starts, marks, tokens, grads, *weights, *tables, *carry]
    aliases = {}
    if earlier is not None:
        aliases = {len(operands) + k: k for k in range(shared)}
        in_specs += [HBM] * shared
        operands += list(earlier)
    operands += list(after)
    in_specs += [ANY] * len(after)
    outs = pl.pallas_call(
        functools.partial(
            forward_kernel,
            block=block,
            first=not carry,
            unread=len(aliases) + len(after),
            project=project,
        ),
        grid=(1,),
        in_specs=in_specs,
        out_specs=[HBM] * shared + [whole(shape) for shape, _ in own],
        out_shape=out_shape,
        scratch_shapes=[
            pltpu.VMEM((ROWS, width), bf16),
            pltpu.VMEM((ROWS, width), bf16),
            *[pltpu.VMEM((ROWS, columns), kind) for columns, kind in stored],
            pltpu.VMEM((chunks, LANES, inner), bf16),
            pltpu.VMEM((ROWS + 8, inner), f32),
            pltpu.VMEM((ROWS + 8, 256), f32),
            pltpu.VMEM((ROWS, inner), bf16),
            pltpu.VMEM((ROWS, inner), f32),
            *[pltpu.VMEM(item.shape, bf16) for item in weights],
            pltpu.VMEM((CHUNK, inner), bf16),
            pltpu.VMEM((CHUNK, inner), f32),
            pltpu.SemaphoreType.DMA((6,)),
            pltpu.SemaphoreType.DMA((11,)),
        ],
        input_output_aliases=aliases,
        compiler_params=pltpu.CompilerParams(vmem_limit_bytes=VMEM_BYTES),
        cost_estimate=BRIEF,
        name="forward_mix",
    )(*operands)
    saved, (partial, sums, *carry) = outs[:shared], outs[shared:]
    return saved, partial, sums, carry


def project_kernel(*refs, count, unread):
    lows, out_weight, outs = refs[:count], refs[count], refs[count + 1 + unread :]
    for low, out in zip(lows, outs):
        for start in range(0, out.shape[1], 512):
            lanes = slice(start, start + 512)
            out[:, lanes] = dot(low[...], out_weight[:, lanes]).astype(bf16)


def project_rows(lows, out_weight, after):
    width = out_weight.shape[1]
    half = lambda columns: pl.BlockSpec((ROWS // 2, columns), lambda i: (i, 0))
    return pl.pallas_call(
        functools.partial(project_kernel, count=len(lows), unread=len(after)),
        grid=(2,),
        in_specs=[half(low.shape[1]) for low in lows]
        + [whole(out_weight.shape)]
        + [ANY] * len(after),
        out_specs=[half(width)] * len(lows),
        out_shape=[jax.ShapeDtypeStruct((low.shape[0], width), bf16) for low in lows],
        compiler_params=compiler_params(),
        cost_estimate=BRIEF,
        name="project_rows",
    )(*lows, out_weight, *after)


def compiler_params():
    return pltpu.CompilerParams(
        dimension_semantics=("arbitrary",), vmem_limit_bytes=VMEM_BYTES
    )


def gate_kernel(total_inner, sums, mixed, gate_raw, back, chan, *rest, unread):
    grad_low, gate_low, gate_out, gain_sums = rest[unread:]
    inner = chan.shape[1]

    @pl.when(pl.program_id(0) == 0)
    def _():
        gain_sums[...] = jnp.zeros_like(gain_sums)

    def chunk(index, carry):
        at = pl.ds(pl.multiple_of(index * CHUNK, CHUNK), CHUNK)
        inverse = lax.rsqrt(sums[0:1, at] / total_inner + epsilon)
        rms = stand(inverse)
        pull = stand(inverse * inverse * inverse * (sums[1:2, at] / total_inner))
        for j in range(inner // LANES):
            lanes = slice(j * LANES, (j + 1) * LANES)
            gate = gate_raw[at, lanes].astype(f32)
            sigma = sigmoid(gate)
            gate_act = gate * sigma
            mix = mixed[at, lanes]
            gated = mix * gate_act
            unit = gated * rms
            out_back = back[at, lanes].astype(f32)
            gate_gain = chan[6:7, lanes]
            gain_sums[:, lanes] += fold(out_back * unit)
            gated_grad = rms * (out_back * gate_gain) - pull * gated
            gate_low[at, lanes] = (
                gated_grad * mix * (sigma + gate_act * (1.0 - sigma))
            ).astype(bf16)
            gate_out[at, lanes] = (unit * gate_gain).astype(bf16)
            grad_low[at, lanes] = (gated_grad * gate_act).astype(bf16)
        return carry

    lax.fori_loop(0, mixed.shape[0] // CHUNK, chunk, 0)


def gate_grads(total_inner, sums, mixed, gate_raw, back, chan, after):
    length, inner = mixed.shape
    rows_of = lambda columns: pl.BlockSpec((ROWS, columns), lambda i: (i, 0))
    return pl.pallas_call(
        functools.partial(gate_kernel, total_inner, unread=len(after)),
        grid=(length // ROWS,),
        in_specs=[
            pl.BlockSpec((2, ROWS), lambda i: (0, i)),
            rows_of(inner),
            rows_of(inner),
            rows_of(inner),
            whole((8, inner)),
            *[ANY] * len(after),
        ],
        out_specs=[rows_of(inner)] * 3 + [held((8, inner))],
        out_shape=[jax.ShapeDtypeStruct((length, inner), bf16)] * 3
        + [jax.ShapeDtypeStruct((8, inner), f32)],
        compiler_params=compiler_params(),
        cost_estimate=BRIEF,
        name="gate_grads",
    )(sums, mixed, gate_raw, back, chan, *after)


def backward_kernel(
    starts,
    marks,
    gain,
    chan,
    state_chan,
    heads,
    *rest,
    block,
    first,
    unread,
    parts,
):
    sources, rest = rest[:14], rest[14:]
    if not first:
        earlier, rest = rest[:6], rest[6:]
    rest = rest[unread:]
    mixer_home, small_home = rest[:2]
    partials, rest = rest[2 : 2 + parts], rest[2 + parts :]
    results, rest = rest[:6], rest[6:]
    state_grad, halo_out, chan_sums, state_sums, head_sums, gain_sums = results
    buffers, rest = rest[:14], rest[14:]
    (
        mixed,
        mixer_grad,
        mixer_in,
        slope,
        small_raw,
        states,
        state_slope,
        kept_states,
        mixer_raw,
        gate_low,
        gate_weight,
        input_weight,
        state_weight,
        tokens,
    ) = buffers
    (
        mixer_low,
        small_low,
        pre_grad,
        state_pre,
        ends_low,
        begins_low,
        normed_grad,
        picks,
        carried_back,
        load_sems,
        store_sems,
    ) = rest
    rows, width = tokens.shape
    inner = gate_weight.shape[1]
    chunks = rows // CHUNK
    half = rows // 2
    here = pl.ds(block * rows, rows)
    sequence = lax.axis_index("dp") * starts.shape[0]

    def part_of(number):
        pairs = [
            (source.at[pl.ds(block * rows + number * half, half), :], buffer.at[pl.ds(number * half, half), :])
            for source, buffer in zip(sources[:7], buffers[:7])
        ]
        count = chunks // 2
        pairs.append(
            (
                sources[7].at[pl.ds(block * chunks + number * count, count)],
                kept_states.at[pl.ds(number * count, count)],
            )
        )
        return pairs

    soon = started(part_of(1), load_sems)
    second = started(part_of(0), load_sems, 8)
    late = started(
        [
            (source if source.shape[0] == buffer.shape[0] else source.at[here, :], buffer)
            for source, buffer in zip(sources[8:], buffers[8:])
        ],
        load_sems,
        16,
    )
    for j in range(inner // LANES):
        column = lax.broadcasted_iota(jnp.int32, (2 * LANES, LANES), 1)
        line = lax.broadcasted_iota(jnp.int32, (2 * LANES, LANES), 0) % LANES
        owner = 2 * j + (line >= LANES // 2).astype(jnp.int32)
        picks[j] = (column == owner).astype(bf16)
    if first:
        for result in results:
            result[...] = jnp.zeros_like(result)
        pre_grad[rows : rows + 8, :] = jnp.zeros((8, inner), f32)
        state_pre[rows : rows + 8, :] = jnp.zeros((8, 256), f32)
    else:
        for result, value in zip(results, earlier):
            result[...] = value[...]
        pre_grad[rows : rows + 8, :] = earlier[1][:, :inner]
        state_pre[rows : rows + 8, :] = earlier[1][:, inner:]
    settle(soon)

    def chunk(turn, carry):
        index = chunks - 1 - turn

        @pl.when(turn == chunks // 2)
        def _():
            settle(second)

        first_row = pl.multiple_of(index * CHUNK, CHUNK)
        at = pl.ds(first_row, CHUNK)
        first_token = block * rows + index * CHUNK
        chunk_first = first_token.astype(f32)
        row_place = place(0).astype(f32) + chunk_first
        lane_place = place(1).astype(f32) + chunk_first
        start_row = marks[0:1, pl.ds(pl.multiple_of(block * rows + index * CHUNK, CHUNK), CHUNK)]
        start_column = stand(start_row)
        seen = (row_place <= lane_place) & (row_place >= start_row)
        last_start = (starts[first_token + CHUNK - 1] - sequence).astype(f32)
        carried = (last_start < chunk_first).astype(f32)
        ends = (row_place >= last_start).astype(f32)
        begins = (start_column < chunk_first).astype(f32)
        state_b = states[at, :LANES]
        state_c = states[at, LANES:]
        scores = jnp.where(seen, dot_nt(state_b, state_c), 0.0)
        step_raw = small_raw[at, 256:].astype(f32)
        field, step_size, levels = step_levels(step_raw, heads)
        levels_row = jnp.transpose(levels)
        state_low = state_grad[...].astype(bf16)
        carried_back[...] = dot(state_b, state_low)
        low = low_lanes()
        score_grad = jnp.zeros((CHUNK, CHUNK), f32)
        level_grad = jnp.zeros((CHUNK, LANES), f32)
        inter_grad = jnp.zeros((CHUNK, LANES), f32)
        crossing_sum = jnp.zeros((8, LANES), f32)
        step_grad = jnp.zeros((CHUNK, LANES), f32)
        for j in range(inner // LANES):
            lanes = slice(j * LANES, (j + 1) * LANES)
            pick = picks[j]
            mix = mixed[at, lanes]
            grad = mixer_grad[at, lanes].astype(f32)
            value = mixer_in[at, lanes].astype(f32)
            skip = chan[5:6, lanes]
            chan_sums[0:8, lanes] += fold(grad * value)
            step_pair = jnp.where(
                low,
                spread(step_size[:, 2 * j : 2 * j + 1]),
                spread(step_size[:, 2 * j + 1 : 2 * j + 2]),
            )
            stepped = value * step_pair
            stepped_low = stepped.astype(bf16)
            stacked = jnp.concatenate(
                [jnp.where(low, grad, 0.0), jnp.where(low, 0.0, grad)], axis=0
            ).astype(bf16)
            cells = dot_nt(stepped_low, stacked)
            level_pair = []
            weights = []
            for k in range(2):
                h = 2 * j + k
                level = spread(levels[:, h : h + 1])
                level_pair.append(level)
                damping = jnp.exp2(jnp.minimum(levels_row[h : h + 1, :] - level, 0.0))
                weights.append((scores * damping).astype(bf16))
                score_grad += cells[:, k * CHUNK : (k + 1) * CHUNK] * damping
            level = jnp.where(low, level_pair[0], level_pair[1])
            end_level = level[CHUNK - 1 : CHUNK, :]
            ending = ends * jnp.exp2(end_level - level)
            beginning = begins * jnp.exp2(level)
            within = dot(jnp.concatenate(weights, axis=1), stacked)
            beyond = ending * carried_back[:, lanes]
            value_grad = within + beyond
            ends_low[:, lanes] = (stepped * ending).astype(bf16)
            begins_low[:, lanes] = (grad * beginning).astype(bf16)
            behind = state_grad[:, lanes]
            crossing = fold(behind * kept_states[index, :, lanes].astype(f32))
            crossing_sum += dot(halves(crossing), pick)
            state_grad[:, lanes] = behind * (carried * jnp.exp2(end_level))
            rows_flow = grad * (mix - skip * value) - stepped_low.astype(f32) * within
            level_grad += dot(halves(rows_flow), pick)
            inter_grad += dot((stepped * beyond).astype(bf16), pick[:LANES])
            step_grad += dot((value * value_grad).astype(bf16), pick[:LANES])
            pre_grad[at, lanes] = (step_pair * value_grad + skip * grad) * slope[
                at, lanes
            ].astype(f32)
        state_grad[...] += dot_tn(state_c, begins_low[...])
        score_low = jnp.where(seen, score_grad, 0.0).astype(bf16)
        state_pre[at, :LANES] = (
            dot(score_low, state_c) + dot_nt(ends_low[...], state_low)
        ) * state_slope[at, :LANES].astype(f32)
        state_pre[at, LANES:] = (
            dot_tn(score_low, state_b) + dot_nt(begins_low[...], kept_states[index])
        ) * state_slope[at, LANES:].astype(f32)
        onward = (place(0) <= place(1)).astype(f32)
        before = (place(0) > place(1)).astype(f32)
        across = jnp.sum(crossing_sum, axis=0, keepdims=True) * (
            carried * jnp.exp2(levels[CHUNK - 1 : CHUNK, :])
        )
        reach = dot(onward, level_grad, highest) + dot(before, inter_grad, highest) + across
        rates = heads[2:3, :]
        field_grad = (step_grad + reach * rates) * sigmoid(field)
        small_low[at, 256:] = field_grad.astype(bf16)
        head_sums[0:8, :] += fold(field_grad)
        head_sums[8:16, :] += fold(reach * step_size * rates)
        return carry

    lax.fori_loop(0, chunks, chunk, 0)
    settle(late)

    def unconv(index, carry):
        first_row = pl.multiple_of(index * CHUNK, CHUNK)
        at = pl.ds(first_row, CHUNK)
        left = stand(marks[1:2, pl.ds(pl.multiple_of(block * rows + index * CHUNK, CHUNK), CHUNK)])
        kept = [(left >= k).astype(f32) for k in range(1, 4)]

        def tile(window, value, taps, lanes, totals, line):
            own = window[:CHUNK]
            total = taps[0:1, lanes] * own
            totals[line : line + 8, lanes] += fold(value * own)
            for k in range(1, 4):
                moved = kept[k - 1] * window[k : k + CHUNK]
                total += taps[k : k + 1, lanes] * moved
                totals[line + 8 * k : line + 8 * k + 8, lanes] += fold(value * moved)
            totals[line + 32 : line + 40, lanes] += fold(own)
            return total.astype(bf16)

        for j in range(inner // LANES):
            lanes = slice(j * LANES, (j + 1) * LANES)
            mixer_low[at, lanes] = tile(
                pre_grad[pl.ds(first_row, CHUNK + 8), lanes],
                mixer_raw[at, lanes].astype(f32),
                chan,
                lanes,
                chan_sums,
                8,
            )
        for j in range(2):
            lanes = slice(j * LANES, (j + 1) * LANES)
            small_low[at, lanes] = tile(
                state_pre[pl.ds(first_row, CHUNK + 8), lanes],
                small_raw[at, lanes].astype(f32),
                state_chan,
                lanes,
                state_sums,
                0,
            )
        return carry

    lax.fori_loop(0, chunks, unconv, 0)
    stores = started(
        [(mixer_low, mixer_home.at[here, :]), (small_low, small_home.at[here, :])], store_sems
    )
    for start in range(0, width, 256):
        lanes = slice(start, start + 256)
        normed_grad[:, lanes] = (
            dot_nt(gate_low[...], gate_weight[lanes, :])
            + dot_nt(mixer_low[...], input_weight[lanes, :])
            + dot_nt(small_low[...], state_weight[lanes, :])
        )

    def unnorm(part, index, carry):
        at = pl.ds(pl.multiple_of(index * 16, 16), 16)
        from_row = pl.ds(pl.multiple_of(part * part_rows + index * 16, 16), 16)
        values = tokens[from_row, :].astype(f32)
        inverse = lax.rsqrt(jnp.mean(values * values, axis=-1, keepdims=True) + epsilon)
        unit = values * inverse
        grad = normed_grad[from_row, :]
        gain_sums[...] += fold(grad * unit)
        grad = grad * gain[...]
        out = partials[part]
        out[at, :] = (
            inverse * (grad - unit * jnp.mean(grad * unit, axis=-1, keepdims=True))
        ).astype(bf16)
        return carry

    part_rows = partials[0].shape[0]
    for part in range(len(partials)):
        lax.fori_loop(0, part_rows // 16, functools.partial(unnorm, part), 0, unroll=2)
    halo_out[:, :inner] = pre_grad[0:8, :]
    halo_out[:, inner:] = state_pre[0:8, :]
    settle(stores)


def backward(block, starts, marks, tokens, params, saved, grads, carry, earlier, after, parts):
    gain, gate_weight, input_weight, small_weight, chan, state_chan, heads, _ = params
    tables = [gain, chan, state_chan, heads]
    length, width = tokens.shape
    inner = gate_weight.shape[1]
    chunks = ROWS // CHUNK
    (gate_raw, mixer_raw, small_raw, mixer_in, slope, states, state_slope, mixed, _, kept) = saved
    mixer_grad, gate_low = grads
    sources = [
        mixed,
        mixer_grad,
        mixer_in,
        slope,
        small_raw,
        states,
        state_slope,
        kept,
        mixer_raw,
        gate_low,
        gate_weight,
        input_weight,
        small_weight,
        tokens,
    ]
    operands = [starts, marks, *tables, *sources, *carry]
    in_specs = [SMEM, *wholes([marks, *tables]), *[HBM] * len(sources), *wholes(carry)]
    aliases = {}
    if earlier is not None:
        aliases = {len(operands) + k: k for k in range(2)}
        in_specs += [HBM] * 2
        operands += list(earlier)
    operands += list(after)
    in_specs += [ANY] * len(after)
    results = [
        (LANES, inner),
        (8, inner + 256),
        (48, inner),
        (40, 256),
        (16, LANES),
        (8, width),
    ]
    outs = pl.pallas_call(
        functools.partial(
            backward_kernel,
            block=block,
            first=not carry,
            unread=len(aliases) + len(after),
            parts=parts,
        ),
        grid=(1,),
        in_specs=in_specs,
        out_specs=[HBM] * 2
        + [whole((ROWS // parts, width))] * parts
        + [whole(shape) for shape in results],
        out_shape=[
            jax.ShapeDtypeStruct((length, inner), bf16),
            jax.ShapeDtypeStruct((length, 384), bf16),
            *[jax.ShapeDtypeStruct((ROWS // parts, width), bf16)] * parts,
            *[jax.ShapeDtypeStruct(shape, f32) for shape in results],
        ],
        scratch_shapes=[
            *[
                pltpu.VMEM((chunks, LANES, inner), bf16)
                if source.ndim == 3
                else pltpu.VMEM(
                    (ROWS if source.shape[0] == length else source.shape[0], source.shape[1]),
                    source.dtype,
                )
                for source in sources
            ],
            pltpu.VMEM((ROWS, inner), bf16),
            pltpu.VMEM((ROWS, 384), bf16),
            pltpu.VMEM((ROWS + 8, inner), f32),
            pltpu.VMEM((ROWS + 8, 256), f32),
            pltpu.VMEM((CHUNK, inner), bf16),
            pltpu.VMEM((CHUNK, inner), bf16),
            pltpu.VMEM((ROWS, width), f32),
            pltpu.VMEM((inner // LANES, 2 * LANES, LANES), bf16),
            pltpu.VMEM((CHUNK, inner), f32),
            pltpu.SemaphoreType.DMA((22,)),
            pltpu.SemaphoreType.DMA((2,)),
        ],
        input_output_aliases=aliases,
        compiler_params=pltpu.CompilerParams(vmem_limit_bytes=VMEM_BYTES),
        cost_estimate=BRIEF,
        name="backward_mix",
    )(*operands)
    return outs[:2], outs[2 : 2 + parts], outs[2 + parts :]


def pack(packed, chan_sums, gate_sums, head_sums, state_sums, gain_sums, step_lines):
    inner = chan_sums.shape[1]
    packed[...] = jnp.zeros_like(packed)
    total = lambda values: jnp.sum(values, axis=0, keepdims=True)
    for k in range(6):
        packed[k : k + 1, :inner] = total(chan_sums[8 * k : 8 * k + 8, :])
    packed[6:7, :inner] = total(gate_sums[...])
    for k in range(2):
        packed[7:8, k * LANES : (k + 1) * LANES] = total(head_sums[8 * k : 8 * k + 8, :])
    for k in range(5):
        packed[8 + k : 9 + k, :256] = total(state_sums[8 * k : 8 * k + 8, :])
    packed[13:14, :] = total(gain_sums[...])
    packed[16:32, :] = step_lines[0:16, :]


def weight_kernel(left, *rest, rights, unread, packs):
    right, rest = rest[:rights], rest[rights:]
    sums, rest = rest[:packs], rest[packs + unread :]
    outs, totals = rest[: rights + bool(packs)], rest[rights + bool(packs) :]
    step = pl.program_id(0)

    @pl.when(step == 0)
    def _():
        for total in totals:
            total[...] = jnp.zeros_like(total)

    for start in range(0, left.shape[1], 256):
        columns = slice(start, start + 256)
        for item, total in zip(right, totals):
            total[columns, :] += dot_tn(left[:, columns], item[...])
        if packs:
            totals[rights][:, columns] += dot_tn(right[-1][:, 256:], left[:, columns])

    @pl.when(step == pl.num_programs(0) - 1)
    def _():
        if packs:
            packed = totals[rights + 1]
            pack(packed, *sums, totals[rights])
            outs[rights][...] = packed[...].astype(bf16)
        for out, total in zip(outs[:rights], totals):
            out[...] = total[:, : out.shape[1]].astype(bf16)


def weight_grads(left, rights, after, sums=()):
    length, height = left.shape
    rows_of = lambda columns: pl.BlockSpec((ROWS, columns), lambda i: (i, 0))
    shapes = [(height, item.shape[1]) for item in rights]
    outs, scratch = list(shapes), list(shapes)
    if sums:
        outs[-1] = (height, 256)
        outs.append((32, height))
        scratch += [(LANES, height), (32, height)]
    return pl.pallas_call(
        functools.partial(
            weight_kernel, rights=len(rights), unread=len(after), packs=len(sums)
        ),
        grid=(length // ROWS,),
        in_specs=[rows_of(height)]
        + [rows_of(item.shape[1]) for item in rights]
        + wholes(sums)
        + [ANY] * len(after),
        out_specs=[held(shape) for shape in outs],
        out_shape=[jax.ShapeDtypeStruct(shape, bf16) for shape in outs],
        scratch_shapes=[pltpu.VMEM(shape, f32) for shape in scratch],
        compiler_params=compiler_params(),
        cost_estimate=BRIEF,
        name="weight_grads",
    )(left, *rights, *sums, *after)


def land_kernel(take, total_home, moved_home, *rest, mode, unread):
    out_home, total, moved, out, load_sems, store_sems = rest[unread:]
    tiles = total.shape[0] // CHUNK
    part = [pl.ds(k * CHUNK, CHUNK) for k in range(tiles)]
    loads = [
        started(
            [
                (total_home.at[part[k], :], total.at[part[k], :]),
                (moved_home.at[part[k], :], moved.at[part[k], :]),
            ],
            load_sems,
            2 * k,
        )
        for k in range(tiles)
    ]
    stores = []
    for k in range(tiles):
        settle(loads[k])
        at = slice(k * CHUNK, (k + 1) * CHUNK)
        if mode == "add":
            out[at, :] = total[at, :] + moved[at, :]
        else:
            out[at, :] = jnp.where(take[0] > 0, moved[at, :], total[at, :])
        stores += started([(out.at[part[k], :], out_home.at[part[k], :])], store_sems, k)
    settle(stores)


def finish_kernel(
    take, total_home, moved_home, base_home, sums, *rest, adds, inner, row, unread
):
    out_home, total, moved, base, out, load_sems, store_sems = rest[unread:]
    rows = total.shape[0]
    tiles = rows // CHUNK
    at_home = lambda k: pl.ds(row + k * CHUNK, CHUNK)
    at_here = lambda k: pl.ds(k * CHUNK, CHUNK)

    def run(pairs):
        loads = [
            started(
                [(home.at[at_here(k), :], here.at[at_here(k), :]) for home, here in pairs]
                + [(base_home.at[at_home(k), :], base.at[at_here(k), :])],
                load_sems,
                3 * k,
            )
            for k in range(tiles)
        ]
        stores = []
        for k in range(tiles):
            at = slice(k * CHUNK, (k + 1) * CHUNK)
            if inner:
                scale = stand(
                    lax.rsqrt(
                        sums[0:1, row + k * CHUNK : row + (k + 1) * CHUNK] / inner + epsilon
                    )
                )
            settle(loads[k])
            for start in range(0, total.shape[1], LANES):
                lanes = slice(start, start + LANES)
                value = pairs[0][1][at, lanes].astype(f32)
                for _, here in pairs[1:]:
                    value += here[at, lanes].astype(f32)
                if inner:
                    value = value * scale
                out[at, lanes] = (value + base[at, lanes].astype(f32)).astype(bf16)
            stores += started(
                [(out.at[at_here(k), :], out_home.at[at_home(k), :])], store_sems, k
            )
        settle(stores)

    if adds:
        run([(moved_home, moved), (total_home, total)])
        return

    @pl.when(take[0] > 0)
    def _():
        run([(moved_home, moved)])

    @pl.when(take[0] <= 0)
    def _():
        run([(total_home, total)])


def land(take, total, moved, mode, after):
    rows, width = total.shape
    return pl.pallas_call(
        functools.partial(land_kernel, mode=mode, unread=len(after)),
        in_specs=[SMEM, HBM, HBM] + [ANY] * len(after),
        out_specs=HBM,
        out_shape=jax.ShapeDtypeStruct((rows, width), bf16),
        scratch_shapes=[
            *[pltpu.VMEM((rows, width), bf16)] * 3,
            pltpu.SemaphoreType.DMA((2 * rows // CHUNK,)),
            pltpu.SemaphoreType.DMA((rows // CHUNK,)),
        ],
        compiler_params=pltpu.CompilerParams(vmem_limit_bytes=VMEM_BYTES),
        cost_estimate=BRIEF,
        name="line_land",
    )(take, total, moved, *after)


def finish(take, total, moved, adds, base, sums, inner, row, earlier, after):
    rows, width = total.shape
    operands = [take, total, moved, base, sums]
    in_specs = [SMEM, HBM, HBM, HBM, whole(sums.shape)]
    aliases = {}
    if earlier is not None:
        aliases = {len(operands): 0}
        operands += [earlier]
        in_specs += [HBM]
    after = [item for item in after if item is not earlier]
    operands += after
    in_specs += [ANY] * len(after)
    return pl.pallas_call(
        functools.partial(
            finish_kernel,
            adds=adds,
            inner=inner,
            row=row,
            unread=len(aliases) + len(after),
        ),
        in_specs=in_specs,
        out_specs=HBM,
        grid=(1,),
        out_shape=jax.ShapeDtypeStruct(base.shape, bf16),
        scratch_shapes=[
            *[pltpu.VMEM((rows, width), bf16)] * 4,
            pltpu.SemaphoreType.DMA((3 * rows // CHUNK,)),
            pltpu.SemaphoreType.DMA((rows // CHUNK,)),
        ],
        input_output_aliases=aliases,
        compiler_params=pltpu.CompilerParams(vmem_limit_bytes=VMEM_BYTES),
        cost_estimate=BRIEF,
        name="line_finish",
    )(*operands)


class Line:
    def __init__(self, members, me):
        middle = members // 2
        self.steps = [
            ("add", [(near, near + 1), (members - 1 - near, members - 2 - near)], near)
            for near in range(middle - 1)
        ]
        self.steps.append(("add", [(middle - 1, middle), (middle, middle - 1)], 0))
        self.steps += [
            ("take", [(near + 1, near), (members - 2 - near, members - 1 - near)], near)
            for near in reversed(range(middle - 1))
        ]
        self.takes = [
            ((me == near) | (me == members - 1 - near)).astype(jnp.int32)[None]
            for _, _, near in self.steps
        ]
        self.flying = [[] for _ in self.steps]
        self.outs = {}

    def push(self, total, name, row):
        self.launch(0, total, name, row)

    def launch(self, step, total, name, row):
        moved = lax.ppermute(total, "tensor", self.steps[step][1])
        self.flying[step].append((total, moved, name, row))

    def tick(self, ending, after, first=1, then=1, last=1):
        ready = []
        for step, queue in enumerate(self.flying):
            count = last if step == len(self.flying) - 1 else then if step else first
            for _ in range(min(len(queue), count)):
                ready.append((step, queue.pop(0)))
        for step, (total, moved, name, row) in ready:
            mode = self.steps[step][0]
            if step < len(self.steps) - 1:
                total = land(self.takes[step], total, moved, mode, after)
                self.launch(step + 1, total, name, row)
                after = [total]
            else:
                base, sums, inner = ending[name]
                out = finish(
                    self.takes[step],
                    total,
                    moved,
                    mode == "add",
                    base,
                    sums,
                    inner,
                    row,
                    self.outs.get(name),
                    after,
                )
                self.outs[name] = out
                after = [out]
        return after

    def busy(self):
        return any(self.flying)

    def pending(self):
        return sum(len(queue) for queue in self.flying)


def sum_over(values, axis, size):
    parts = [values]
    for k in range(1, size):
        parts.append(lax.ppermute(values, axis, [(i, i ^ k) for i in range(size)]))
    while len(parts) > 1:
        parts = [parts[k] + parts[k + 1] for k in range(0, len(parts), 2)]
    return parts[0]


def part_kernel(me, lines, values, *rest, size, unread):
    outs = rest[unread:]
    rows = values.shape[0] // size
    for k in range(size):
        first = pl.multiple_of((me[0] ^ k) * rows, 32)
        outs[k][:rows, :] = values[pl.ds(first, rows), :]
        for j in range(lines.shape[1] // 256):
            at = slice(rows + 16 * j, rows + 16 * j + 16)
            outs[k][at, :] = lines[0:16, 256 * j : 256 * j + 256]


def join_kernel(*refs):
    parts, (line_sums, value_sums) = list(refs[:-2]), refs[-2:]
    rows = value_sums.shape[0]
    for out, at in [(value_sums, slice(0, rows)), (line_sums, slice(rows, None))]:
        totals = [part[at, :].astype(f32) for part in parts]
        while len(totals) > 1:
            totals = [totals[k] + totals[k + 1] for k in range(0, len(totals), 2)]
        out[...] = totals[0]


def sum_pieces(lines, values, axis, size, me, after):
    rows = values.shape[0] // size
    height = rows + 16 * (lines.shape[1] // 256)
    shape = jax.ShapeDtypeStruct((height, 256), bf16)
    own, *sent = pl.pallas_call(
        functools.partial(part_kernel, size=size, unread=len(after)),
        grid=(1,),
        in_specs=[SMEM, *wholes([lines, values]), *[ANY] * len(after)],
        out_specs=[whole(shape.shape)] * size,
        out_shape=[shape] * size,
        compiler_params=compiler_params(),
        cost_estimate=BRIEF,
        name="part_pieces",
    )(me[None], lines, values, *after)
    parts = [own] + [
        lax.ppermute(sent[k - 1], axis, [(i, i ^ k) for i in range(size)])
        for k in range(1, size)
    ]
    outs = [(height - rows, 256), (rows, 256)]
    line_sums, value_sums = pl.pallas_call(
        join_kernel,
        grid=(1,),
        in_specs=wholes(parts),
        out_specs=[whole(item) for item in outs],
        out_shape=[jax.ShapeDtypeStruct(item, f32) for item in outs],
        compiler_params=compiler_params(),
        cost_estimate=BRIEF,
        name="join_pieces",
    )(*parts)
    return line_sums.reshape(-1, 16, 256), value_sums


def on_device(
    block_input,
    segment_ids,
    norm_gain,
    gate_weight,
    input_weight,
    state_weight,
    step_weight,
    mixer_conv,
    mixer_shift,
    state_conv,
    state_shift,
    step_bias,
    decay_log,
    skip_gain,
    gate_gain,
    out_weight,
    out_grad,
):
    length, width = block_input.shape
    inner = gate_weight.shape[1]
    heads_local = step_weight.shape[1]
    groups = lax.axis_size("tensor")
    member = lax.axis_index("tensor")
    columns = width // groups
    total_inner = inner * groups

    gain, marks, chan, state_chan, heads, small_weight = prepare(
        length,
        width,
        inner,
        (
            segment_ids,
            norm_gain,
            mixer_conv,
            mixer_shift,
            state_conv,
            state_shift,
            step_bias,
            decay_log,
            skip_gain,
            gate_gain,
            state_weight,
            step_weight,
        ),
    )
    params = (
        gain,
        gate_weight,
        input_weight,
        small_weight,
        chan,
        state_chan,
        heads,
        out_weight,
    )
    blocks = length // ROWS
    line = Line(groups, member)
    saved, carry, after = None, [], []
    block_sums, waiting = [], []
    for block in range(blocks):
        early = block < blocks // 2
        saved, partial, sums, carry = forward(
            block,
            segment_ids,
            marks,
            block_input,
            out_grad,
            params,
            carry,
            saved,
            after,
            early,
        )
        block_sums.append(sums)
        after = [partial]
        if early:
            line.push(partial, "output", block * ROWS)
        else:
            waiting.append(partial)
        if block == blocks // 2:
            after = line.tick({}, after)
    sums = jnp.concatenate(block_sums, axis=1)
    after = line.tick({}, [sums])
    sums = sum_over(sums, "tensor", groups)
    partials = project_rows(waiting, out_weight, [*after, sums])
    ending = {
        "output": (block_input, sums, total_inner),
        "input": (out_grad, sums, 0),
    }
    for k, partial in enumerate(partials):
        line.push(partial, "output", (blocks // 2 + k) * ROWS)
    after = [partials[0]]
    normed, *saved = saved
    grad_low, gate_low, gate_out, gate_sums = gate_grads(
        total_inner, sums, saved[7], saved[0], saved[8], chan, after
    )
    (gate_weight_grad,) = weight_grads(normed, [gate_low], [grad_low])
    (out_weight_grad,) = weight_grads(gate_out, [out_grad], [gate_weight_grad])
    after = [out_weight_grad]
    gate_weight_grad, out_weight_grad = lax.psum((gate_weight_grad, out_weight_grad), "dp")
    after = line.tick(ending, after)
    lows, carry = None, []
    for block in reversed(range(blocks)):
        lows, partials, carry = backward(
            block,
            segment_ids,
            marks,
            block_input,
            params,
            saved,
            (grad_low, gate_low),
            carry,
            lows,
            after + [gate_weight_grad, out_weight_grad] if block == blocks // 2 - 1 else after,
            2 if block == 0 else 1,
        )
        after = [partials[0]]
        for k, partial in enumerate(partials):
            line.push(partial, "input", block * ROWS + k * partial.shape[0])
        if block > 0:
            after = line.tick(ending, after)
    mixer_low, small_low = lows
    chan_sums, state_sums, head_sums, gain_sums = carry[2:]
    weight_sums = weight_grads(
        normed,
        [mixer_low, small_low],
        after,
        (chan_sums, gate_sums, head_sums, state_sums, gain_sums),
    )
    after = [weight_sums[0]]
    input_weight_grad, state_weight_grad, packed = lax.psum(tuple(weight_sums), "dp")
    after = line.tick(ending, after, first=2)
    ticks = 0
    while line.busy():
        after = after + [input_weight_grad] if ticks == 1 else after
        if line.pending() == 1:
            line_sums, state_weight_grad = sum_pieces(
                packed, state_weight_grad, "tensor", groups, member, after
            )
        after = line.tick(ending, after, first=2)
        ticks += 1
    block_output = line.outs["output"]
    input_grad = line.outs["input"]
    packed = packed.astype(f32)
    return (
        block_output,
        input_grad,
        lax.dynamic_slice_in_dim(line_sums[:, 13].reshape(-1), member * columns, columns, 0),
        gate_weight_grad.astype(f32),
        input_weight_grad.astype(f32),
        state_weight_grad,
        packed[16 : 16 + heads_local].T,
        packed[1:5, :inner],
        packed[5, :inner],
        line_sums[0, 8:12],
        line_sums[0, 12],
        packed[7, :heads_local],
        packed[7, LANES : LANES + heads_local],
        packed[0, :inner].reshape(heads_local, inner // heads_local).sum(axis=1),
        packed[6, :inner],
        out_weight_grad.astype(f32),
    )


def solution(mesh):
    return jax.shard_map(
        on_device,
        mesh=mesh,
        in_specs=(
            P("dp", None),
            P("dp"),
            P(),
            P(None, "tensor"),
            P(None, "tensor"),
            P(),
            P(None, "tensor"),
            P(None, "tensor"),
            P("tensor"),
            P(),
            P(),
            P("tensor"),
            P("tensor"),
            P("tensor"),
            P("tensor"),
            P("tensor", None),
            P("dp", None),
        ),
        out_specs=(
            P("dp", None),
            P("dp", None),
            P("tensor"),
            P(None, "tensor"),
            P(None, "tensor"),
            P("tensor", None),
            P(None, "tensor"),
            P(None, "tensor"),
            P("tensor"),
            P(),
            P(),
            P("tensor"),
            P("tensor"),
            P("tensor"),
            P("tensor"),
            P("tensor", None),
        ),
        check_vma=False,
    )
```

```python
import functools

import jax
import jax.numpy as jnp
from jax import lax
from jax.experimental import pallas as pl
from jax.experimental.pallas import tpu as pltpu
from jax.sharding import PartitionSpec as P

epsilon = 1e-05
highest = lax.Precision.HIGHEST
f32 = jnp.float32
bf16 = jnp.bfloat16
LOG2E = 1.4426950408889634
CHUNK = 128
LANES = 128
ROWS = 512
VMEM_BYTES = 60 * 1024 * 1024
BRIEF = pl.CostEstimate(flops=1000, bytes_accessed=1000, transcendentals=0)


def dot(left, right, precision=None):
    return lax.dot_general(
        left, right, (((1,), (0,)), ((), ())), precision=precision, preferred_element_type=f32
    )


def dot_nt(left, right):
    return lax.dot_general(left, right, (((1,), (1,)), ((), ())), preferred_element_type=f32)


def dot_tn(left, right):
    return lax.dot_general(left, right, (((0,), (0,)), ((), ())), preferred_element_type=f32)


def sigmoid(values):
    return 0.5 * jnp.tanh(0.5 * values) + 0.5


def softplus(values):
    power = jnp.exp(-jnp.abs(values))
    above = 1.0 + power
    exact = above == 1.0
    tail = jnp.log(above) * (power / jnp.where(exact, 1.0, above - 1.0))
    return jnp.maximum(values, 0.0) + jnp.where(exact, power, tail)


def spread(column):
    return jnp.broadcast_to(column, (column.shape[0], LANES))


def stand(row):
    return jnp.transpose(jnp.broadcast_to(row, (CHUNK, CHUNK)))


def fold(values):
    return jnp.sum(values.reshape(values.shape[0] // 8, 8, values.shape[1]), axis=0)


def halves(values):
    upper = values.astype(bf16)
    lower = (values - upper.astype(f32)).astype(bf16)
    return jnp.concatenate([upper, lower], axis=1)


def place(axis):
    return lax.broadcasted_iota(jnp.int32, (CHUNK, CHUNK), axis)


def low_lanes():
    return place(1) < LANES // 2


def column_step(width):
    return 256 if width % 256 == 0 else 128


def conv_pre(window, taps, lanes, kept):
    total = taps[4:5, lanes] + taps[0:1, lanes] * window[8:]
    for offset in range(1, 4):
        moved = window[8 - offset : 8 - offset + CHUNK]
        total = total + taps[offset : offset + 1, lanes] * (kept[offset - 1] * moved)
    return total


def step_levels(step_raw, heads):
    field = step_raw + heads[0:1, :]
    step = softplus(field)
    tri = (place(0) >= place(1)).astype(f32)
    levels = dot(tri, step * heads[1:2, :], highest)
    return field, step, levels


HBM = pl.BlockSpec(memory_space=pl.ANY)
SMEM = pl.BlockSpec(memory_space=pltpu.SMEM)
ANY = pl.BlockSpec(memory_space=pl.ANY)


def spread_heads(step_size, levels, begins, ends, owners):
    end_level = levels[CHUNK - 1 : CHUNK, :]
    last = jnp.broadcast_to(jnp.exp2(end_level), (8, LANES))
    compact = jnp.concatenate(
        [
            halves(step_size),
            halves(begins * jnp.exp2(levels)),
            halves(ends * jnp.exp2(end_level - levels)),
            halves(last),
        ],
        axis=0,
    )
    return dot(compact, owners[...])


def whole(shape):
    return pl.BlockSpec(shape, lambda i: (0,) * len(shape), pipeline_mode=pl.Buffered(1))


def held(shape):
    return pl.BlockSpec(shape, lambda i: (0,) * len(shape))


def wholes(items):
    return [whole(item.shape) for item in items]


def started(pairs, semaphores, first=0):
    copies = []
    for k, (source, target) in enumerate(pairs):
        copy = pltpu.make_async_copy(source, target, semaphores.at[first + k])
        copy.start()
        copies.append(copy)
    return copies


def settle(copies):
    for copy in copies:
        copy.wait()


def line_of(values):
    return values[...].reshape(1, values.shape[0])


def prepare_kernel(
    segments,
    norm_gain,
    mixer_conv,
    mixer_shift,
    state_conv,
    state_shift,
    step_bias,
    decay_log,
    skip_gain,
    gate_gain,
    state_weight,
    step_weight,
    gain,
    marks,
    chan,
    state_chan,
    heads,
    small_weight,
    owners,
):
    length = segments.shape[0]
    inner = gate_gain.shape[0]
    count = step_bias.shape[0]
    gain[...] = line_of(norm_gain)
    place_line = lax.broadcasted_iota(jnp.int32, (8, length), 1)
    first = lax.axis_index("dp") * length
    start = jnp.broadcast_to(line_of(segments), (8, length)) - first
    left = jnp.zeros((8, length), f32)
    for k in range(1, 4):
        later = pltpu.roll(start, length - k, 1)
        same = (later <= place_line) & (place_line < length - k)
        left += same.astype(f32)
    marks[0:1, :] = start[0:1].astype(f32)
    marks[1:2, :] = left[0:1]
    heads[...] = jnp.zeros_like(heads)
    rates = -jnp.exp(line_of(decay_log))
    heads[0:1, :count] = line_of(step_bias)
    heads[1:2, :count] = rates * LOG2E
    heads[2:3, :count] = rates
    heads[3:4, :count] = line_of(skip_gain)
    chan[...] = jnp.zeros_like(chan)
    chan[0:4, :] = mixer_conv[...]
    chan[4:5, :] = line_of(mixer_shift)
    owner = lax.broadcasted_iota(jnp.int32, (LANES, inner), 0)
    channel = lax.broadcasted_iota(jnp.int32, (LANES, inner), 1)
    owns = (channel // (inner // count) == owner).astype(f32)
    chan[5:6, :] = dot(heads[...], owns, highest)[3:4]
    owners[:LANES, :] = owns.astype(bf16)
    owners[LANES:, :] = owns.astype(bf16)
    chan[6:7, :] = line_of(gate_gain)
    state_chan[...] = jnp.zeros_like(state_chan)
    state_chan[0:4, :] = state_conv[...]
    state_chan[4:5, :] = line_of(state_shift)
    small_weight[:, :256] = state_weight[...]
    small_weight[:, 256:] = jnp.zeros((small_weight.shape[0], LANES), bf16)
    small_weight[:, 256 : 256 + count] = step_weight[...]


def prepare(length, width, inner, values):
    shapes = [
        ((1, width), f32),
        ((2, length), f32),
        ((8, inner), f32),
        ((8, 256), f32),
        ((8, LANES), f32),
        ((width, 384), bf16),
        ((2 * LANES, inner), bf16),
    ]
    return pl.pallas_call(
        prepare_kernel,
        grid=(1,),
        in_specs=wholes(values),
        out_specs=[whole(shape) for shape, _ in shapes],
        out_shape=[jax.ShapeDtypeStruct(shape, kind) for shape, kind in shapes],
        compiler_params=pltpu.CompilerParams(vmem_limit_bytes=VMEM_BYTES),
        cost_estimate=BRIEF,
        name="prepare",
    )(*values)


def forward_kernel(
    starts,
    marks,
    tokens_home,
    grads_home,
    input_home,
    gate_home,
    small_home,
    out_home,
    gain,
    chan,
    state_chan,
    heads,
    owners,
    *rest,
    block,
    first,
    unread,
    project,
):
    if not first:
        state_in, halo_in = rest[:2]
        rest = rest[2:]
    rest = rest[unread:]
    homes, rest = rest[:11], rest[11:]
    (
        partial,
        sums,
        state,
        halo_out,
        tokens,
        grads,
        normed,
        gate_raw,
        mixer_raw,
        small_raw,
        mixer_in,
        slope,
        states,
        state_slope,
        mixed,
        back,
        kept_states,
        raw,
        state_raw,
        gated_low,
        wide_back,
        input_weight,
        gate_weight,
        state_weight,
        out_weight,
        damped,
        carried_out,
        by_head,
        load_sems,
        store_sems,
    ) = rest
    rows, width = tokens.shape
    inner = gate_weight.shape[1]
    wide = column_step(inner)
    here = pl.ds(block * rows, rows)
    sequence = lax.axis_index("dp") * starts.shape[0]
    loads = started(
        [
            (tokens_home.at[here, :], tokens),
            (small_home, state_weight),
            (input_home, input_weight),
            (gate_home, gate_weight),
            (grads_home.at[here, :], grads),
            (out_home, out_weight),
        ],
        load_sems,
    )
    if first:
        state[...] = jnp.zeros_like(state)
        raw[0:8, :] = jnp.zeros((8, inner), f32)
        state_raw[0:8, :] = jnp.zeros((8, 256), f32)
    else:
        state[...] = state_in[...]
        raw[0:8, :] = halo_in[:, :inner]
        state_raw[0:8, :] = halo_in[:, inner:]

    def norm_rows(index, carry):
        at = pl.ds(pl.multiple_of(index * 16, 16), 16)
        values = tokens[at, :].astype(f32)
        inverse = lax.rsqrt(jnp.mean(values * values, axis=-1, keepdims=True) + epsilon)
        normed[at, :] = (values * inverse * gain[...]).astype(bf16)
        return carry

    settle(loads[:1])
    lax.fori_loop(0, rows // 16, norm_rows, 0, unroll=4)
    stores = started([(normed, homes[0].at[here, :])], store_sems, 0)
    settle(loads[1:2])
    small = dot(normed[...], state_weight[...]).astype(bf16)
    small_raw[...] = small
    state_raw[8 : 8 + rows, :] = small[:, :256].astype(f32)
    settle(loads[2:4])
    for start in range(0, inner, wide):
        lanes = slice(start, start + wide)
        low = dot(normed[...], input_weight[:, lanes]).astype(bf16)
        mixer_raw[:, lanes] = low
        raw[8 : 8 + rows, lanes] = low.astype(f32)
        gate_raw[:, lanes] = dot(normed[...], gate_weight[:, lanes]).astype(bf16)
    settle(loads[4:])
    for start in range(0, inner, wide):
        lanes = slice(start, start + wide)
        wide_back[:, lanes] = dot_nt(grads[...], out_weight[lanes, :])

    stores += started(
        [
            (gate_raw, homes[1].at[here, :]),
            (mixer_raw, homes[2].at[here, :]),
            (small_raw, homes[3].at[here, :]),
        ],
        store_sems,
        1,
    )

    def chunk(index, carry):
        first_row = pl.multiple_of(index * CHUNK, CHUNK)
        at = pl.ds(first_row, CHUNK)
        first_token = block * rows + index * CHUNK
        chunk_first = first_token.astype(f32)
        row_place = place(0).astype(f32) + chunk_first
        lane_place = place(1).astype(f32) + chunk_first
        start_column = stand(marks[0:1, pl.ds(pl.multiple_of(block * rows + index * CHUNK, CHUNK), CHUNK)])
        age = row_place - start_column
        kept = [(age >= k).astype(f32) for k in range(1, 4)]
        for j in range(2):
            lanes = slice(j * LANES, (j + 1) * LANES)
            pre = conv_pre(
                state_raw[pl.ds(first_row, CHUNK + 8), lanes], state_chan, lanes, kept
            )
            sigma = sigmoid(pre)
            act = pre * sigma
            states[at, lanes] = act.astype(bf16)
            state_slope[at, lanes] = (sigma + act * (1.0 - sigma)).astype(bf16)
        state_b = states[at, :LANES]
        state_c = states[at, LANES:]
        scores = jnp.where(
            (lane_place <= row_place) & (lane_place >= start_column),
            dot_nt(state_c, state_b),
            0.0,
        )
        _, step_size, levels = step_levels(small_raw[at, 256:].astype(f32), heads)
        levels_row = jnp.transpose(levels)
        last_start = (starts[first_token + CHUNK - 1] - sequence).astype(f32)
        carried = (last_start < chunk_first).astype(f32)
        ends = (row_place >= last_start).astype(f32)
        begins = (start_column < chunk_first).astype(f32)
        state_low = state[...].astype(bf16)
        kept_states[index] = state_low
        carried_out[...] = dot(state_c, state_low)
        by_head[...] = spread_heads(step_size, levels, begins, ends, owners)
        low = low_lanes()
        squares = jnp.zeros((CHUNK, LANES), f32)
        crosses = jnp.zeros((CHUNK, LANES), f32)
        for j in range(inner // LANES):
            lanes = slice(j * LANES, (j + 1) * LANES)
            pre = conv_pre(raw[pl.ds(first_row, CHUNK + 8), lanes], chan, lanes, kept)
            sigma = sigmoid(pre)
            act = pre * sigma
            value = act.astype(bf16)
            mixer_in[at, lanes] = value
            slope[at, lanes] = (sigma + act * (1.0 - sigma)).astype(bf16)
            value = value.astype(f32)
            weights = []
            for h in (2 * j, 2 * j + 1):
                level = spread(levels[:, h : h + 1])
                damping = jnp.exp2(jnp.minimum(level - levels_row[h : h + 1, :], 0.0))
                weights.append((scores * damping).astype(bf16))
            step_pair = by_head[0:CHUNK, lanes]
            beginning = by_head[CHUNK : 2 * CHUNK, lanes]
            ending = by_head[2 * CHUNK : 3 * CHUNK, lanes]
            last = by_head[3 * CHUNK : 3 * CHUNK + 1, lanes]
            stepped = value * step_pair
            stacked = jnp.concatenate(
                [jnp.where(low, stepped, 0.0), jnp.where(low, 0.0, stepped)], axis=0
            ).astype(bf16)
            result = dot(jnp.concatenate(weights, axis=1), stacked)
            result += beginning * carried_out[:, lanes]
            damped[:, lanes] = (stepped * ending).astype(bf16)
            state[:, lanes] = state[:, lanes] * (carried * last)
            result += chan[5:6, lanes] * value
            mixed[at, lanes] = result
            gate = gate_raw[at, lanes].astype(f32)
            gated = result * (gate * sigmoid(gate))
            squares += gated * gated
            gained = gated * chan[6:7, lanes]
            gated_low[at, lanes] = gained.astype(bf16)
            out_back = wide_back[at, lanes]
            back[at, lanes] = out_back.astype(bf16)
            crosses += out_back * gained
        state[...] += dot_tn(state_b, damped[...])
        sums[0:1, at] = jnp.sum(jnp.transpose(squares), axis=0, keepdims=True)
        sums[1:2, at] = jnp.sum(jnp.transpose(crosses), axis=0, keepdims=True)
        return carry

    lax.fori_loop(0, rows // CHUNK, chunk, 0)
    stores += started(
        [
            (mixer_in, homes[4].at[here, :]),
            (slope, homes[5].at[here, :]),
            (states, homes[6].at[here, :]),
            (state_slope, homes[7].at[here, :]),
            (mixed, homes[8].at[here, :]),
            (back, homes[9].at[here, :]),
            (kept_states, homes[10].at[pl.ds(block * (rows // CHUNK), rows // CHUNK)]),
        ],
        store_sems,
        4,
    )
    if project:
        for start in range(0, width, 512):
            lanes = slice(start, start + 512)
            partial[:, lanes] = dot(gated_low[...], out_weight[:, lanes]).astype(bf16)
    else:
        partial[...] = gated_low[...]
    halo_out[:, :inner] = raw[rows : rows + 8, :]
    halo_out[:, inner:] = state_raw[rows : rows + 8, :]
    settle(stores)


def forward(block, starts, marks, tokens, grads, params, carry, earlier, after, project):
    gain, gate_weight, input_weight, small_weight, *tables, out_weight = params
    tables = [gain, *tables]
    weights = [input_weight, gate_weight, small_weight, out_weight]
    length, width = tokens.shape
    inner = gate_weight.shape[1]
    chunks = ROWS // CHUNK
    stored = [
        (width, bf16),
        (inner, bf16),
        (inner, bf16),
        (384, bf16),
        (inner, bf16),
        (inner, bf16),
        (256, bf16),
        (256, bf16),
        (inner, f32),
        (inner, bf16),
    ]
    out_shape = [jax.ShapeDtypeStruct((length, columns), kind) for columns, kind in stored]
    out_shape += [jax.ShapeDtypeStruct((length // CHUNK, LANES, inner), bf16)]
    shared = len(out_shape)
    own = [
        ((ROWS, width if project else inner), bf16),
        ((2, ROWS), f32),
        ((LANES, inner), f32),
        ((8, inner + 256), f32),
    ]
    out_shape += [jax.ShapeDtypeStruct(shape, kind) for shape, kind in own]
    in_specs = [SMEM, whole(marks.shape)] + [HBM] * 6 + wholes(tables) + wholes(carry)
    operands = [starts, marks, tokens, grads, *weights, *tables, *carry]
    aliases = {}
    if earlier is not None:
        aliases = {len(operands) + k: k for k in range(shared)}
        in_specs += [HBM] * shared
        operands += list(earlier)
    operands += list(after)
    in_specs += [ANY] * len(after)
    outs = pl.pallas_call(
        functools.partial(
            forward_kernel,
            block=block,
            first=not carry,
            unread=len(aliases) + len(after),
            project=project,
        ),
        grid=(1,),
        in_specs=in_specs,
        out_specs=[HBM] * shared + [whole(shape) for shape, _ in own],
        out_shape=out_shape,
        scratch_shapes=[
            pltpu.VMEM((ROWS, width), bf16),
            pltpu.VMEM((ROWS, width), bf16),
            *[pltpu.VMEM((ROWS, columns), kind) for columns, kind in stored],
            pltpu.VMEM((chunks, LANES, inner), bf16),
            pltpu.VMEM((ROWS + 8, inner), f32),
            pltpu.VMEM((ROWS + 8, 256), f32),
            pltpu.VMEM((ROWS, inner), bf16),
            pltpu.VMEM((ROWS, inner), f32),
            *[pltpu.VMEM(item.shape, bf16) for item in weights],
            pltpu.VMEM((CHUNK, inner), bf16),
            pltpu.VMEM((CHUNK, inner), f32),
            pltpu.VMEM((3 * CHUNK + 8, inner), f32),
            pltpu.SemaphoreType.DMA((6,)),
            pltpu.SemaphoreType.DMA((11,)),
        ],
        input_output_aliases=aliases,
        compiler_params=pltpu.CompilerParams(vmem_limit_bytes=VMEM_BYTES),
        cost_estimate=BRIEF,
        name="forward_mix",
    )(*operands)
    saved, (partial, sums, *carry) = outs[:shared], outs[shared:]
    return saved, partial, sums, carry


def project_kernel(*refs, count, unread):
    lows, out_weight, outs = refs[:count], refs[count], refs[count + 1 + unread :]
    for low, out in zip(lows, outs):
        for start in range(0, out.shape[1], 512):
            lanes = slice(start, start + 512)
            out[:, lanes] = dot(low[...], out_weight[:, lanes]).astype(bf16)


def project_rows(lows, out_weight, after):
    width = out_weight.shape[1]
    half = lambda columns: pl.BlockSpec((ROWS // 2, columns), lambda i: (i, 0))
    return pl.pallas_call(
        functools.partial(project_kernel, count=len(lows), unread=len(after)),
        grid=(2,),
        in_specs=[half(low.shape[1]) for low in lows]
        + [whole(out_weight.shape)]
        + [ANY] * len(after),
        out_specs=[half(width)] * len(lows),
        out_shape=[jax.ShapeDtypeStruct((low.shape[0], width), bf16) for low in lows],
        compiler_params=compiler_params(),
        cost_estimate=BRIEF,
        name="project_rows",
    )(*lows, out_weight, *after)


def compiler_params():
    return pltpu.CompilerParams(
        dimension_semantics=("arbitrary",), vmem_limit_bytes=VMEM_BYTES
    )


def gate_kernel(total_inner, sums, mixed, gate_raw, back, chan, *rest, unread):
    grad_low, gate_low, gate_out, gain_sums = rest[unread:]
    inner = chan.shape[1]

    @pl.when(pl.program_id(0) == 0)
    def _():
        gain_sums[...] = jnp.zeros_like(gain_sums)

    def chunk(index, carry):
        at = pl.ds(pl.multiple_of(index * CHUNK, CHUNK), CHUNK)
        inverse = lax.rsqrt(sums[0:1, at] / total_inner + epsilon)
        rms = stand(inverse)
        pull = stand(inverse * inverse * inverse * (sums[1:2, at] / total_inner))
        for j in range(inner // LANES):
            lanes = slice(j * LANES, (j + 1) * LANES)
            gate = gate_raw[at, lanes].astype(f32)
            sigma = sigmoid(gate)
            gate_act = gate * sigma
            mix = mixed[at, lanes]
            gated = mix * gate_act
            unit = gated * rms
            out_back = back[at, lanes].astype(f32)
            gate_gain = chan[6:7, lanes]
            gain_sums[:, lanes] += fold(out_back * unit)
            gated_grad = rms * (out_back * gate_gain) - pull * gated
            gate_low[at, lanes] = (
                gated_grad * mix * (sigma + gate_act * (1.0 - sigma))
            ).astype(bf16)
            gate_out[at, lanes] = (unit * gate_gain).astype(bf16)
            grad_low[at, lanes] = (gated_grad * gate_act).astype(bf16)
        return carry

    lax.fori_loop(0, mixed.shape[0] // CHUNK, chunk, 0)


def gate_grads(total_inner, sums, mixed, gate_raw, back, chan, after):
    length, inner = mixed.shape
    rows_of = lambda columns: pl.BlockSpec((ROWS, columns), lambda i: (i, 0))
    return pl.pallas_call(
        functools.partial(gate_kernel, total_inner, unread=len(after)),
        grid=(length // ROWS,),
        in_specs=[
            pl.BlockSpec((2, ROWS), lambda i: (0, i)),
            rows_of(inner),
            rows_of(inner),
            rows_of(inner),
            whole((8, inner)),
            *[ANY] * len(after),
        ],
        out_specs=[rows_of(inner)] * 3 + [held((8, inner))],
        out_shape=[jax.ShapeDtypeStruct((length, inner), bf16)] * 3
        + [jax.ShapeDtypeStruct((8, inner), f32)],
        compiler_params=compiler_params(),
        cost_estimate=BRIEF,
        name="gate_grads",
    )(sums, mixed, gate_raw, back, chan, *after)


def backward_kernel(
    starts,
    marks,
    gain,
    chan,
    state_chan,
    heads,
    owners,
    *rest,
    block,
    first,
    unread,
    parts,
):
    sources, rest = rest[:14], rest[14:]
    if not first:
        earlier, rest = rest[:6], rest[6:]
    rest = rest[unread:]
    mixer_home, small_home = rest[:2]
    partials, rest = rest[2 : 2 + parts], rest[2 + parts :]
    results, rest = rest[:6], rest[6:]
    state_grad, halo_out, chan_sums, state_sums, head_sums, gain_sums = results
    buffers, rest = rest[:14], rest[14:]
    (
        mixed,
        mixer_grad,
        mixer_in,
        slope,
        small_raw,
        states,
        state_slope,
        kept_states,
        mixer_raw,
        gate_low,
        gate_weight,
        input_weight,
        state_weight,
        tokens,
    ) = buffers
    (
        mixer_low,
        small_low,
        pre_grad,
        state_pre,
        ends_low,
        begins_low,
        normed_grad,
        picks,
        carried_back,
        by_head,
        load_sems,
        store_sems,
    ) = rest
    rows, width = tokens.shape
    inner = gate_weight.shape[1]
    chunks = rows // CHUNK
    half = rows // 2
    here = pl.ds(block * rows, rows)
    sequence = lax.axis_index("dp") * starts.shape[0]

    def part_of(number):
        pairs = [
            (source.at[pl.ds(block * rows + number * half, half), :], buffer.at[pl.ds(number * half, half), :])
            for source, buffer in zip(sources[:7], buffers[:7])
        ]
        count = chunks // 2
        pairs.append(
            (
                sources[7].at[pl.ds(block * chunks + number * count, count)],
                kept_states.at[pl.ds(number * count, count)],
            )
        )
        return pairs

    soon = started(part_of(1), load_sems)
    second = started(part_of(0), load_sems, 8)
    late = started(
        [
            (source if source.shape[0] == buffer.shape[0] else source.at[here, :], buffer)
            for source, buffer in zip(sources[8:], buffers[8:])
        ],
        load_sems,
        16,
    )
    for j in range(inner // LANES):
        column = lax.broadcasted_iota(jnp.int32, (2 * LANES, LANES), 1)
        line = lax.broadcasted_iota(jnp.int32, (2 * LANES, LANES), 0) % LANES
        owner = 2 * j + (line >= LANES // 2).astype(jnp.int32)
        picks[j] = (column == owner).astype(bf16)
    if first:
        for result in results:
            result[...] = jnp.zeros_like(result)
        pre_grad[rows : rows + 8, :] = jnp.zeros((8, inner), f32)
        state_pre[rows : rows + 8, :] = jnp.zeros((8, 256), f32)
    else:
        for result, value in zip(results, earlier):
            result[...] = value[...]
        pre_grad[rows : rows + 8, :] = earlier[1][:, :inner]
        state_pre[rows : rows + 8, :] = earlier[1][:, inner:]
    settle(soon)

    def chunk(turn, carry):
        index = chunks - 1 - turn

        @pl.when(turn == chunks // 2)
        def _():
            settle(second)

        first_row = pl.multiple_of(index * CHUNK, CHUNK)
        at = pl.ds(first_row, CHUNK)
        first_token = block * rows + index * CHUNK
        chunk_first = first_token.astype(f32)
        row_place = place(0).astype(f32) + chunk_first
        lane_place = place(1).astype(f32) + chunk_first
        start_row = marks[0:1, pl.ds(pl.multiple_of(block * rows + index * CHUNK, CHUNK), CHUNK)]
        start_column = stand(start_row)
        seen = (row_place <= lane_place) & (row_place >= start_row)
        last_start = (starts[first_token + CHUNK - 1] - sequence).astype(f32)
        carried = (last_start < chunk_first).astype(f32)
        ends = (row_place >= last_start).astype(f32)
        begins = (start_column < chunk_first).astype(f32)
        state_b = states[at, :LANES]
        state_c = states[at, LANES:]
        scores = jnp.where(seen, dot_nt(state_b, state_c), 0.0)
        step_raw = small_raw[at, 256:].astype(f32)
        field, step_size, levels = step_levels(step_raw, heads)
        levels_row = jnp.transpose(levels)
        state_low = state_grad[...].astype(bf16)
        carried_back[...] = dot(state_b, state_low)
        by_head[...] = spread_heads(step_size, levels, begins, ends, owners)
        low = low_lanes()
        score_grad = jnp.zeros((CHUNK, CHUNK), f32)
        level_grad = jnp.zeros((CHUNK, LANES), f32)
        inter_grad = jnp.zeros((CHUNK, LANES), f32)
        crossing_sum = jnp.zeros((8, LANES), f32)
        step_grad = jnp.zeros((CHUNK, LANES), f32)
        for j in range(inner // LANES):
            lanes = slice(j * LANES, (j + 1) * LANES)
            pick = picks[j]
            mix = mixed[at, lanes]
            grad = mixer_grad[at, lanes].astype(f32)
            value = mixer_in[at, lanes].astype(f32)
            skip = chan[5:6, lanes]
            chan_sums[0:8, lanes] += fold(grad * value)
            step_pair = by_head[0:CHUNK, lanes]
            beginning = by_head[CHUNK : 2 * CHUNK, lanes]
            ending = by_head[2 * CHUNK : 3 * CHUNK, lanes]
            last = by_head[3 * CHUNK : 3 * CHUNK + 1, lanes]
            stepped = value * step_pair
            stepped_low = stepped.astype(bf16)
            stacked = jnp.concatenate(
                [jnp.where(low, grad, 0.0), jnp.where(low, 0.0, grad)], axis=0
            ).astype(bf16)
            cells = dot_nt(stepped_low, stacked)
            weights = []
            for k in range(2):
                h = 2 * j + k
                level = spread(levels[:, h : h + 1])
                damping = jnp.exp2(jnp.minimum(levels_row[h : h + 1, :] - level, 0.0))
                weights.append((scores * damping).astype(bf16))
                score_grad += cells[:, k * CHUNK : (k + 1) * CHUNK] * damping
            within = dot(jnp.concatenate(weights, axis=1), stacked)
            beyond = ending * carried_back[:, lanes]
            value_grad = within + beyond
            ends_low[:, lanes] = (stepped * ending).astype(bf16)
            begins_low[:, lanes] = (grad * beginning).astype(bf16)
            behind = state_grad[:, lanes]
            crossing = fold(behind * kept_states[index, :, lanes].astype(f32))
            crossing_sum += dot(halves(crossing), pick)
            state_grad[:, lanes] = behind * (carried * last)
            rows_flow = grad * (mix - skip * value) - stepped_low.astype(f32) * within
            level_grad += dot(halves(rows_flow), pick)
            inter_grad += dot((stepped * beyond).astype(bf16), pick[:LANES])
            step_grad += dot((value * value_grad).astype(bf16), pick[:LANES])
            pre_grad[at, lanes] = (step_pair * value_grad + skip * grad) * slope[
                at, lanes
            ].astype(f32)
        state_grad[...] += dot_tn(state_c, begins_low[...])
        score_low = jnp.where(seen, score_grad, 0.0).astype(bf16)
        state_pre[at, :LANES] = (
            dot(score_low, state_c) + dot_nt(ends_low[...], state_low)
        ) * state_slope[at, :LANES].astype(f32)
        state_pre[at, LANES:] = (
            dot_tn(score_low, state_b) + dot_nt(begins_low[...], kept_states[index])
        ) * state_slope[at, LANES:].astype(f32)
        onward = (place(0) <= place(1)).astype(f32)
        before = (place(0) > place(1)).astype(f32)
        across = jnp.sum(crossing_sum, axis=0, keepdims=True) * (
            carried * jnp.exp2(levels[CHUNK - 1 : CHUNK, :])
        )
        reach = dot(onward, level_grad, highest) + dot(before, inter_grad, highest) + across
        rates = heads[2:3, :]
        field_grad = (step_grad + reach * rates) * sigmoid(field)
        small_low[at, 256:] = field_grad.astype(bf16)
        head_sums[0:8, :] += fold(field_grad)
        head_sums[8:16, :] += fold(reach * step_size * rates)
        return carry

    lax.fori_loop(0, chunks, chunk, 0)
    settle(late)

    def unconv(index, carry):
        first_row = pl.multiple_of(index * CHUNK, CHUNK)
        at = pl.ds(first_row, CHUNK)
        left = stand(marks[1:2, pl.ds(pl.multiple_of(block * rows + index * CHUNK, CHUNK), CHUNK)])
        kept = [(left >= k).astype(f32) for k in range(1, 4)]

        def tile(window, value, taps, lanes, totals, line):
            own = window[:CHUNK]
            total = taps[0:1, lanes] * own
            totals[line : line + 8, lanes] += fold(value * own)
            for k in range(1, 4):
                moved = kept[k - 1] * window[k : k + CHUNK]
                total += taps[k : k + 1, lanes] * moved
                totals[line + 8 * k : line + 8 * k + 8, lanes] += fold(value * moved)
            totals[line + 32 : line + 40, lanes] += fold(own)
            return total.astype(bf16)

        for j in range(inner // LANES):
            lanes = slice(j * LANES, (j + 1) * LANES)
            mixer_low[at, lanes] = tile(
                pre_grad[pl.ds(first_row, CHUNK + 8), lanes],
                mixer_raw[at, lanes].astype(f32),
                chan,
                lanes,
                chan_sums,
                8,
            )
        for j in range(2):
            lanes = slice(j * LANES, (j + 1) * LANES)
            small_low[at, lanes] = tile(
                state_pre[pl.ds(first_row, CHUNK + 8), lanes],
                small_raw[at, lanes].astype(f32),
                state_chan,
                lanes,
                state_sums,
                0,
            )
        return carry

    lax.fori_loop(0, chunks, unconv, 0)
    stores = started(
        [(mixer_low, mixer_home.at[here, :]), (small_low, small_home.at[here, :])], store_sems
    )
    for start in range(0, width, 256):
        lanes = slice(start, start + 256)
        normed_grad[:, lanes] = (
            dot_nt(gate_low[...], gate_weight[lanes, :])
            + dot_nt(mixer_low[...], input_weight[lanes, :])
            + dot_nt(small_low[...], state_weight[lanes, :])
        )

    def unnorm(part, index, carry):
        at = pl.ds(pl.multiple_of(index * 16, 16), 16)
        from_row = pl.ds(pl.multiple_of(part * part_rows + index * 16, 16), 16)
        values = tokens[from_row, :].astype(f32)
        inverse = lax.rsqrt(jnp.mean(values * values, axis=-1, keepdims=True) + epsilon)
        unit = values * inverse
        grad = normed_grad[from_row, :]
        gain_sums[...] += fold(grad * unit)
        grad = grad * gain[...]
        out = partials[part]
        out[at, :] = (
            inverse * (grad - unit * jnp.mean(grad * unit, axis=-1, keepdims=True))
        ).astype(bf16)
        return carry

    part_rows = partials[0].shape[0]
    for part in range(len(partials)):
        lax.fori_loop(0, part_rows // 16, functools.partial(unnorm, part), 0, unroll=2)
    halo_out[:, :inner] = pre_grad[0:8, :]
    halo_out[:, inner:] = state_pre[0:8, :]
    settle(stores)


def backward(block, starts, marks, tokens, params, saved, grads, carry, earlier, after, parts):
    gain, gate_weight, input_weight, small_weight, *tables, _ = params
    tables = [gain, *tables]
    length, width = tokens.shape
    inner = gate_weight.shape[1]
    chunks = ROWS // CHUNK
    (gate_raw, mixer_raw, small_raw, mixer_in, slope, states, state_slope, mixed, _, kept) = saved
    mixer_grad, gate_low = grads
    sources = [
        mixed,
        mixer_grad,
        mixer_in,
        slope,
        small_raw,
        states,
        state_slope,
        kept,
        mixer_raw,
        gate_low,
        gate_weight,
        input_weight,
        small_weight,
        tokens,
    ]
    operands = [starts, marks, *tables, *sources, *carry]
    in_specs = [SMEM, *wholes([marks, *tables]), *[HBM] * len(sources), *wholes(carry)]
    aliases = {}
    if earlier is not None:
        aliases = {len(operands) + k: k for k in range(2)}
        in_specs += [HBM] * 2
        operands += list(earlier)
    operands += list(after)
    in_specs += [ANY] * len(after)
    results = [
        (LANES, inner),
        (8, inner + 256),
        (48, inner),
        (40, 256),
        (16, LANES),
        (8, width),
    ]
    outs = pl.pallas_call(
        functools.partial(
            backward_kernel,
            block=block,
            first=not carry,
            unread=len(aliases) + len(after),
            parts=parts,
        ),
        grid=(1,),
        in_specs=in_specs,
        out_specs=[HBM] * 2
        + [whole((ROWS // parts, width))] * parts
        + [whole(shape) for shape in results],
        out_shape=[
            jax.ShapeDtypeStruct((length, inner), bf16),
            jax.ShapeDtypeStruct((length, 384), bf16),
            *[jax.ShapeDtypeStruct((ROWS // parts, width), bf16)] * parts,
            *[jax.ShapeDtypeStruct(shape, f32) for shape in results],
        ],
        scratch_shapes=[
            *[
                pltpu.VMEM((chunks, LANES, inner), bf16)
                if source.ndim == 3
                else pltpu.VMEM(
                    (ROWS if source.shape[0] == length else source.shape[0], source.shape[1]),
                    source.dtype,
                )
                for source in sources
            ],
            pltpu.VMEM((ROWS, inner), bf16),
            pltpu.VMEM((ROWS, 384), bf16),
            pltpu.VMEM((ROWS + 8, inner), f32),
            pltpu.VMEM((ROWS + 8, 256), f32),
            pltpu.VMEM((CHUNK, inner), bf16),
            pltpu.VMEM((CHUNK, inner), bf16),
            pltpu.VMEM((ROWS, width), f32),
            pltpu.VMEM((inner // LANES, 2 * LANES, LANES), bf16),
            pltpu.VMEM((CHUNK, inner), f32),
            pltpu.VMEM((3 * CHUNK + 8, inner), f32),
            pltpu.SemaphoreType.DMA((22,)),
            pltpu.SemaphoreType.DMA((2,)),
        ],
        input_output_aliases=aliases,
        compiler_params=pltpu.CompilerParams(vmem_limit_bytes=VMEM_BYTES),
        cost_estimate=BRIEF,
        name="backward_mix",
    )(*operands)
    return outs[:2], outs[2 : 2 + parts], outs[2 + parts :]


def pack(packed, chan_sums, gate_sums, head_sums, state_sums, gain_sums, step_lines):
    inner = chan_sums.shape[1]
    packed[...] = jnp.zeros_like(packed)
    total = lambda values: jnp.sum(values, axis=0, keepdims=True)
    for k in range(6):
        packed[k : k + 1, :inner] = total(chan_sums[8 * k : 8 * k + 8, :])
    packed[6:7, :inner] = total(gate_sums[...])
    for k in range(2):
        packed[7:8, k * LANES : (k + 1) * LANES] = total(head_sums[8 * k : 8 * k + 8, :])
    for k in range(5):
        packed[8 + k : 9 + k, :256] = total(state_sums[8 * k : 8 * k + 8, :])
    packed[13:14, :] = total(gain_sums[...])
    packed[16:32, :] = step_lines[0:16, :]


def weight_kernel(left, *rest, rights, unread, packs):
    right, rest = rest[:rights], rest[rights:]
    sums, rest = rest[:packs], rest[packs + unread :]
    outs, totals = rest[: rights + bool(packs)], rest[rights + bool(packs) :]
    step = pl.program_id(0)

    @pl.when(step == 0)
    def _():
        for total in totals:
            total[...] = jnp.zeros_like(total)

    for start in range(0, left.shape[1], 256):
        columns = slice(start, start + 256)
        for item, total in zip(right, totals):
            total[columns, :] += dot_tn(left[:, columns], item[...])
        if packs:
            totals[rights][:, columns] += dot_tn(right[-1][:, 256:], left[:, columns])

    @pl.when(step == pl.num_programs(0) - 1)
    def _():
        if packs:
            packed = totals[rights + 1]
            pack(packed, *sums, totals[rights])
            outs[rights][...] = packed[...].astype(bf16)
        for out, total in zip(outs[:rights], totals):
            out[...] = total[:, : out.shape[1]].astype(bf16)


def weight_grads(left, rights, after, sums=()):
    length, height = left.shape
    rows_of = lambda columns: pl.BlockSpec((ROWS, columns), lambda i: (i, 0))
    shapes = [(height, item.shape[1]) for item in rights]
    outs, scratch = list(shapes), list(shapes)
    if sums:
        outs[-1] = (height, 256)
        outs.append((32, height))
        scratch += [(LANES, height), (32, height)]
    return pl.pallas_call(
        functools.partial(
            weight_kernel, rights=len(rights), unread=len(after), packs=len(sums)
        ),
        grid=(length // ROWS,),
        in_specs=[rows_of(height)]
        + [rows_of(item.shape[1]) for item in rights]
        + wholes(sums)
        + [ANY] * len(after),
        out_specs=[held(shape) for shape in outs],
        out_shape=[jax.ShapeDtypeStruct(shape, bf16) for shape in outs],
        scratch_shapes=[pltpu.VMEM(shape, f32) for shape in scratch],
        compiler_params=compiler_params(),
        cost_estimate=BRIEF,
        name="weight_grads",
    )(left, *rights, *sums, *after)


def land_kernel(take, total_home, moved_home, *rest, mode, unread):
    out_home, total, moved, out, load_sems, store_sems = rest[unread:]
    tiles = total.shape[0] // CHUNK
    part = [pl.ds(k * CHUNK, CHUNK) for k in range(tiles)]
    loads = [
        started(
            [
                (total_home.at[part[k], :], total.at[part[k], :]),
                (moved_home.at[part[k], :], moved.at[part[k], :]),
            ],
            load_sems,
            2 * k,
        )
        for k in range(tiles)
    ]
    stores = []
    for k in range(tiles):
        settle(loads[k])
        at = slice(k * CHUNK, (k + 1) * CHUNK)
        if mode == "add":
            out[at, :] = total[at, :] + moved[at, :]
        else:
            out[at, :] = jnp.where(take[0] > 0, moved[at, :], total[at, :])
        stores += started([(out.at[part[k], :], out_home.at[part[k], :])], store_sems, k)
    settle(stores)


def finish_kernel(
    take, total_home, moved_home, base_home, sums, *rest, adds, inner, row, unread
):
    out_home, total, moved, base, out, load_sems, store_sems = rest[unread:]
    rows = total.shape[0]
    tiles = rows // CHUNK
    at_home = lambda k: pl.ds(row + k * CHUNK, CHUNK)
    at_here = lambda k: pl.ds(k * CHUNK, CHUNK)

    def run(pairs):
        loads = [
            started(
                [(home.at[at_here(k), :], here.at[at_here(k), :]) for home, here in pairs]
                + [(base_home.at[at_home(k), :], base.at[at_here(k), :])],
                load_sems,
                3 * k,
            )
            for k in range(tiles)
        ]
        stores = []
        for k in range(tiles):
            at = slice(k * CHUNK, (k + 1) * CHUNK)
            if inner:
                scale = stand(
                    lax.rsqrt(
                        sums[0:1, row + k * CHUNK : row + (k + 1) * CHUNK] / inner + epsilon
                    )
                )
            settle(loads[k])
            for start in range(0, total.shape[1], LANES):
                lanes = slice(start, start + LANES)
                value = pairs[0][1][at, lanes].astype(f32)
                for _, here in pairs[1:]:
                    value += here[at, lanes].astype(f32)
                if inner:
                    value = value * scale
                out[at, lanes] = (value + base[at, lanes].astype(f32)).astype(bf16)
            stores += started(
                [(out.at[at_here(k), :], out_home.at[at_home(k), :])], store_sems, k
            )
        settle(stores)

    if adds:
        run([(moved_home, moved), (total_home, total)])
        return

    @pl.when(take[0] > 0)
    def _():
        run([(moved_home, moved)])

    @pl.when(take[0] <= 0)
    def _():
        run([(total_home, total)])


def land(take, total, moved, mode, after):
    rows, width = total.shape
    return pl.pallas_call(
        functools.partial(land_kernel, mode=mode, unread=len(after)),
        in_specs=[SMEM, HBM, HBM] + [ANY] * len(after),
        out_specs=HBM,
        out_shape=jax.ShapeDtypeStruct((rows, width), bf16),
        scratch_shapes=[
            *[pltpu.VMEM((rows, width), bf16)] * 3,
            pltpu.SemaphoreType.DMA((2 * rows // CHUNK,)),
            pltpu.SemaphoreType.DMA((rows // CHUNK,)),
        ],
        compiler_params=pltpu.CompilerParams(vmem_limit_bytes=VMEM_BYTES),
        cost_estimate=BRIEF,
        name="line_land",
    )(take, total, moved, *after)


def finish(take, total, moved, adds, base, sums, inner, row, earlier, after):
    rows, width = total.shape
    operands = [take, total, moved, base, sums]
    in_specs = [SMEM, HBM, HBM, HBM, whole(sums.shape)]
    aliases = {}
    if earlier is not None:
        aliases = {len(operands): 0}
        operands += [earlier]
        in_specs += [HBM]
    after = [item for item in after if item is not earlier]
    operands += after
    in_specs += [ANY] * len(after)
    return pl.pallas_call(
        functools.partial(
            finish_kernel,
            adds=adds,
            inner=inner,
            row=row,
            unread=len(aliases) + len(after),
        ),
        in_specs=in_specs,
        out_specs=HBM,
        grid=(1,),
        out_shape=jax.ShapeDtypeStruct(base.shape, bf16),
        scratch_shapes=[
            *[pltpu.VMEM((rows, width), bf16)] * 4,
            pltpu.SemaphoreType.DMA((3 * rows // CHUNK,)),
            pltpu.SemaphoreType.DMA((rows // CHUNK,)),
        ],
        input_output_aliases=aliases,
        compiler_params=pltpu.CompilerParams(vmem_limit_bytes=VMEM_BYTES),
        cost_estimate=BRIEF,
        name="line_finish",
    )(*operands)


class Line:
    def __init__(self, members, me):
        middle = members // 2
        self.steps = [
            ("add", [(near, near + 1), (members - 1 - near, members - 2 - near)], near)
            for near in range(middle - 1)
        ]
        self.steps.append(("add", [(middle - 1, middle), (middle, middle - 1)], 0))
        self.steps += [
            ("take", [(near + 1, near), (members - 2 - near, members - 1 - near)], near)
            for near in reversed(range(middle - 1))
        ]
        self.takes = [
            ((me == near) | (me == members - 1 - near)).astype(jnp.int32)[None]
            for _, _, near in self.steps
        ]
        self.flying = [[] for _ in self.steps]
        self.outs = {}

    def push(self, total, name, row):
        self.launch(0, total, name, row)

    def launch(self, step, total, name, row):
        moved = lax.ppermute(total, "tensor", self.steps[step][1])
        self.flying[step].append((total, moved, name, row))

    def tick(self, ending, after, first=1, then=1, last=1):
        ready = []
        for step, queue in enumerate(self.flying):
            count = last if step == len(self.flying) - 1 else then if step else first
            for _ in range(min(len(queue), count)):
                ready.append((step, queue.pop(0)))
        for step, (total, moved, name, row) in ready:
            mode = self.steps[step][0]
            if step < len(self.steps) - 1:
                total = land(self.takes[step], total, moved, mode, after)
                self.launch(step + 1, total, name, row)
                after = [total]
            else:
                base, sums, inner = ending[name]
                out = finish(
                    self.takes[step],
                    total,
                    moved,
                    mode == "add",
                    base,
                    sums,
                    inner,
                    row,
                    self.outs.get(name),
                    after,
                )
                self.outs[name] = out
                after = [out]
        return after

    def busy(self):
        return any(self.flying)

    def pending(self):
        return sum(len(queue) for queue in self.flying)


def sum_over(values, axis, size):
    parts = [values]
    for k in range(1, size):
        parts.append(lax.ppermute(values, axis, [(i, i ^ k) for i in range(size)]))
    while len(parts) > 1:
        parts = [parts[k] + parts[k + 1] for k in range(0, len(parts), 2)]
    return parts[0]


def part_kernel(me, lines, values, *rest, size, unread):
    outs = rest[unread:]
    rows = values.shape[0] // size
    for k in range(size):
        first = pl.multiple_of((me[0] ^ k) * rows, 32)
        outs[k][:rows, :] = values[pl.ds(first, rows), :]
        for j in range(lines.shape[1] // 256):
            at = slice(rows + 16 * j, rows + 16 * j + 16)
            outs[k][at, :] = lines[0:16, 256 * j : 256 * j + 256]


def join_kernel(*refs):
    parts, (line_sums, value_sums) = list(refs[:-2]), refs[-2:]
    rows = value_sums.shape[0]
    for out, at in [(value_sums, slice(0, rows)), (line_sums, slice(rows, None))]:
        totals = [part[at, :].astype(f32) for part in parts]
        while len(totals) > 1:
            totals = [totals[k] + totals[k + 1] for k in range(0, len(totals), 2)]
        out[...] = totals[0]


def sum_pieces(lines, values, axis, size, me, after):
    rows = values.shape[0] // size
    height = rows + 16 * (lines.shape[1] // 256)
    shape = jax.ShapeDtypeStruct((height, 256), bf16)
    own, *sent = pl.pallas_call(
        functools.partial(part_kernel, size=size, unread=len(after)),
        grid=(1,),
        in_specs=[SMEM, *wholes([lines, values]), *[ANY] * len(after)],
        out_specs=[whole(shape.shape)] * size,
        out_shape=[shape] * size,
        compiler_params=compiler_params(),
        cost_estimate=BRIEF,
        name="part_pieces",
    )(me[None], lines, values, *after)
    parts = [own] + [
        lax.ppermute(sent[k - 1], axis, [(i, i ^ k) for i in range(size)])
        for k in range(1, size)
    ]
    outs = [(height - rows, 256), (rows, 256)]
    line_sums, value_sums = pl.pallas_call(
        join_kernel,
        grid=(1,),
        in_specs=wholes(parts),
        out_specs=[whole(item) for item in outs],
        out_shape=[jax.ShapeDtypeStruct(item, f32) for item in outs],
        compiler_params=compiler_params(),
        cost_estimate=BRIEF,
        name="join_pieces",
    )(*parts)
    return line_sums.reshape(-1, 16, 256), value_sums


def on_device(
    block_input,
    segment_ids,
    norm_gain,
    gate_weight,
    input_weight,
    state_weight,
    step_weight,
    mixer_conv,
    mixer_shift,
    state_conv,
    state_shift,
    step_bias,
    decay_log,
    skip_gain,
    gate_gain,
    out_weight,
    out_grad,
):
    length, width = block_input.shape
    inner = gate_weight.shape[1]
    heads_local = step_weight.shape[1]
    groups = lax.axis_size("tensor")
    member = lax.axis_index("tensor")
    columns = width // groups
    total_inner = inner * groups

    gain, marks, chan, state_chan, heads, small_weight, owners = prepare(
        length,
        width,
        inner,
        (
            segment_ids,
            norm_gain,
            mixer_conv,
            mixer_shift,
            state_conv,
            state_shift,
            step_bias,
            decay_log,
            skip_gain,
            gate_gain,
            state_weight,
            step_weight,
        ),
    )
    params = (
        gain,
        gate_weight,
        input_weight,
        small_weight,
        chan,
        state_chan,
        heads,
        owners,
        out_weight,
    )
    blocks = length // ROWS
    line = Line(groups, member)
    saved, carry, after = None, [], []
    block_sums, waiting = [], []
    for block in range(blocks):
        early = block < blocks // 2
        saved, partial, sums, carry = forward(
            block,
            segment_ids,
            marks,
            block_input,
            out_grad,
            params,
            carry,
            saved,
            after,
            early,
        )
        block_sums.append(sums)
        after = [partial]
        if early:
            line.push(partial, "output", block * ROWS)
        else:
            waiting.append(partial)
        if block == blocks // 2:
            after = line.tick({}, after)
    sums = jnp.concatenate(block_sums, axis=1)
    after = line.tick({}, [sums])
    sums = sum_over(sums, "tensor", groups)
    partials = project_rows(waiting, out_weight, [*after, sums])
    ending = {
        "output": (block_input, sums, total_inner),
        "input": (out_grad, sums, 0),
    }
    for k, partial in enumerate(partials):
        line.push(partial, "output", (blocks // 2 + k) * ROWS)
    after = [partials[0]]
    normed, *saved = saved
    grad_low, gate_low, gate_out, gate_sums = gate_grads(
        total_inner, sums, saved[7], saved[0], saved[8], chan, after
    )
    (gate_weight_grad,) = weight_grads(normed, [gate_low], [grad_low])
    (out_weight_grad,) = weight_grads(gate_out, [out_grad], [gate_weight_grad])
    after = [out_weight_grad]
    gate_weight_grad, out_weight_grad = lax.psum((gate_weight_grad, out_weight_grad), "dp")
    after = line.tick(ending, after)
    lows, carry = None, []
    for block in reversed(range(blocks)):
        lows, partials, carry = backward(
            block,
            segment_ids,
            marks,
            block_input,
            params,
            saved,
            (grad_low, gate_low),
            carry,
            lows,
            after + [gate_weight_grad, out_weight_grad] if block == blocks // 2 - 1 else after,
            2 if block == 0 else 1,
        )
        after = [partials[0]]
        for k, partial in enumerate(partials):
            line.push(partial, "input", block * ROWS + k * partial.shape[0])
        if block > 0:
            after = line.tick(ending, after)
        else:
            after = line.tick(ending, after, then=0, last=0)
    mixer_low, small_low = lows
    chan_sums, state_sums, head_sums, gain_sums = carry[2:]
    weight_sums = weight_grads(
        normed,
        [mixer_low, small_low],
        after,
        (chan_sums, gate_sums, head_sums, state_sums, gain_sums),
    )
    after = [weight_sums[0]]
    input_weight_grad, state_weight_grad, packed = lax.psum(tuple(weight_sums), "dp")
    after = line.tick(ending, after, first=2, then=2)
    ticks = 0
    while line.busy():
        after = after + [input_weight_grad] if ticks == 1 else after
        if line.pending() == 1:
            line_sums, state_weight_grad = sum_pieces(
                packed, state_weight_grad, "tensor", groups, member, after
            )
        after = line.tick(ending, after, first=2)
        ticks += 1
    block_output = line.outs["output"]
    input_grad = line.outs["input"]
    packed = packed.astype(f32)
    return (
        block_output,
        input_grad,
        lax.dynamic_slice_in_dim(line_sums[:, 13].reshape(-1), member * columns, columns, 0),
        gate_weight_grad.astype(f32),
        input_weight_grad.astype(f32),
        state_weight_grad,
        packed[16 : 16 + heads_local].T,
        packed[1:5, :inner],
        packed[5, :inner],
        line_sums[0, 8:12],
        line_sums[0, 12],
        packed[7, :heads_local],
        packed[7, LANES : LANES + heads_local],
        packed[0, :inner].reshape(heads_local, inner // heads_local).sum(axis=1),
        packed[6, :inner],
        out_weight_grad.astype(f32),
    )


def solution(mesh):
    return jax.shard_map(
        on_device,
        mesh=mesh,
        in_specs=(
            P("dp", None),
            P("dp"),
            P(),
            P(None, "tensor"),
            P(None, "tensor"),
            P(),
            P(None, "tensor"),
            P(None, "tensor"),
            P("tensor"),
            P(),
            P(),
            P("tensor"),
            P("tensor"),
            P("tensor"),
            P("tensor"),
            P("tensor", None),
            P("dp", None),
        ),
        out_specs=(
            P("dp", None),
            P("dp", None),
            P("tensor"),
            P(None, "tensor"),
            P(None, "tensor"),
            P("tensor", None),
            P(None, "tensor"),
            P(None, "tensor"),
            P("tensor"),
            P(),
            P(),
            P("tensor"),
            P("tensor"),
            P("tensor"),
            P("tensor"),
            P("tensor", None),
        ),
        check_vma=False,
    )
```

```python
import functools

import jax
import jax.numpy as jnp
from jax import lax
from jax.experimental import pallas as pl
from jax.experimental.pallas import tpu as pltpu
from jax.sharding import PartitionSpec as P

epsilon = 1e-05
highest = lax.Precision.HIGHEST
f32 = jnp.float32
bf16 = jnp.bfloat16
LOG2E = 1.4426950408889634
CHUNK = 128
LANES = 128
ROWS = 512
VMEM_BYTES = 61 * 1024 * 1024
LONG = pl.CostEstimate(flops=10**11, bytes_accessed=3 * 10**8, transcendentals=0)
BRIEF = pl.CostEstimate(flops=1000, bytes_accessed=1000, transcendentals=0)


def dot(left, right, precision=None):
    return lax.dot_general(
        left, right, (((1,), (0,)), ((), ())), precision=precision, preferred_element_type=f32
    )


def dot_nt(left, right):
    return lax.dot_general(left, right, (((1,), (1,)), ((), ())), preferred_element_type=f32)


def dot_tn(left, right):
    return lax.dot_general(left, right, (((0,), (0,)), ((), ())), preferred_element_type=f32)


def sigmoid(values):
    return 0.5 * jnp.tanh(0.5 * values) + 0.5


def softplus(values):
    power = jnp.exp(-jnp.abs(values))
    above = 1.0 + power
    exact = above == 1.0
    tail = jnp.log(above) * (power / jnp.where(exact, 1.0, above - 1.0))
    return jnp.maximum(values, 0.0) + jnp.where(exact, power, tail)


def spread(column):
    return jnp.broadcast_to(column, (column.shape[0], LANES))


def stand(row):
    return jnp.transpose(jnp.broadcast_to(row, (CHUNK, CHUNK)))


def fold(values):
    return jnp.sum(values.reshape(values.shape[0] // 8, 8, values.shape[1]), axis=0)


def halves(values):
    upper = values.astype(bf16)
    lower = (values - upper.astype(f32)).astype(bf16)
    return jnp.concatenate([upper, lower], axis=1)


def place(axis):
    return lax.broadcasted_iota(jnp.int32, (CHUNK, CHUNK), axis)


def low_lanes():
    return place(1) < LANES // 2


def column_step(width):
    return 256 if width % 256 == 0 else 128


def conv_pre(window, taps, lanes, kept):
    total = taps[4:5, lanes] + taps[0:1, lanes] * window[8:]
    for offset in range(1, 4):
        moved = window[8 - offset : 8 - offset + CHUNK]
        total = total + taps[offset : offset + 1, lanes] * (kept[offset - 1] * moved)
    return total


def step_levels(step_raw, heads):
    field = step_raw + heads[0:1, :]
    step = softplus(field)
    tri = (place(0) >= place(1)).astype(bf16)
    levels = dot(tri, halves(step * heads[1:2, :]))
    levels = levels[:, :LANES] + levels[:, LANES:]
    return field, step, levels


HBM = pl.BlockSpec(memory_space=pl.ANY)
SMEM = pl.BlockSpec(memory_space=pltpu.SMEM)
ANY = pl.BlockSpec(memory_space=pl.ANY)


def spread_heads(step_size, levels, begins, ends, owners):
    end_level = levels[CHUNK - 1 : CHUNK, :]
    last = jnp.broadcast_to(jnp.exp2(end_level), (8, LANES))
    compact = jnp.concatenate(
        [
            halves(step_size),
            halves(begins * jnp.exp2(levels)),
            halves(ends * jnp.exp2(end_level - levels)),
            halves(last),
        ],
        axis=0,
    )
    return dot(compact, owners[...])


def whole(shape):
    return pl.BlockSpec(shape, lambda i: (0,) * len(shape), pipeline_mode=pl.Buffered(1))


def held(shape):
    return pl.BlockSpec(shape, lambda i: (0,) * len(shape))


def wholes(items):
    return [whole(item.shape) for item in items]


def started(pairs, semaphores, first=0):
    copies = []
    for k, (source, target) in enumerate(pairs):
        copy = pltpu.make_async_copy(source, target, semaphores.at[first + k])
        copy.start()
        copies.append(copy)
    return copies


def settle(copies):
    for copy in copies:
        copy.wait()


def line_of(values):
    return values[...].reshape(1, values.shape[0])


def prepare_kernel(
    segments,
    norm_gain,
    mixer_conv,
    mixer_shift,
    state_conv,
    state_shift,
    step_bias,
    decay_log,
    skip_gain,
    gate_gain,
    state_weight,
    step_weight,
    gain,
    marks,
    chan,
    state_chan,
    heads,
    small_weight,
    owners,
):
    length = segments.shape[0]
    inner = gate_gain.shape[0]
    count = step_bias.shape[0]
    gain[...] = line_of(norm_gain)
    place_line = lax.broadcasted_iota(jnp.int32, (8, length), 1)
    first = lax.axis_index("dp") * length
    start = jnp.broadcast_to(line_of(segments), (8, length)) - first
    left = jnp.zeros((8, length), f32)
    for k in range(1, 4):
        later = pltpu.roll(start, length - k, 1)
        same = (later <= place_line) & (place_line < length - k)
        left += same.astype(f32)
    marks[0:1, :] = start[0:1].astype(f32)
    marks[1:2, :] = left[0:1]
    heads[...] = jnp.zeros_like(heads)
    rates = -jnp.exp(line_of(decay_log))
    heads[0:1, :count] = line_of(step_bias)
    heads[1:2, :count] = rates * LOG2E
    heads[2:3, :count] = rates
    heads[3:4, :count] = line_of(skip_gain)
    chan[...] = jnp.zeros_like(chan)
    chan[0:4, :] = mixer_conv[...]
    chan[4:5, :] = line_of(mixer_shift)
    owner = lax.broadcasted_iota(jnp.int32, (LANES, inner), 0)
    channel = lax.broadcasted_iota(jnp.int32, (LANES, inner), 1)
    owns = (channel // (inner // count) == owner).astype(f32)
    chan[5:6, :] = dot(heads[...], owns, highest)[3:4]
    owners[:LANES, :] = owns.astype(bf16)
    owners[LANES:, :] = owns.astype(bf16)
    chan[6:7, :] = line_of(gate_gain)
    state_chan[...] = jnp.zeros_like(state_chan)
    state_chan[0:4, :] = state_conv[...]
    state_chan[4:5, :] = line_of(state_shift)
    small_weight[:, :256] = state_weight[...]
    small_weight[:, 256:] = jnp.zeros((small_weight.shape[0], LANES), bf16)
    small_weight[:, 256 : 256 + count] = step_weight[...]


def prepare(length, width, inner, values):
    shapes = [
        ((1, width), f32),
        ((2, length), f32),
        ((8, inner), f32),
        ((8, 256), f32),
        ((8, LANES), f32),
        ((width, 384), bf16),
        ((2 * LANES, inner), bf16),
    ]
    return pl.pallas_call(
        prepare_kernel,
        grid=(1,),
        in_specs=wholes(values),
        out_specs=[whole(shape) for shape, _ in shapes],
        out_shape=[jax.ShapeDtypeStruct(shape, kind) for shape, kind in shapes],
        compiler_params=pltpu.CompilerParams(vmem_limit_bytes=VMEM_BYTES),
        cost_estimate=BRIEF,
        name="prepare",
    )(*values)


def forward_kernel(
    starts,
    marks,
    tokens_home,
    grads_home,
    input_home,
    gate_home,
    small_home,
    out_home,
    gain,
    chan,
    state_chan,
    heads,
    owners,
    *rest,
    block,
    first,
    unread,
    project,
):
    if not first:
        state_in, halo_in = rest[:2]
        rest = rest[2:]
    rest = rest[unread:]
    homes, rest = rest[:11], rest[11:]
    (
        partial,
        sums,
        state,
        halo_out,
        tokens,
        grads,
        normed,
        gate_raw,
        mixer_raw,
        small_raw,
        mixer_in,
        slope,
        states,
        state_slope,
        mixed,
        back,
        kept_states,
        raw,
        state_raw,
        gated_low,
        wide_back,
        input_weight,
        gate_weight,
        state_weight,
        out_weight,
        damped,
        carried_out,
        by_head,
        load_sems,
        store_sems,
    ) = rest
    rows, width = tokens.shape
    inner = gate_weight.shape[1]
    wide = column_step(inner)
    here = pl.ds(block * rows, rows)
    sequence = lax.axis_index("dp") * starts.shape[0]
    loads = started(
        [
            (tokens_home.at[here, :], tokens),
            (small_home, state_weight),
            (input_home, input_weight),
            (gate_home, gate_weight),
            (grads_home.at[here, :], grads),
            (out_home, out_weight),
        ],
        load_sems,
    )
    if first:
        state[...] = jnp.zeros_like(state)
        raw[0:8, :] = jnp.zeros((8, inner), f32)
        state_raw[0:8, :] = jnp.zeros((8, 256), f32)
    else:
        state[...] = state_in[...]
        raw[0:8, :] = halo_in[:, :inner]
        state_raw[0:8, :] = halo_in[:, inner:]

    def norm_rows(index, carry):
        at = pl.ds(pl.multiple_of(index * 16, 16), 16)
        values = tokens[at, :].astype(f32)
        inverse = lax.rsqrt(jnp.mean(values * values, axis=-1, keepdims=True) + epsilon)
        normed[at, :] = (values * inverse * gain[...]).astype(bf16)
        return carry

    settle(loads[:1])
    lax.fori_loop(0, rows // 16, norm_rows, 0, unroll=4)
    stores = started([(normed, homes[0].at[here, :])], store_sems, 0)
    settle(loads[1:2])
    small = dot(normed[...], state_weight[...]).astype(bf16)
    small_raw[...] = small
    state_raw[8 : 8 + rows, :] = small[:, :256].astype(f32)
    settle(loads[2:4])
    for start in range(0, inner, wide):
        lanes = slice(start, start + wide)
        low = dot(normed[...], input_weight[:, lanes]).astype(bf16)
        mixer_raw[:, lanes] = low
        raw[8 : 8 + rows, lanes] = low.astype(f32)
        gate_raw[:, lanes] = dot(normed[...], gate_weight[:, lanes]).astype(bf16)
    settle(loads[4:])
    for start in range(0, inner, wide):
        lanes = slice(start, start + wide)
        wide_back[:, lanes] = dot_nt(grads[...], out_weight[lanes, :])

    stores += started(
        [
            (gate_raw, homes[1].at[here, :]),
            (mixer_raw, homes[2].at[here, :]),
            (small_raw, homes[3].at[here, :]),
        ],
        store_sems,
        1,
    )

    def chunk(index, carry):
        first_row = pl.multiple_of(index * CHUNK, CHUNK)
        at = pl.ds(first_row, CHUNK)
        first_token = block * rows + index * CHUNK
        chunk_first = first_token.astype(f32)
        row_place = place(0).astype(f32) + chunk_first
        lane_place = place(1).astype(f32) + chunk_first
        start_column = stand(marks[0:1, pl.ds(pl.multiple_of(block * rows + index * CHUNK, CHUNK), CHUNK)])
        age = row_place - start_column
        kept = [(age >= k).astype(f32) for k in range(1, 4)]
        for j in range(2):
            lanes = slice(j * LANES, (j + 1) * LANES)
            pre = conv_pre(
                state_raw[pl.ds(first_row, CHUNK + 8), lanes], state_chan, lanes, kept
            )
            sigma = sigmoid(pre)
            act = pre * sigma
            states[at, lanes] = act.astype(bf16)
            state_slope[at, lanes] = (sigma + act * (1.0 - sigma)).astype(bf16)
        state_b = states[at, :LANES]
        state_c = states[at, LANES:]
        scores = jnp.where(
            (lane_place <= row_place) & (lane_place >= start_column),
            dot_nt(state_c, state_b),
            0.0,
        )
        _, step_size, levels = step_levels(small_raw[at, 256:].astype(f32), heads)
        levels_row = jnp.transpose(levels)
        last_start = (starts[first_token + CHUNK - 1] - sequence).astype(f32)
        carried = (last_start < chunk_first).astype(f32)
        ends = (row_place >= last_start).astype(f32)
        begins = (start_column < chunk_first).astype(f32)
        state_low = state[...].astype(bf16)
        kept_states[index] = state_low
        carried_out[...] = dot(state_c, state_low)
        by_head[...] = spread_heads(step_size, levels, begins, ends, owners)
        low = low_lanes()
        squares = jnp.zeros((CHUNK, LANES), f32)
        crosses = jnp.zeros((CHUNK, LANES), f32)
        for j in range(inner // LANES):
            lanes = slice(j * LANES, (j + 1) * LANES)
            pre = conv_pre(raw[pl.ds(first_row, CHUNK + 8), lanes], chan, lanes, kept)
            sigma = sigmoid(pre)
            act = pre * sigma
            value = act.astype(bf16)
            mixer_in[at, lanes] = value
            slope[at, lanes] = (sigma + act * (1.0 - sigma)).astype(bf16)
            value = value.astype(f32)
            weights = []
            for h in (2 * j, 2 * j + 1):
                level = spread(levels[:, h : h + 1])
                damping = jnp.exp2(jnp.minimum(level - levels_row[h : h + 1, :], 0.0))
                weights.append((scores * damping).astype(bf16))
            step_pair = by_head[0:CHUNK, lanes]
            beginning = by_head[CHUNK : 2 * CHUNK, lanes]
            ending = by_head[2 * CHUNK : 3 * CHUNK, lanes]
            last = by_head[3 * CHUNK : 3 * CHUNK + 1, lanes]
            stepped = value * step_pair
            stacked = jnp.concatenate(
                [jnp.where(low, stepped, 0.0), jnp.where(low, 0.0, stepped)], axis=0
            ).astype(bf16)
            result = dot(jnp.concatenate(weights, axis=1), stacked)
            result += beginning * carried_out[:, lanes]
            damped[:, lanes] = (stepped * ending).astype(bf16)
            state[:, lanes] = state[:, lanes] * (carried * last)
            result += chan[5:6, lanes] * value
            mixed[at, lanes] = result
            gate = gate_raw[at, lanes].astype(f32)
            gated = result * (gate * sigmoid(gate))
            squares += gated * gated
            gained = gated * chan[6:7, lanes]
            gated_low[at, lanes] = gained.astype(bf16)
            out_back = wide_back[at, lanes]
            back[at, lanes] = out_back.astype(bf16)
            crosses += out_back * gained
        state[...] += dot_tn(state_b, damped[...])
        sums[0:1, at] = jnp.sum(jnp.transpose(squares), axis=0, keepdims=True)
        sums[1:2, at] = jnp.sum(jnp.transpose(crosses), axis=0, keepdims=True)
        return carry

    lax.fori_loop(0, rows // CHUNK, chunk, 0)
    stores += started(
        [
            (mixer_in, homes[4].at[here, :]),
            (slope, homes[5].at[here, :]),
            (states, homes[6].at[here, :]),
            (state_slope, homes[7].at[here, :]),
            (mixed, homes[8].at[here, :]),
            (back, homes[9].at[here, :]),
            (kept_states, homes[10].at[pl.ds(block * (rows // CHUNK), rows // CHUNK)]),
        ],
        store_sems,
        4,
    )
    if project:
        for start in range(0, width, 512):
            lanes = slice(start, start + 512)
            partial[:, lanes] = dot(gated_low[...], out_weight[:, lanes]).astype(bf16)
    else:
        partial[...] = gated_low[...]
    halo_out[:, :inner] = raw[rows : rows + 8, :]
    halo_out[:, inner:] = state_raw[rows : rows + 8, :]
    settle(stores)


def forward(block, starts, marks, tokens, grads, params, carry, earlier, after, project):
    gain, gate_weight, input_weight, small_weight, *tables, out_weight = params
    tables = [gain, *tables]
    weights = [input_weight, gate_weight, small_weight, out_weight]
    length, width = tokens.shape
    inner = gate_weight.shape[1]
    chunks = ROWS // CHUNK
    stored = [
        (width, bf16),
        (inner, bf16),
        (inner, bf16),
        (384, bf16),
        (inner, bf16),
        (inner, bf16),
        (256, bf16),
        (256, bf16),
        (inner, f32),
        (inner, bf16),
    ]
    out_shape = [jax.ShapeDtypeStruct((length, columns), kind) for columns, kind in stored]
    out_shape += [jax.ShapeDtypeStruct((length // CHUNK, LANES, inner), bf16)]
    shared = len(out_shape)
    own = [
        ((ROWS, width if project else inner), bf16),
        ((2, ROWS), f32),
        ((LANES, inner), f32),
        ((8, inner + 256), f32),
    ]
    out_shape += [jax.ShapeDtypeStruct(shape, kind) for shape, kind in own]
    in_specs = [SMEM, whole(marks.shape)] + [HBM] * 6 + wholes(tables) + wholes(carry)
    operands = [starts, marks, tokens, grads, *weights, *tables, *carry]
    aliases = {}
    if earlier is not None:
        aliases = {len(operands) + k: k for k in range(shared)}
        in_specs += [HBM] * shared
        operands += list(earlier)
    operands += list(after)
    in_specs += [ANY] * len(after)
    outs = pl.pallas_call(
        functools.partial(
            forward_kernel,
            block=block,
            first=not carry,
            unread=len(aliases) + len(after),
            project=project,
        ),
        grid=(1,),
        in_specs=in_specs,
        out_specs=[HBM] * shared + [whole(shape) for shape, _ in own],
        out_shape=out_shape,
        scratch_shapes=[
            pltpu.VMEM((ROWS, width), bf16),
            pltpu.VMEM((ROWS, width), bf16),
            *[pltpu.VMEM((ROWS, columns), kind) for columns, kind in stored],
            pltpu.VMEM((chunks, LANES, inner), bf16),
            pltpu.VMEM((ROWS + 8, inner), f32),
            pltpu.VMEM((ROWS + 8, 256), f32),
            pltpu.VMEM((ROWS, inner), bf16),
            pltpu.VMEM((ROWS, inner), f32),
            *[pltpu.VMEM(item.shape, bf16) for item in weights],
            pltpu.VMEM((CHUNK, inner), bf16),
            pltpu.VMEM((CHUNK, inner), f32),
            pltpu.VMEM((3 * CHUNK + 8, inner), f32),
            pltpu.SemaphoreType.DMA((6,)),
            pltpu.SemaphoreType.DMA((11,)),
        ],
        input_output_aliases=aliases,
        compiler_params=pltpu.CompilerParams(vmem_limit_bytes=VMEM_BYTES),
        cost_estimate=BRIEF,
        name="forward_mix",
    )(*operands)
    saved, (partial, sums, *carry) = outs[:shared], outs[shared:]
    return saved, partial, sums, carry


def project_kernel(*refs, count, unread):
    lows, out_weight, outs = refs[:count], refs[count], refs[count + 1 + unread :]
    for low, out in zip(lows, outs):
        for start in range(0, out.shape[1], 512):
            lanes = slice(start, start + 512)
            out[:, lanes] = dot(low[...], out_weight[:, lanes]).astype(bf16)


def project_rows(lows, out_weight, after):
    width = out_weight.shape[1]
    half = lambda columns: pl.BlockSpec((ROWS // 2, columns), lambda i: (i, 0))
    return pl.pallas_call(
        functools.partial(project_kernel, count=len(lows), unread=len(after)),
        grid=(2,),
        in_specs=[half(low.shape[1]) for low in lows]
        + [whole(out_weight.shape)]
        + [ANY] * len(after),
        out_specs=[half(width)] * len(lows),
        out_shape=[jax.ShapeDtypeStruct((low.shape[0], width), bf16) for low in lows],
        compiler_params=compiler_params(),
        cost_estimate=BRIEF,
        name="project_rows",
    )(*lows, out_weight, *after)


def compiler_params():
    return pltpu.CompilerParams(
        dimension_semantics=("arbitrary",), vmem_limit_bytes=VMEM_BYTES
    )


def gate_kernel(total_inner, sums, mixed, gate_raw, back, chan, *rest, unread):
    grad_low, gate_low, gate_out, gain_sums = rest[unread:]
    inner = chan.shape[1]

    @pl.when(pl.program_id(0) == 0)
    def _():
        gain_sums[...] = jnp.zeros_like(gain_sums)

    def chunk(index, carry):
        at = pl.ds(pl.multiple_of(index * CHUNK, CHUNK), CHUNK)
        inverse = lax.rsqrt(sums[0:1, at] / total_inner + epsilon)
        rms = stand(inverse)
        pull = stand(inverse * inverse * inverse * (sums[1:2, at] / total_inner))
        for j in range(inner // LANES):
            lanes = slice(j * LANES, (j + 1) * LANES)
            gate = gate_raw[at, lanes].astype(f32)
            sigma = sigmoid(gate)
            gate_act = gate * sigma
            mix = mixed[at, lanes]
            gated = mix * gate_act
            unit = gated * rms
            out_back = back[at, lanes].astype(f32)
            gate_gain = chan[6:7, lanes]
            gain_sums[:, lanes] += fold(out_back * unit)
            gated_grad = rms * (out_back * gate_gain) - pull * gated
            gate_low[at, lanes] = (
                gated_grad * mix * (sigma + gate_act * (1.0 - sigma))
            ).astype(bf16)
            gate_out[at, lanes] = (unit * gate_gain).astype(bf16)
            grad_low[at, lanes] = (gated_grad * gate_act).astype(bf16)
        return carry

    lax.fori_loop(0, mixed.shape[0] // CHUNK, chunk, 0)


def gate_grads(total_inner, sums, mixed, gate_raw, back, chan, after):
    length, inner = mixed.shape
    rows_of = lambda columns: pl.BlockSpec((ROWS, columns), lambda i: (i, 0))
    return pl.pallas_call(
        functools.partial(gate_kernel, total_inner, unread=len(after)),
        grid=(length // ROWS,),
        in_specs=[
            pl.BlockSpec((2, ROWS), lambda i: (0, i)),
            rows_of(inner),
            rows_of(inner),
            rows_of(inner),
            whole((8, inner)),
            *[ANY] * len(after),
        ],
        out_specs=[rows_of(inner)] * 3 + [held((8, inner))],
        out_shape=[jax.ShapeDtypeStruct((length, inner), bf16)] * 3
        + [jax.ShapeDtypeStruct((8, inner), f32)],
        compiler_params=compiler_params(),
        cost_estimate=BRIEF,
        name="gate_grads",
    )(sums, mixed, gate_raw, back, chan, *after)


def backward_kernel(
    starts,
    marks,
    gain,
    chan,
    state_chan,
    heads,
    owners,
    *rest,
    block,
    first,
    unread,
    parts,
):
    sources, rest = rest[:14], rest[14:]
    if not first:
        earlier, rest = rest[:6], rest[6:]
    rest = rest[unread:]
    mixer_home, small_home = rest[:2]
    partials, rest = rest[2 : 2 + parts], rest[2 + parts :]
    results, rest = rest[:6], rest[6:]
    state_grad, halo_out, chan_sums, state_sums, head_sums, gain_sums = results
    buffers, rest = rest[:14], rest[14:]
    (
        mixed,
        mixer_grad,
        mixer_in,
        slope,
        small_raw,
        states,
        state_slope,
        kept_states,
        mixer_raw,
        gate_low,
        gate_weight,
        input_weight,
        state_weight,
        tokens,
    ) = buffers
    (
        mixer_low,
        small_low,
        pre_grad,
        state_pre,
        ends_low,
        begins_low,
        normed_grad,
        picks,
        pairs,
        carried_back,
        by_head,
        load_sems,
        store_sems,
    ) = rest
    rows, width = tokens.shape
    inner = gate_weight.shape[1]
    chunks = rows // CHUNK
    half = rows // 2
    here = pl.ds(block * rows, rows)
    sequence = lax.axis_index("dp") * starts.shape[0]

    def part_of(number):
        pairs = [
            (source.at[pl.ds(block * rows + number * half, half), :], buffer.at[pl.ds(number * half, half), :])
            for source, buffer in zip(sources[:7], buffers[:7])
        ]
        count = chunks // 2
        pairs.append(
            (
                sources[7].at[pl.ds(block * chunks + number * count, count)],
                kept_states.at[pl.ds(number * count, count)],
            )
        )
        return pairs

    soon = started(part_of(1), load_sems)
    second = started(part_of(0), load_sems, 8)
    late = started(
        [
            (source if source.shape[0] == buffer.shape[0] else source.at[here, :], buffer)
            for source, buffer in zip(sources[8:], buffers[8:])
        ],
        load_sems,
        16,
    )
    for j in range(inner // LANES):
        column = lax.broadcasted_iota(jnp.int32, (2 * LANES, LANES), 1)
        line = lax.broadcasted_iota(jnp.int32, (2 * LANES, LANES), 0) % LANES
        owner = 2 * j + (line >= LANES // 2).astype(jnp.int32)
        picks[j] = (column == owner).astype(bf16)
        beyond_half = lax.broadcasted_iota(jnp.int32, (2 * LANES, LANES), 0) >= LANES
        pairs[j] = (column == owner + jnp.where(beyond_half, LANES // 2, 0)).astype(bf16)
    if first:
        for result in results:
            result[...] = jnp.zeros_like(result)
        pre_grad[rows : rows + 8, :] = jnp.zeros((8, inner), f32)
        state_pre[rows : rows + 8, :] = jnp.zeros((8, 256), f32)
    else:
        for result, value in zip(results, earlier):
            result[...] = value[...]
        pre_grad[rows : rows + 8, :] = earlier[1][:, :inner]
        state_pre[rows : rows + 8, :] = earlier[1][:, inner:]
    settle(soon)

    def chunk(turn, carry):
        index = chunks - 1 - turn

        @pl.when(turn == chunks // 2)
        def _():
            settle(second)

        first_row = pl.multiple_of(index * CHUNK, CHUNK)
        at = pl.ds(first_row, CHUNK)
        first_token = block * rows + index * CHUNK
        chunk_first = first_token.astype(f32)
        row_place = place(0).astype(f32) + chunk_first
        lane_place = place(1).astype(f32) + chunk_first
        start_row = marks[0:1, pl.ds(pl.multiple_of(block * rows + index * CHUNK, CHUNK), CHUNK)]
        start_column = stand(start_row)
        seen = (row_place <= lane_place) & (row_place >= start_row)
        last_start = (starts[first_token + CHUNK - 1] - sequence).astype(f32)
        carried = (last_start < chunk_first).astype(f32)
        ends = (row_place >= last_start).astype(f32)
        begins = (start_column < chunk_first).astype(f32)
        state_b = states[at, :LANES]
        state_c = states[at, LANES:]
        scores = jnp.where(seen, dot_nt(state_b, state_c), 0.0)
        step_raw = small_raw[at, 256:].astype(f32)
        field, step_size, levels = step_levels(step_raw, heads)
        levels_row = jnp.transpose(levels)
        state_low = state_grad[...].astype(bf16)
        carried_back[...] = dot(state_b, state_low)
        by_head[...] = spread_heads(step_size, levels, begins, ends, owners)
        low = low_lanes()
        score_grad = jnp.zeros((CHUNK, CHUNK), f32)
        level_grad = jnp.zeros((CHUNK + 8, LANES), f32)
        step_grad = jnp.zeros((CHUNK, LANES), f32)
        for j in range(inner // LANES):
            lanes = slice(j * LANES, (j + 1) * LANES)
            pick = picks[j]
            mix = mixed[at, lanes]
            grad = mixer_grad[at, lanes].astype(f32)
            value = mixer_in[at, lanes].astype(f32)
            skip = chan[5:6, lanes]
            chan_sums[0:8, lanes] += fold(grad * value)
            step_pair = by_head[0:CHUNK, lanes]
            beginning = by_head[CHUNK : 2 * CHUNK, lanes]
            ending = by_head[2 * CHUNK : 3 * CHUNK, lanes]
            last = by_head[3 * CHUNK : 3 * CHUNK + 1, lanes]
            stepped = value * step_pair
            stepped_low = stepped.astype(bf16)
            stacked = jnp.concatenate(
                [jnp.where(low, grad, 0.0), jnp.where(low, 0.0, grad)], axis=0
            ).astype(bf16)
            cells = dot_nt(stepped_low, stacked)
            weights = []
            for k in range(2):
                h = 2 * j + k
                level = spread(levels[:, h : h + 1])
                damping = jnp.exp2(jnp.minimum(levels_row[h : h + 1, :] - level, 0.0))
                weights.append((scores * damping).astype(bf16))
                score_grad += cells[:, k * CHUNK : (k + 1) * CHUNK] * damping
            within = dot(jnp.concatenate(weights, axis=1), stacked)
            beyond = ending * carried_back[:, lanes]
            value_grad = within + beyond
            ends_low[:, lanes] = (stepped * ending).astype(bf16)
            begins_low[:, lanes] = (grad * beginning).astype(bf16)
            behind = state_grad[:, lanes]
            crossing = fold(behind * kept_states[index, :, lanes].astype(f32))
            state_grad[:, lanes] = behind * (carried * last)
            rows_flow = grad * (mix - skip * value) - stepped_low.astype(f32) * within
            level_grad += dot(halves(jnp.concatenate([rows_flow, crossing], axis=0)), pick)
            both = jnp.concatenate([value * value_grad, stepped * beyond], axis=1)
            step_grad += dot(both.astype(bf16), pairs[j])
            pre_grad[at, lanes] = (step_pair * value_grad + skip * grad) * slope[
                at, lanes
            ].astype(f32)
        state_grad[...] += dot_tn(state_c, begins_low[...])
        score_low = jnp.where(seen, score_grad, 0.0).astype(bf16)
        state_pre[at, :LANES] = (
            dot(score_low, state_c) + dot_nt(ends_low[...], state_low)
        ) * state_slope[at, :LANES].astype(f32)
        state_pre[at, LANES:] = (
            dot_tn(score_low, state_b) + dot_nt(begins_low[...], kept_states[index])
        ) * state_slope[at, LANES:].astype(f32)
        sums_over = jnp.concatenate(
            [(place(0) <= place(1)).astype(bf16), (place(0) > place(1)).astype(bf16)], axis=1
        )
        inter_grad = pltpu.roll(step_grad, LANES // 2, 1)
        flows = jnp.concatenate([halves(level_grad[:CHUNK]), halves(inter_grad)], axis=0)
        reach = dot(sums_over, flows)
        across = jnp.sum(level_grad[CHUNK:], axis=0, keepdims=True) * (
            carried * jnp.exp2(levels[CHUNK - 1 : CHUNK, :])
        )
        reach = reach[:, :LANES] + reach[:, LANES:] + across
        own = (place(1) < LANES // 2).astype(f32)
        reach = reach * own
        step_grad = step_grad * own
        rates = heads[2:3, :]
        field_grad = (step_grad + reach * rates) * sigmoid(field)
        small_low[at, 256:] = field_grad.astype(bf16)
        head_sums[0:8, :] += fold(field_grad)
        head_sums[8:16, :] += fold(reach * step_size * rates)
        return carry

    lax.fori_loop(0, chunks, chunk, 0)
    settle(late)

    def unconv(index, carry):
        first_row = pl.multiple_of(index * CHUNK, CHUNK)
        at = pl.ds(first_row, CHUNK)
        left = stand(marks[1:2, pl.ds(pl.multiple_of(block * rows + index * CHUNK, CHUNK), CHUNK)])
        kept = [(left >= k).astype(f32) for k in range(1, 4)]

        def tile(window, value, taps, lanes, totals, line):
            own = window[:CHUNK]
            total = taps[0:1, lanes] * own
            totals[line : line + 8, lanes] += fold(value * own)
            for k in range(1, 4):
                moved = kept[k - 1] * window[k : k + CHUNK]
                total += taps[k : k + 1, lanes] * moved
                totals[line + 8 * k : line + 8 * k + 8, lanes] += fold(value * moved)
            totals[line + 32 : line + 40, lanes] += fold(own)
            return total.astype(bf16)

        for j in range(inner // LANES):
            lanes = slice(j * LANES, (j + 1) * LANES)
            mixer_low[at, lanes] = tile(
                pre_grad[pl.ds(first_row, CHUNK + 8), lanes],
                mixer_raw[at, lanes].astype(f32),
                chan,
                lanes,
                chan_sums,
                8,
            )
        for j in range(2):
            lanes = slice(j * LANES, (j + 1) * LANES)
            small_low[at, lanes] = tile(
                state_pre[pl.ds(first_row, CHUNK + 8), lanes],
                small_raw[at, lanes].astype(f32),
                state_chan,
                lanes,
                state_sums,
                0,
            )
        return carry

    lax.fori_loop(0, chunks, unconv, 0)
    stores = started(
        [(mixer_low, mixer_home.at[here, :]), (small_low, small_home.at[here, :])], store_sems
    )
    for start in range(0, width, 256):
        lanes = slice(start, start + 256)
        normed_grad[:, lanes] = (
            dot_nt(gate_low[...], gate_weight[lanes, :])
            + dot_nt(mixer_low[...], input_weight[lanes, :])
            + dot_nt(small_low[...], state_weight[lanes, :])
        )

    def unnorm(part, index, carry):
        at = pl.ds(pl.multiple_of(index * 16, 16), 16)
        from_row = pl.ds(pl.multiple_of(part * part_rows + index * 16, 16), 16)
        values = tokens[from_row, :].astype(f32)
        inverse = lax.rsqrt(jnp.mean(values * values, axis=-1, keepdims=True) + epsilon)
        unit = values * inverse
        grad = normed_grad[from_row, :]
        gain_sums[...] += fold(grad * unit)
        grad = grad * gain[...]
        out = partials[part]
        out[at, :] = (
            inverse * (grad - unit * jnp.mean(grad * unit, axis=-1, keepdims=True))
        ).astype(bf16)
        return carry

    part_rows = partials[0].shape[0]
    for part in range(len(partials)):
        lax.fori_loop(0, part_rows // 16, functools.partial(unnorm, part), 0, unroll=2)
    halo_out[:, :inner] = pre_grad[0:8, :]
    halo_out[:, inner:] = state_pre[0:8, :]
    settle(stores)


def backward(block, starts, marks, tokens, params, saved, grads, carry, earlier, after, parts):
    gain, gate_weight, input_weight, small_weight, *tables, _ = params
    tables = [gain, *tables]
    length, width = tokens.shape
    inner = gate_weight.shape[1]
    chunks = ROWS // CHUNK
    (gate_raw, mixer_raw, small_raw, mixer_in, slope, states, state_slope, mixed, _, kept) = saved
    mixer_grad, gate_low = grads
    sources = [
        mixed,
        mixer_grad,
        mixer_in,
        slope,
        small_raw,
        states,
        state_slope,
        kept,
        mixer_raw,
        gate_low,
        gate_weight,
        input_weight,
        small_weight,
        tokens,
    ]
    operands = [starts, marks, *tables, *sources, *carry]
    in_specs = [SMEM, *wholes([marks, *tables]), *[HBM] * len(sources), *wholes(carry)]
    aliases = {}
    if earlier is not None:
        aliases = {len(operands) + k: k for k in range(2)}
        in_specs += [HBM] * 2
        operands += list(earlier)
    operands += list(after)
    in_specs += [ANY] * len(after)
    results = [
        (LANES, inner),
        (8, inner + 256),
        (48, inner),
        (40, 256),
        (16, LANES),
        (8, width),
    ]
    outs = pl.pallas_call(
        functools.partial(
            backward_kernel,
            block=block,
            first=not carry,
            unread=len(aliases) + len(after),
            parts=parts,
        ),
        grid=(1,),
        in_specs=in_specs,
        out_specs=[HBM] * 2
        + [whole((ROWS // parts, width))] * parts
        + [whole(shape) for shape in results],
        out_shape=[
            jax.ShapeDtypeStruct((length, inner), bf16),
            jax.ShapeDtypeStruct((length, 384), bf16),
            *[jax.ShapeDtypeStruct((ROWS // parts, width), bf16)] * parts,
            *[jax.ShapeDtypeStruct(shape, f32) for shape in results],
        ],
        scratch_shapes=[
            *[
                pltpu.VMEM((chunks, LANES, inner), bf16)
                if source.ndim == 3
                else pltpu.VMEM(
                    (ROWS if source.shape[0] == length else source.shape[0], source.shape[1]),
                    source.dtype,
                )
                for source in sources
            ],
            pltpu.VMEM((ROWS, inner), bf16),
            pltpu.VMEM((ROWS, 384), bf16),
            pltpu.VMEM((ROWS + 8, inner), f32),
            pltpu.VMEM((ROWS + 8, 256), f32),
            pltpu.VMEM((CHUNK, inner), bf16),
            pltpu.VMEM((CHUNK, inner), bf16),
            pltpu.VMEM((ROWS, width), f32),
            *[pltpu.VMEM((inner // LANES, 2 * LANES, LANES), bf16)] * 2,
            pltpu.VMEM((CHUNK, inner), f32),
            pltpu.VMEM((3 * CHUNK + 8, inner), f32),
            pltpu.SemaphoreType.DMA((22,)),
            pltpu.SemaphoreType.DMA((2,)),
        ],
        input_output_aliases=aliases,
        compiler_params=pltpu.CompilerParams(vmem_limit_bytes=VMEM_BYTES),
        cost_estimate=LONG,
        name="backward_mix",
    )(*operands)
    return outs[:2], outs[2 : 2 + parts], outs[2 + parts :]


def pack(packed, chan_sums, gate_sums, head_sums, state_sums, gain_sums, small_total):
    inner = chan_sums.shape[1]
    packed[...] = jnp.zeros_like(packed)
    total = lambda values: jnp.sum(values, axis=0, keepdims=True)
    for k in range(6):
        packed[k : k + 1, :inner] = total(chan_sums[8 * k : 8 * k + 8, :])
    packed[6:7, :inner] = total(gate_sums[...])
    for k in range(2):
        packed[7:8, k * LANES : (k + 1) * LANES] = total(head_sums[8 * k : 8 * k + 8, :])
    for k in range(5):
        packed[8 + k : 9 + k, :256] = total(state_sums[8 * k : 8 * k + 8, :])
    packed[13:14, :] = total(gain_sums[...])
    for start in range(0, packed.shape[1], LANES):
        lanes = slice(start, start + LANES)
        packed[16:32, lanes] = jnp.transpose(small_total[lanes, 256:])[0:16]


def weight_kernel(left, *rest, rights, unread, packs):
    right, rest = rest[:rights], rest[rights:]
    sums, rest = rest[:packs], rest[packs + unread :]
    outs, totals = rest[: rights + bool(packs)], rest[rights + bool(packs) :]
    step = pl.program_id(0)

    @pl.when(step == 0)
    def _():
        for total in totals:
            total[...] = jnp.zeros_like(total)

    for start in range(0, left.shape[1], 256):
        columns = slice(start, start + 256)
        for item, total in zip(right, totals):
            total[columns, :] += dot_tn(left[:, columns], item[...])

    @pl.when(step == pl.num_programs(0) - 1)
    def _():
        if packs:
            packed = totals[rights]
            pack(packed, *sums, totals[rights - 1])
            outs[rights][...] = packed[...].astype(bf16)
        for out, total in zip(outs[:rights], totals):
            out[...] = total[:, : out.shape[1]].astype(bf16)


def weight_grads(left, rights, after, sums=()):
    length, height = left.shape
    rows_of = lambda columns: pl.BlockSpec((ROWS, columns), lambda i: (i, 0))
    shapes = [(height, item.shape[1]) for item in rights]
    outs, scratch = list(shapes), list(shapes)
    if sums:
        outs[-1] = (height, 256)
        outs.append((32, height))
        scratch.append((32, height))
    return pl.pallas_call(
        functools.partial(
            weight_kernel, rights=len(rights), unread=len(after), packs=len(sums)
        ),
        grid=(length // ROWS,),
        in_specs=[rows_of(height)]
        + [rows_of(item.shape[1]) for item in rights]
        + wholes(sums)
        + [ANY] * len(after),
        out_specs=[held(shape) for shape in outs],
        out_shape=[jax.ShapeDtypeStruct(shape, bf16) for shape in outs],
        scratch_shapes=[pltpu.VMEM(shape, f32) for shape in scratch],
        compiler_params=compiler_params(),
        cost_estimate=BRIEF,
        name="weight_grads",
    )(left, *rights, *sums, *after)


def land_kernel(take, total_home, moved_home, *rest, mode, unread):
    out_home, total, moved, out, load_sems, store_sems = rest[unread:]
    tiles = total.shape[0] // CHUNK
    part = [pl.ds(k * CHUNK, CHUNK) for k in range(tiles)]
    loads = [
        started(
            [
                (total_home.at[part[k], :], total.at[part[k], :]),
                (moved_home.at[part[k], :], moved.at[part[k], :]),
            ],
            load_sems,
            2 * k,
        )
        for k in range(tiles)
    ]
    stores = []
    for k in range(tiles):
        settle(loads[k])
        at = slice(k * CHUNK, (k + 1) * CHUNK)
        if mode == "add":
            out[at, :] = total[at, :] + moved[at, :]
        else:
            out[at, :] = jnp.where(take[0] > 0, moved[at, :], total[at, :])
        stores += started([(out.at[part[k], :], out_home.at[part[k], :])], store_sems, k)
    settle(stores)


def finish_kernel(
    take, total_home, moved_home, base_home, sums, *rest, adds, inner, row, unread
):
    out_home, total, moved, base, out, load_sems, store_sems = rest[unread:]
    rows = total.shape[0]
    tiles = rows // CHUNK
    at_home = lambda k: pl.ds(row + k * CHUNK, CHUNK)
    at_here = lambda k: pl.ds(k * CHUNK, CHUNK)

    def run(pairs):
        loads = [
            started(
                [(home.at[at_here(k), :], here.at[at_here(k), :]) for home, here in pairs]
                + [(base_home.at[at_home(k), :], base.at[at_here(k), :])],
                load_sems,
                3 * k,
            )
            for k in range(tiles)
        ]
        stores = []
        for k in range(tiles):
            at = slice(k * CHUNK, (k + 1) * CHUNK)
            if inner:
                scale = stand(
                    lax.rsqrt(
                        sums[0:1, row + k * CHUNK : row + (k + 1) * CHUNK] / inner + epsilon
                    )
                )
            settle(loads[k])
            for start in range(0, total.shape[1], LANES):
                lanes = slice(start, start + LANES)
                value = pairs[0][1][at, lanes].astype(f32)
                for _, here in pairs[1:]:
                    value += here[at, lanes].astype(f32)
                if inner:
                    value = value * scale
                out[at, lanes] = (value + base[at, lanes].astype(f32)).astype(bf16)
            stores += started(
                [(out.at[at_here(k), :], out_home.at[at_home(k), :])], store_sems, k
            )
        settle(stores)

    if adds:
        run([(moved_home, moved), (total_home, total)])
        return

    @pl.when(take[0] > 0)
    def _():
        run([(moved_home, moved)])

    @pl.when(take[0] <= 0)
    def _():
        run([(total_home, total)])


def land(take, total, moved, mode, after):
    rows, width = total.shape
    return pl.pallas_call(
        functools.partial(land_kernel, mode=mode, unread=len(after)),
        in_specs=[SMEM, HBM, HBM] + [ANY] * len(after),
        out_specs=HBM,
        out_shape=jax.ShapeDtypeStruct((rows, width), bf16),
        scratch_shapes=[
            *[pltpu.VMEM((rows, width), bf16)] * 3,
            pltpu.SemaphoreType.DMA((2 * rows // CHUNK,)),
            pltpu.SemaphoreType.DMA((rows // CHUNK,)),
        ],
        compiler_params=pltpu.CompilerParams(vmem_limit_bytes=VMEM_BYTES),
        cost_estimate=BRIEF,
        name="line_land",
    )(take, total, moved, *after)


def turn_kernel(take, total_home, moved_home, next_home, *rest, unread):
    out_home, total, moved, out, load_sems, store_sems = rest[unread:]
    land_refs = (out_home, total, moved, out, load_sems, store_sems)

    @pl.when(take[0] > 0)
    def _():
        tiles = out.shape[0] // CHUNK
        part = [pl.ds(k * CHUNK, CHUNK) for k in range(tiles)]
        loads = started([(next_home.at[at, :], out.at[at, :]) for at in part], load_sems)
        stores = []
        for k, at in enumerate(part):
            settle(loads[k : k + 1])
            stores += started([(out.at[at, :], out_home.at[at, :])], store_sems, k)
        settle(stores)

    @pl.when(take[0] <= 0)
    def _():
        land_kernel(take, total_home, moved_home, *land_refs, mode="add", unread=0)


def turn(take, total, moved, following, after):
    rows, width = total.shape
    return pl.pallas_call(
        functools.partial(turn_kernel, unread=len(after)),
        in_specs=[SMEM, HBM, HBM, HBM] + [ANY] * len(after),
        out_specs=HBM,
        out_shape=jax.ShapeDtypeStruct((rows, width), bf16),
        scratch_shapes=[
            *[pltpu.VMEM((rows, width), bf16)] * 3,
            pltpu.SemaphoreType.DMA((2 * rows // CHUNK,)),
            pltpu.SemaphoreType.DMA((rows // CHUNK,)),
        ],
        compiler_params=pltpu.CompilerParams(vmem_limit_bytes=VMEM_BYTES),
        cost_estimate=BRIEF,
        name="line_turn",
    )(take, total, moved, following, *after)


def finish(take, total, moved, adds, base, sums, inner, row, earlier, after):
    rows, width = total.shape
    operands = [take, total, moved, base, sums]
    in_specs = [SMEM, HBM, HBM, HBM, whole(sums.shape)]
    aliases = {}
    if earlier is not None:
        aliases = {len(operands): 0}
        operands += [earlier]
        in_specs += [HBM]
    after = [item for item in after if item is not earlier]
    operands += after
    in_specs += [ANY] * len(after)
    return pl.pallas_call(
        functools.partial(
            finish_kernel,
            adds=adds,
            inner=inner,
            row=row,
            unread=len(aliases) + len(after),
        ),
        in_specs=in_specs,
        out_specs=HBM,
        grid=(1,),
        out_shape=jax.ShapeDtypeStruct(base.shape, bf16),
        scratch_shapes=[
            *[pltpu.VMEM((rows, width), bf16)] * 4,
            pltpu.SemaphoreType.DMA((3 * rows // CHUNK,)),
            pltpu.SemaphoreType.DMA((rows // CHUNK,)),
        ],
        input_output_aliases=aliases,
        compiler_params=pltpu.CompilerParams(vmem_limit_bytes=VMEM_BYTES),
        cost_estimate=BRIEF,
        name="line_finish",
    )(*operands)


class Line:
    def __init__(self, members, me):
        middle = members // 2
        self.steps = [
            ("add", [(near, near + 1), (members - 1 - near, members - 2 - near)], near)
            for near in range(middle - 1)
        ]
        self.steps.append(("add", [(middle - 1, middle), (middle, middle - 1)], 0))
        self.steps += [
            ("take", [(near + 1, near), (members - 2 - near, members - 1 - near)], near)
            for near in reversed(range(middle - 1))
        ]
        self.takes = [
            ((me == near) | (me == members - 1 - near)).astype(jnp.int32)[None]
            for _, _, near in self.steps
        ]
        self.flying = [[] for _ in self.steps]
        self.outs = {}

    def push(self, total, name, row):
        self.launch(0, total, name, row)

    def launch(self, step, total, name, row):
        moved = lax.ppermute(total, "tensor", self.steps[step][1])
        self.flying[step].append((total, moved, name, row))

    def tick(self, ending, after, first=1, then=1, last=1):
        ready = []
        for step, queue in enumerate(self.flying):
            count = last if step == len(self.flying) - 1 else then if step else first
            for _ in range(min(len(queue), count)):
                ready.append((step, queue.pop(0)))
        for step, (total, moved, name, row) in ready:
            mode = self.steps[step][0]
            if step < len(self.steps) - 1:
                total = land(self.takes[step], total, moved, mode, after)
                self.launch(step + 1, total, name, row)
                after = [total]
            else:
                base, sums, inner = ending[name]
                out = finish(
                    self.takes[step],
                    total,
                    moved,
                    mode == "add",
                    base,
                    sums,
                    inner,
                    row,
                    self.outs.get(name),
                    after,
                )
                self.outs[name] = out
                after = [out]
        return after

    def busy(self):
        return any(self.flying)

    def inward(self, after):
        return self.tick({}, after, then=0, last=0)

    def outward(self, ending, after):
        return self.tick(ending, after, first=0)

    def round(self, ending, after):
        return self.tick(ending, after)


class CrossLine:
    def __init__(self, me):
        self.take = ((me == 0) | (me == 3)).astype(jnp.int32)[None]
        self.crossing, self.meeting, self.ready, self.waiting = [], [], [], []
        self.arrived = None
        self.outs = {}

    def push(self, total, name, row):
        self.waiting.append((total, name, row))

    def launch(self, total, inbound, outbound):
        moved = lax.ppermute(total, "tensor", [(0, 1), (1, 0), (2, 3), (3, 2)])
        self.crossing.append((moved, inbound, outbound))

    def send(self):
        item = self.waiting.pop(0)
        self.launch(item[0], item, None)

    def inward(self, after):
        self.ready, self.meeting = self.meeting, []
        self.arrived = self.crossing.pop(0) if self.crossing else None
        if self.arrived and self.arrived[1]:
            moved, (total, name, row), _ = self.arrived
            total = land(self.take, total, moved, "add", after)
            met = lax.ppermute(total, "tensor", [(1, 2), (2, 1)])
            self.meeting.append((total, met, name, row))
            after = [total]
        return after

    def outward(self, ending, after):
        if self.ready:
            ((total, met, name, row),) = self.ready
            following = self.waiting.pop(0) if self.waiting else None
            if following:
                total = turn(self.take, total, met, following[0], after)
            else:
                total = land(self.take, total, met, "add", after)
            self.launch(total, following, (total, name, row))
            self.ready = []
            after = [total]
        elif self.waiting:
            self.send()
        if self.arrived and self.arrived[2]:
            moved, _, (total, name, row) = self.arrived
            base, sums, inner = ending[name]
            earlier = self.outs.get(name)
            out = finish(
                self.take, total, moved, False, base, sums, inner, row, earlier, after
            )
            self.outs[name] = out
            after = [out]
        return after

    def round(self, ending, after):
        return self.outward(ending, self.inward(after))

    def busy(self):
        return bool(self.crossing or self.meeting or self.waiting)


def sum_over(values, axis, size):
    parts = [values]
    for k in range(1, size):
        parts.append(lax.ppermute(values, axis, [(i, i ^ k) for i in range(size)]))
    while len(parts) > 1:
        parts = [parts[k] + parts[k + 1] for k in range(0, len(parts), 2)]
    return parts[0]


def part_kernel(me, lines, values, *rest, size, unread):
    outs = rest[unread:]
    rows = values.shape[0] // size
    for k in range(size):
        first = pl.multiple_of((me[0] ^ k) * rows, 32)
        outs[k][:rows, :] = values[pl.ds(first, rows), :]
        for j in range(lines.shape[1] // 256):
            at = slice(rows + 16 * j, rows + 16 * j + 16)
            outs[k][at, :] = lines[0:16, 256 * j : 256 * j + 256]


def join_kernel(*refs):
    parts, (line_sums, value_sums) = list(refs[:-2]), refs[-2:]
    rows = value_sums.shape[0]
    for out, at in [(value_sums, slice(0, rows)), (line_sums, slice(rows, None))]:
        totals = [part[at, :].astype(f32) for part in parts]
        while len(totals) > 1:
            totals = [totals[k] + totals[k + 1] for k in range(0, len(totals), 2)]
        out[...] = totals[0]


def sum_pieces(lines, values, axis, size, me, after):
    rows = values.shape[0] // size
    height = rows + 16 * (lines.shape[1] // 256)
    shape = jax.ShapeDtypeStruct((height, 256), bf16)
    own, *sent = pl.pallas_call(
        functools.partial(part_kernel, size=size, unread=len(after)),
        grid=(1,),
        in_specs=[SMEM, *wholes([lines, values]), *[ANY] * len(after)],
        out_specs=[whole(shape.shape)] * size,
        out_shape=[shape] * size,
        compiler_params=compiler_params(),
        cost_estimate=BRIEF,
        name="part_pieces",
    )(me[None], lines, values, *after)
    parts = [own] + [
        lax.ppermute(sent[k - 1], axis, [(i, i ^ k) for i in range(size)])
        for k in range(1, size)
    ]
    outs = [(height - rows, 256), (rows, 256)]
    line_sums, value_sums = pl.pallas_call(
        join_kernel,
        grid=(1,),
        in_specs=wholes(parts),
        out_specs=[whole(item) for item in outs],
        out_shape=[jax.ShapeDtypeStruct(item, f32) for item in outs],
        compiler_params=compiler_params(),
        cost_estimate=BRIEF,
        name="join_pieces",
    )(*parts)
    return line_sums.reshape(-1, 16, 256), value_sums


def on_device(
    block_input,
    segment_ids,
    norm_gain,
    gate_weight,
    input_weight,
    state_weight,
    step_weight,
    mixer_conv,
    mixer_shift,
    state_conv,
    state_shift,
    step_bias,
    decay_log,
    skip_gain,
    gate_gain,
    out_weight,
    out_grad,
):
    length, width = block_input.shape
    inner = gate_weight.shape[1]
    heads_local = step_weight.shape[1]
    groups = lax.axis_size("tensor")
    member = lax.axis_index("tensor")
    columns = width // groups
    total_inner = inner * groups

    gain, marks, chan, state_chan, heads, small_weight, owners = prepare(
        length,
        width,
        inner,
        (
            segment_ids,
            norm_gain,
            mixer_conv,
            mixer_shift,
            state_conv,
            state_shift,
            step_bias,
            decay_log,
            skip_gain,
            gate_gain,
            state_weight,
            step_weight,
        ),
    )
    params = (
        gain,
        gate_weight,
        input_weight,
        small_weight,
        chan,
        state_chan,
        heads,
        owners,
        out_weight,
    )
    blocks = length // ROWS
    line = CrossLine(member) if groups == 4 else Line(groups, member)
    saved, carry, after = None, [], []
    block_sums, waiting = [], []
    for block in range(blocks):
        early = block < blocks // 2
        saved, partial, sums, carry = forward(
            block,
            segment_ids,
            marks,
            block_input,
            out_grad,
            params,
            carry,
            saved,
            after,
            early,
        )
        block_sums.append(sums)
        after = [partial]
        if early:
            line.push(partial, "output", block * ROWS)
            if groups == 4:
                line.send()
        else:
            waiting.append(partial)
        if block == blocks // 2:
            after = line.inward(after)
    sums = jnp.concatenate(block_sums, axis=1)
    after = line.inward([sums])
    sums = sum_over(sums, "tensor", groups)
    ending = {
        "output": (block_input, sums, total_inner),
        "input": (out_grad, sums, 0),
    }
    partials = project_rows(waiting, out_weight, [*after, sums])
    for k, partial in enumerate(partials):
        line.push(partial, "output", (blocks // 2 + k) * ROWS)
    after = line.outward(ending, [partials[0]])
    normed, *saved = saved
    grad_low, gate_low, gate_out, gate_sums = gate_grads(
        total_inner, sums, saved[7], saved[0], saved[8], chan, after
    )
    (gate_weight_grad,) = weight_grads(normed, [gate_low], [grad_low])
    (out_weight_grad,) = weight_grads(gate_out, [out_grad], [gate_weight_grad])
    after = [out_weight_grad]
    gate_weight_grad, out_weight_grad = lax.psum((gate_weight_grad, out_weight_grad), "dp")
    after = line.round(ending, after)
    lows, carry = None, []
    for block in reversed(range(blocks)):
        lows, partials, carry = backward(
            block,
            segment_ids,
            marks,
            block_input,
            params,
            saved,
            (grad_low, gate_low),
            carry,
            lows,
            after + [gate_weight_grad, out_weight_grad] if block == 0 else after,
            1,
        )
        after = [partials[0]]
        for k, partial in enumerate(partials):
            line.push(partial, "input", block * ROWS + k * partial.shape[0])
        after = line.round(ending, after)
    mixer_low, small_low = lows
    chan_sums, state_sums, head_sums, gain_sums = carry[2:]
    weight_sums = weight_grads(
        normed,
        [mixer_low, small_low],
        after,
        (chan_sums, gate_sums, head_sums, state_sums, gain_sums),
    )
    after = [weight_sums[0]]
    input_weight_grad, state_weight_grad, packed = lax.psum(tuple(weight_sums), "dp")
    for _ in range(2):
        after = line.round(ending, after)
    line_sums, state_weight_grad = sum_pieces(
        packed, state_weight_grad, "tensor", groups, member, after
    )
    while line.busy():
        after = line.round(ending, after)
    block_output = line.outs["output"]
    input_grad = line.outs["input"]
    packed = packed.astype(f32)
    return (
        block_output,
        input_grad,
        lax.dynamic_slice_in_dim(line_sums[:, 13].reshape(-1), member * columns, columns, 0),
        gate_weight_grad.astype(f32),
        input_weight_grad.astype(f32),
        state_weight_grad,
        packed[16 : 16 + heads_local].T,
        packed[1:5, :inner],
        packed[5, :inner],
        line_sums[0, 8:12],
        line_sums[0, 12],
        packed[7, :heads_local],
        packed[7, LANES : LANES + heads_local],
        packed[0, :inner].reshape(heads_local, inner // heads_local).sum(axis=1),
        packed[6, :inner],
        out_weight_grad.astype(f32),
    )


def solution(mesh):
    return jax.shard_map(
        on_device,
        mesh=mesh,
        in_specs=(
            P("dp", None),
            P("dp"),
            P(),
            P(None, "tensor"),
            P(None, "tensor"),
            P(),
            P(None, "tensor"),
            P(None, "tensor"),
            P("tensor"),
            P(),
            P(),
            P("tensor"),
            P("tensor"),
            P("tensor"),
            P("tensor"),
            P("tensor", None),
            P("dp", None),
        ),
        out_specs=(
            P("dp", None),
            P("dp", None),
            P("tensor"),
            P(None, "tensor"),
            P(None, "tensor"),
            P("tensor", None),
            P(None, "tensor"),
            P(None, "tensor"),
            P("tensor"),
            P(),
            P(),
            P("tensor"),
            P("tensor"),
            P("tensor"),
            P("tensor"),
            P("tensor", None),
        ),
        check_vma=False,
    )
```

```python
import functools

import jax
import jax.numpy as jnp
from jax import lax
from jax.experimental import pallas as pl
from jax.experimental.pallas import tpu as pltpu
from jax.sharding import PartitionSpec as P

epsilon = 1e-05
highest = lax.Precision.HIGHEST
f32 = jnp.float32
bf16 = jnp.bfloat16
LOG2E = 1.4426950408889634
CHUNK = 128
LANES = 128
ROWS = 512
VMEM_BYTES = 61 * 1024 * 1024
LONG = pl.CostEstimate(flops=10**11, bytes_accessed=3 * 10**8, transcendentals=0)
BRIEF = pl.CostEstimate(flops=1000, bytes_accessed=1000, transcendentals=0)


def dot(left, right, precision=None):
    return lax.dot_general(
        left, right, (((1,), (0,)), ((), ())), precision=precision, preferred_element_type=f32
    )


def dot_nt(left, right):
    return lax.dot_general(left, right, (((1,), (1,)), ((), ())), preferred_element_type=f32)


def dot_tn(left, right):
    return lax.dot_general(left, right, (((0,), (0,)), ((), ())), preferred_element_type=f32)


def sigmoid(values):
    return 0.5 * jnp.tanh(0.5 * values) + 0.5


def softplus(values):
    power = jnp.exp(-jnp.abs(values))
    above = 1.0 + power
    exact = above == 1.0
    tail = jnp.log(above) * (power / jnp.where(exact, 1.0, above - 1.0))
    return jnp.maximum(values, 0.0) + jnp.where(exact, power, tail)


def spread(column):
    return jnp.broadcast_to(column, (column.shape[0], LANES))


def stand(row):
    return jnp.transpose(jnp.broadcast_to(row, (CHUNK, CHUNK)))


def fold(values):
    return jnp.sum(values.reshape(values.shape[0] // 8, 8, values.shape[1]), axis=0)


def halves(values):
    upper = values.astype(bf16)
    lower = (values - upper.astype(f32)).astype(bf16)
    return jnp.concatenate([upper, lower], axis=1)


def place(axis):
    return lax.broadcasted_iota(jnp.int32, (CHUNK, CHUNK), axis)


def low_lanes():
    return place(1) < LANES // 2


def column_step(width):
    return 256 if width % 256 == 0 else 128


def conv_pre(window, taps, lanes, kept):
    total = taps[4:5, lanes] + taps[0:1, lanes] * window[8:]
    for offset in range(1, 4):
        moved = window[8 - offset : 8 - offset + CHUNK]
        total = total + taps[offset : offset + 1, lanes] * (kept[offset - 1] * moved)
    return total


def step_levels(step_raw, heads):
    field = step_raw + heads[0:1, :]
    step = softplus(field)
    tri = (place(0) >= place(1)).astype(bf16)
    levels = dot(tri, halves(step * heads[1:2, :]))
    levels = levels[:, :LANES] + levels[:, LANES:]
    return field, step, levels


HBM = pl.BlockSpec(memory_space=pl.ANY)
SMEM = pl.BlockSpec(memory_space=pltpu.SMEM)
ANY = pl.BlockSpec(memory_space=pl.ANY)


def spread_heads(step_size, levels, begins, ends, owners):
    end_level = levels[CHUNK - 1 : CHUNK, :]
    last = jnp.broadcast_to(jnp.exp2(end_level), (8, LANES))
    compact = jnp.concatenate(
        [
            halves(step_size),
            halves(begins * jnp.exp2(levels)),
            halves(ends * jnp.exp2(end_level - levels)),
            halves(last),
        ],
        axis=0,
    )
    return dot(compact, owners[...])


def whole(shape):
    return pl.BlockSpec(shape, lambda i: (0,) * len(shape), pipeline_mode=pl.Buffered(1))


def held(shape):
    return pl.BlockSpec(shape, lambda i: (0,) * len(shape))


def wholes(items):
    return [whole(item.shape) for item in items]


def started(pairs, semaphores, first=0):
    copies = []
    for k, (source, target) in enumerate(pairs):
        copy = pltpu.make_async_copy(source, target, semaphores.at[first + k])
        copy.start()
        copies.append(copy)
    return copies


def settle(copies):
    for copy in copies:
        copy.wait()


def line_of(values):
    return values[...].reshape(1, values.shape[0])


def prepare_kernel(
    segments,
    norm_gain,
    mixer_conv,
    mixer_shift,
    state_conv,
    state_shift,
    step_bias,
    decay_log,
    skip_gain,
    gate_gain,
    state_weight,
    step_weight,
    gain,
    marks,
    chan,
    state_chan,
    heads,
    small_weight,
    owners,
):
    length = segments.shape[0]
    inner = gate_gain.shape[0]
    count = step_bias.shape[0]
    gain[...] = line_of(norm_gain)
    place_line = lax.broadcasted_iota(jnp.int32, (8, length), 1)
    first = lax.axis_index("dp") * length
    start = jnp.broadcast_to(line_of(segments), (8, length)) - first
    left = jnp.zeros((8, length), f32)
    for k in range(1, 4):
        later = pltpu.roll(start, length - k, 1)
        same = (later <= place_line) & (place_line < length - k)
        left += same.astype(f32)
    marks[0:1, :] = start[0:1].astype(f32)
    marks[1:2, :] = left[0:1]
    heads[...] = jnp.zeros_like(heads)
    rates = -jnp.exp(line_of(decay_log))
    heads[0:1, :count] = line_of(step_bias)
    heads[1:2, :count] = rates * LOG2E
    heads[2:3, :count] = rates
    heads[3:4, :count] = line_of(skip_gain)
    chan[...] = jnp.zeros_like(chan)
    chan[0:4, :] = mixer_conv[...]
    chan[4:5, :] = line_of(mixer_shift)
    owner = lax.broadcasted_iota(jnp.int32, (LANES, inner), 0)
    channel = lax.broadcasted_iota(jnp.int32, (LANES, inner), 1)
    owns = (channel // (inner // count) == owner).astype(f32)
    chan[5:6, :] = dot(heads[...], owns, highest)[3:4]
    owners[:LANES, :] = owns.astype(bf16)
    owners[LANES:, :] = owns.astype(bf16)
    chan[6:7, :] = line_of(gate_gain)
    state_chan[...] = jnp.zeros_like(state_chan)
    state_chan[0:4, :] = state_conv[...]
    state_chan[4:5, :] = line_of(state_shift)
    small_weight[:, :256] = state_weight[...]
    small_weight[:, 256:] = jnp.zeros((small_weight.shape[0], LANES), bf16)
    small_weight[:, 256 : 256 + count] = step_weight[...]


def prepare(length, width, inner, values):
    shapes = [
        ((1, width), f32),
        ((2, length), f32),
        ((8, inner), f32),
        ((8, 256), f32),
        ((8, LANES), f32),
        ((width, 384), bf16),
        ((2 * LANES, inner), bf16),
    ]
    return pl.pallas_call(
        prepare_kernel,
        grid=(1,),
        in_specs=wholes(values),
        out_specs=[whole(shape) for shape, _ in shapes],
        out_shape=[jax.ShapeDtypeStruct(shape, kind) for shape, kind in shapes],
        compiler_params=pltpu.CompilerParams(vmem_limit_bytes=VMEM_BYTES),
        cost_estimate=BRIEF,
        name="prepare",
    )(*values)


def forward_kernel(
    starts,
    marks,
    tokens_home,
    grads_home,
    input_home,
    gate_home,
    small_home,
    out_home,
    gain,
    chan,
    state_chan,
    heads,
    owners,
    *rest,
    block,
    first,
    unread,
    project,
):
    if not first:
        state_in, halo_in = rest[:2]
        rest = rest[2:]
    rest = rest[unread:]
    homes, rest = rest[:11], rest[11:]
    (
        partial,
        sums,
        state,
        halo_out,
        tokens,
        grads,
        normed,
        gate_raw,
        mixer_raw,
        small_raw,
        mixer_in,
        slope,
        states,
        state_slope,
        mixed,
        back,
        kept_states,
        raw,
        state_raw,
        gated_low,
        wide_back,
        input_weight,
        gate_weight,
        state_weight,
        out_weight,
        damped,
        carried_out,
        by_head,
        load_sems,
        store_sems,
    ) = rest
    rows, width = tokens.shape
    inner = gate_weight.shape[1]
    wide = column_step(inner)
    here = pl.ds(block * rows, rows)
    sequence = lax.axis_index("dp") * starts.shape[0]
    loads = started(
        [
            (tokens_home.at[here, :], tokens),
            (small_home, state_weight),
            (input_home, input_weight),
            (gate_home, gate_weight),
            (grads_home.at[here, :], grads),
            (out_home, out_weight),
        ],
        load_sems,
    )
    if first:
        state[...] = jnp.zeros_like(state)
        raw[0:8, :] = jnp.zeros((8, inner), f32)
        state_raw[0:8, :] = jnp.zeros((8, 256), f32)
    else:
        state[...] = state_in[...]
        raw[0:8, :] = halo_in[:, :inner]
        state_raw[0:8, :] = halo_in[:, inner:]

    def norm_rows(index, carry):
        at = pl.ds(pl.multiple_of(index * 16, 16), 16)
        values = tokens[at, :].astype(f32)
        inverse = lax.rsqrt(jnp.mean(values * values, axis=-1, keepdims=True) + epsilon)
        normed[at, :] = (values * inverse * gain[...]).astype(bf16)
        return carry

    settle(loads[:1])
    lax.fori_loop(0, rows // 16, norm_rows, 0, unroll=4)
    stores = started([(normed, homes[0].at[here, :])], store_sems, 0)
    settle(loads[1:2])
    small = dot(normed[...], state_weight[...]).astype(bf16)
    small_raw[...] = small
    state_raw[8 : 8 + rows, :] = small[:, :256].astype(f32)
    settle(loads[2:4])
    for start in range(0, inner, wide):
        lanes = slice(start, start + wide)
        low = dot(normed[...], input_weight[:, lanes]).astype(bf16)
        mixer_raw[:, lanes] = low
        raw[8 : 8 + rows, lanes] = low.astype(f32)
        gate_raw[:, lanes] = dot(normed[...], gate_weight[:, lanes]).astype(bf16)
    settle(loads[4:])
    for start in range(0, inner, wide):
        lanes = slice(start, start + wide)
        wide_back[:, lanes] = dot_nt(grads[...], out_weight[lanes, :])

    stores += started(
        [
            (gate_raw, homes[1].at[here, :]),
            (mixer_raw, homes[2].at[here, :]),
            (small_raw, homes[3].at[here, :]),
        ],
        store_sems,
        1,
    )

    def chunk(index, carry):
        first_row = pl.multiple_of(index * CHUNK, CHUNK)
        at = pl.ds(first_row, CHUNK)
        first_token = block * rows + index * CHUNK
        chunk_first = first_token.astype(f32)
        row_place = place(0).astype(f32) + chunk_first
        lane_place = place(1).astype(f32) + chunk_first
        start_column = stand(marks[0:1, pl.ds(pl.multiple_of(block * rows + index * CHUNK, CHUNK), CHUNK)])
        age = row_place - start_column
        kept = [(age >= k).astype(f32) for k in range(1, 4)]
        for j in range(2):
            lanes = slice(j * LANES, (j + 1) * LANES)
            pre = conv_pre(
                state_raw[pl.ds(first_row, CHUNK + 8), lanes], state_chan, lanes, kept
            )
            sigma = sigmoid(pre)
            act = pre * sigma
            states[at, lanes] = act.astype(bf16)
            state_slope[at, lanes] = (sigma + act * (1.0 - sigma)).astype(bf16)
        state_b = states[at, :LANES]
        state_c = states[at, LANES:]
        scores = jnp.where(
            (lane_place <= row_place) & (lane_place >= start_column),
            dot_nt(state_c, state_b),
            0.0,
        )
        _, step_size, levels = step_levels(small_raw[at, 256:].astype(f32), heads)
        levels_row = jnp.transpose(levels)
        last_start = (starts[first_token + CHUNK - 1] - sequence).astype(f32)
        carried = (last_start < chunk_first).astype(f32)
        ends = (row_place >= last_start).astype(f32)
        begins = (start_column < chunk_first).astype(f32)
        state_low = state[...].astype(bf16)
        kept_states[index] = state_low
        carried_out[...] = dot(state_c, state_low)
        by_head[...] = spread_heads(step_size, levels, begins, ends, owners)
        low = low_lanes()
        squares = jnp.zeros((CHUNK, LANES), f32)
        crosses = jnp.zeros((CHUNK, LANES), f32)
        for j in range(inner // LANES):
            lanes = slice(j * LANES, (j + 1) * LANES)
            pre = conv_pre(raw[pl.ds(first_row, CHUNK + 8), lanes], chan, lanes, kept)
            sigma = sigmoid(pre)
            act = pre * sigma
            value = act.astype(bf16)
            mixer_in[at, lanes] = value
            slope[at, lanes] = (sigma + act * (1.0 - sigma)).astype(bf16)
            value = value.astype(f32)
            weights = []
            for h in (2 * j, 2 * j + 1):
                level = spread(levels[:, h : h + 1])
                damping = jnp.exp2(jnp.minimum(level - levels_row[h : h + 1, :], 0.0))
                weights.append((scores * damping).astype(bf16))
            step_pair = by_head[0:CHUNK, lanes]
            beginning = by_head[CHUNK : 2 * CHUNK, lanes]
            ending = by_head[2 * CHUNK : 3 * CHUNK, lanes]
            last = by_head[3 * CHUNK : 3 * CHUNK + 1, lanes]
            stepped = value * step_pair
            stacked = jnp.concatenate(
                [jnp.where(low, stepped, 0.0), jnp.where(low, 0.0, stepped)], axis=0
            ).astype(bf16)
            result = dot(jnp.concatenate(weights, axis=1), stacked)
            result += beginning * carried_out[:, lanes]
            damped[:, lanes] = (stepped * ending).astype(bf16)
            state[:, lanes] = state[:, lanes] * (carried * last)
            result += chan[5:6, lanes] * value
            mixed[at, lanes] = result
            gate = gate_raw[at, lanes].astype(f32)
            gated = result * (gate * sigmoid(gate))
            squares += gated * gated
            gained = gated * chan[6:7, lanes]
            gated_low[at, lanes] = gained.astype(bf16)
            out_back = wide_back[at, lanes]
            back[at, lanes] = out_back.astype(bf16)
            crosses += out_back * gained
        state[...] += dot_tn(state_b, damped[...])
        sums[0:1, at] = jnp.sum(jnp.transpose(squares), axis=0, keepdims=True)
        sums[1:2, at] = jnp.sum(jnp.transpose(crosses), axis=0, keepdims=True)
        return carry

    lax.fori_loop(0, rows // CHUNK, chunk, 0)
    stores += started(
        [
            (mixer_in, homes[4].at[here, :]),
            (slope, homes[5].at[here, :]),
            (states, homes[6].at[here, :]),
            (state_slope, homes[7].at[here, :]),
            (mixed, homes[8].at[here, :]),
            (back, homes[9].at[here, :]),
            (kept_states, homes[10].at[pl.ds(block * (rows // CHUNK), rows // CHUNK)]),
        ],
        store_sems,
        4,
    )
    if project:
        for start in range(0, width, 512):
            lanes = slice(start, start + 512)
            partial[:, lanes] = dot(gated_low[...], out_weight[:, lanes]).astype(bf16)
    else:
        partial[...] = gated_low[...]
    halo_out[:, :inner] = raw[rows : rows + 8, :]
    halo_out[:, inner:] = state_raw[rows : rows + 8, :]
    settle(stores)


def forward(block, starts, marks, tokens, grads, params, carry, earlier, after, project):
    gain, gate_weight, input_weight, small_weight, *tables, out_weight = params
    tables = [gain, *tables]
    weights = [input_weight, gate_weight, small_weight, out_weight]
    length, width = tokens.shape
    inner = gate_weight.shape[1]
    chunks = ROWS // CHUNK
    stored = [
        (width, bf16),
        (inner, bf16),
        (inner, bf16),
        (384, bf16),
        (inner, bf16),
        (inner, bf16),
        (256, bf16),
        (256, bf16),
        (inner, f32),
        (inner, bf16),
    ]
    out_shape = [jax.ShapeDtypeStruct((length, columns), kind) for columns, kind in stored]
    out_shape += [jax.ShapeDtypeStruct((length // CHUNK, LANES, inner), bf16)]
    shared = len(out_shape)
    own = [
        ((ROWS, width if project else inner), bf16),
        ((2, ROWS), f32),
        ((LANES, inner), f32),
        ((8, inner + 256), f32),
    ]
    out_shape += [jax.ShapeDtypeStruct(shape, kind) for shape, kind in own]
    in_specs = [SMEM, whole(marks.shape)] + [HBM] * 6 + wholes(tables) + wholes(carry)
    operands = [starts, marks, tokens, grads, *weights, *tables, *carry]
    aliases = {}
    if earlier is not None:
        aliases = {len(operands) + k: k for k in range(shared)}
        in_specs += [HBM] * shared
        operands += list(earlier)
    operands += list(after)
    in_specs += [ANY] * len(after)
    outs = pl.pallas_call(
        functools.partial(
            forward_kernel,
            block=block,
            first=not carry,
            unread=len(aliases) + len(after),
            project=project,
        ),
        grid=(1,),
        in_specs=in_specs,
        out_specs=[HBM] * shared + [whole(shape) for shape, _ in own],
        out_shape=out_shape,
        scratch_shapes=[
            pltpu.VMEM((ROWS, width), bf16),
            pltpu.VMEM((ROWS, width), bf16),
            *[pltpu.VMEM((ROWS, columns), kind) for columns, kind in stored],
            pltpu.VMEM((chunks, LANES, inner), bf16),
            pltpu.VMEM((ROWS + 8, inner), f32),
            pltpu.VMEM((ROWS + 8, 256), f32),
            pltpu.VMEM((ROWS, inner), bf16),
            pltpu.VMEM((ROWS, inner), f32),
            *[pltpu.VMEM(item.shape, bf16) for item in weights],
            pltpu.VMEM((CHUNK, inner), bf16),
            pltpu.VMEM((CHUNK, inner), f32),
            pltpu.VMEM((3 * CHUNK + 8, inner), f32),
            pltpu.SemaphoreType.DMA((6,)),
            pltpu.SemaphoreType.DMA((11,)),
        ],
        input_output_aliases=aliases,
        compiler_params=pltpu.CompilerParams(vmem_limit_bytes=VMEM_BYTES),
        cost_estimate=BRIEF,
        name="forward_mix",
    )(*operands)
    saved, (partial, sums, *carry) = outs[:shared], outs[shared:]
    return saved, partial, sums, carry


def project_kernel(*refs, count, unread):
    lows, out_weight, outs = refs[:count], refs[count], refs[count + 1 + unread :]
    for low, out in zip(lows, outs):
        for start in range(0, out.shape[1], 512):
            lanes = slice(start, start + 512)
            out[:, lanes] = dot(low[...], out_weight[:, lanes]).astype(bf16)


def project_rows(lows, out_weight, after):
    width = out_weight.shape[1]
    half = lambda columns: pl.BlockSpec((ROWS // 2, columns), lambda i: (i, 0))
    return pl.pallas_call(
        functools.partial(project_kernel, count=len(lows), unread=len(after)),
        grid=(2,),
        in_specs=[half(low.shape[1]) for low in lows]
        + [whole(out_weight.shape)]
        + [ANY] * len(after),
        out_specs=[half(width)] * len(lows),
        out_shape=[jax.ShapeDtypeStruct((low.shape[0], width), bf16) for low in lows],
        compiler_params=compiler_params(),
        cost_estimate=BRIEF,
        name="project_rows",
    )(*lows, out_weight, *after)


def compiler_params():
    return pltpu.CompilerParams(
        dimension_semantics=("arbitrary",), vmem_limit_bytes=VMEM_BYTES
    )


def gate_kernel(total_inner, sums, mixed, gate_raw, back, chan, *rest, unread):
    grad_low, gate_low, gate_out, gain_sums = rest[unread:]
    inner = chan.shape[1]

    @pl.when(pl.program_id(0) == 0)
    def _():
        gain_sums[...] = jnp.zeros_like(gain_sums)

    def chunk(index, carry):
        at = pl.ds(pl.multiple_of(index * CHUNK, CHUNK), CHUNK)
        inverse = lax.rsqrt(sums[0:1, at] / total_inner + epsilon)
        rms = stand(inverse)
        pull = stand(inverse * inverse * inverse * (sums[1:2, at] / total_inner))
        for j in range(inner // LANES):
            lanes = slice(j * LANES, (j + 1) * LANES)
            gate = gate_raw[at, lanes].astype(f32)
            sigma = sigmoid(gate)
            gate_act = gate * sigma
            mix = mixed[at, lanes]
            gated = mix * gate_act
            unit = gated * rms
            out_back = back[at, lanes].astype(f32)
            gate_gain = chan[6:7, lanes]
            gain_sums[:, lanes] += fold(out_back * unit)
            gated_grad = rms * (out_back * gate_gain) - pull * gated
            gate_low[at, lanes] = (
                gated_grad * mix * (sigma + gate_act * (1.0 - sigma))
            ).astype(bf16)
            gate_out[at, lanes] = (unit * gate_gain).astype(bf16)
            grad_low[at, lanes] = (gated_grad * gate_act).astype(bf16)
        return carry

    lax.fori_loop(0, mixed.shape[0] // CHUNK, chunk, 0)


def gate_grads(total_inner, sums, mixed, gate_raw, back, chan, after):
    length, inner = mixed.shape
    rows_of = lambda columns: pl.BlockSpec((ROWS, columns), lambda i: (i, 0))
    return pl.pallas_call(
        functools.partial(gate_kernel, total_inner, unread=len(after)),
        grid=(length // ROWS,),
        in_specs=[
            pl.BlockSpec((2, ROWS), lambda i: (0, i)),
            rows_of(inner),
            rows_of(inner),
            rows_of(inner),
            whole((8, inner)),
            *[ANY] * len(after),
        ],
        out_specs=[rows_of(inner)] * 3 + [held((8, inner))],
        out_shape=[jax.ShapeDtypeStruct((length, inner), bf16)] * 3
        + [jax.ShapeDtypeStruct((8, inner), f32)],
        compiler_params=compiler_params(),
        cost_estimate=BRIEF,
        name="gate_grads",
    )(sums, mixed, gate_raw, back, chan, *after)


def backward_kernel(
    starts,
    marks,
    gain,
    chan,
    state_chan,
    heads,
    owners,
    *rest,
    block,
    first,
    unread,
    parts,
):
    sources, rest = rest[:14], rest[14:]
    if not first:
        earlier, rest = rest[:6], rest[6:]
    rest = rest[unread:]
    mixer_home, small_home = rest[:2]
    partials, rest = rest[2 : 2 + parts], rest[2 + parts :]
    results, rest = rest[:6], rest[6:]
    state_grad, halo_out, chan_sums, state_sums, head_sums, gain_sums = results
    buffers, rest = rest[:14], rest[14:]
    (
        mixed,
        mixer_grad,
        mixer_in,
        slope,
        small_raw,
        states,
        state_slope,
        kept_states,
        mixer_raw,
        gate_low,
        gate_weight,
        input_weight,
        state_weight,
        tokens,
    ) = buffers
    (
        mixer_low,
        small_low,
        pre_grad,
        state_pre,
        ends_low,
        begins_low,
        normed_grad,
        picks,
        pairs,
        carried_back,
        by_head,
        load_sems,
        store_sems,
    ) = rest
    rows, width = tokens.shape
    inner = gate_weight.shape[1]
    chunks = rows // CHUNK
    half = rows // 2
    here = pl.ds(block * rows, rows)
    sequence = lax.axis_index("dp") * starts.shape[0]

    def part_of(number):
        pairs = [
            (source.at[pl.ds(block * rows + number * half, half), :], buffer.at[pl.ds(number * half, half), :])
            for source, buffer in zip(sources[:7], buffers[:7])
        ]
        count = chunks // 2
        pairs.append(
            (
                sources[7].at[pl.ds(block * chunks + number * count, count)],
                kept_states.at[pl.ds(number * count, count)],
            )
        )
        return pairs

    soon = started(part_of(1), load_sems)
    second = started(part_of(0), load_sems, 8)
    late = started(
        [
            (source if source.shape[0] == buffer.shape[0] else source.at[here, :], buffer)
            for source, buffer in zip(sources[8:], buffers[8:])
        ],
        load_sems,
        16,
    )
    for j in range(inner // LANES):
        column = lax.broadcasted_iota(jnp.int32, (2 * LANES, LANES), 1)
        line = lax.broadcasted_iota(jnp.int32, (2 * LANES, LANES), 0) % LANES
        owner = 2 * j + (line >= LANES // 2).astype(jnp.int32)
        picks[j] = (column == owner).astype(bf16)
        beyond_half = lax.broadcasted_iota(jnp.int32, (2 * LANES, LANES), 0) >= LANES
        pairs[j] = (column == owner + jnp.where(beyond_half, LANES // 2, 0)).astype(bf16)
    if first:
        for result in results:
            result[...] = jnp.zeros_like(result)
        pre_grad[rows : rows + 8, :] = jnp.zeros((8, inner), f32)
        state_pre[rows : rows + 8, :] = jnp.zeros((8, 256), f32)
    else:
        for result, value in zip(results, earlier):
            result[...] = value[...]
        pre_grad[rows : rows + 8, :] = earlier[1][:, :inner]
        state_pre[rows : rows + 8, :] = earlier[1][:, inner:]
    settle(soon)

    def chunk(turn, carry):
        index = chunks - 1 - turn

        @pl.when(turn == chunks // 2)
        def _():
            settle(second)

        first_row = pl.multiple_of(index * CHUNK, CHUNK)
        at = pl.ds(first_row, CHUNK)
        first_token = block * rows + index * CHUNK
        chunk_first = first_token.astype(f32)
        row_place = place(0).astype(f32) + chunk_first
        lane_place = place(1).astype(f32) + chunk_first
        start_row = marks[0:1, pl.ds(pl.multiple_of(block * rows + index * CHUNK, CHUNK), CHUNK)]
        start_column = stand(start_row)
        seen = (row_place <= lane_place) & (row_place >= start_row)
        last_start = (starts[first_token + CHUNK - 1] - sequence).astype(f32)
        carried = (last_start < chunk_first).astype(f32)
        ends = (row_place >= last_start).astype(f32)
        begins = (start_column < chunk_first).astype(f32)
        state_b = states[at, :LANES]
        state_c = states[at, LANES:]
        scores = jnp.where(seen, dot_nt(state_b, state_c), 0.0)
        step_raw = small_raw[at, 256:].astype(f32)
        field, step_size, levels = step_levels(step_raw, heads)
        levels_row = jnp.transpose(levels)
        state_low = state_grad[...].astype(bf16)
        carried_back[...] = dot(state_b, state_low)
        by_head[...] = spread_heads(step_size, levels, begins, ends, owners)
        low = low_lanes()
        score_grad = jnp.zeros((CHUNK, CHUNK), f32)
        level_grad = jnp.zeros((CHUNK + 8, LANES), f32)
        step_grad = jnp.zeros((CHUNK, LANES), f32)
        for j in range(inner // LANES):
            lanes = slice(j * LANES, (j + 1) * LANES)
            pick = picks[j]
            mix = mixed[at, lanes]
            grad = mixer_grad[at, lanes].astype(f32)
            value = mixer_in[at, lanes].astype(f32)
            skip = chan[5:6, lanes]
            chan_sums[0:8, lanes] += fold(grad * value)
            step_pair = by_head[0:CHUNK, lanes]
            beginning = by_head[CHUNK : 2 * CHUNK, lanes]
            ending = by_head[2 * CHUNK : 3 * CHUNK, lanes]
            last = by_head[3 * CHUNK : 3 * CHUNK + 1, lanes]
            stepped = value * step_pair
            stepped_low = stepped.astype(bf16)
            stacked = jnp.concatenate(
                [jnp.where(low, grad, 0.0), jnp.where(low, 0.0, grad)], axis=0
            ).astype(bf16)
            cells = dot_nt(stepped_low, stacked)
            weights = []
            for k in range(2):
                h = 2 * j + k
                level = spread(levels[:, h : h + 1])
                damping = jnp.exp2(jnp.minimum(levels_row[h : h + 1, :] - level, 0.0))
                weights.append((scores * damping).astype(bf16))
                score_grad += cells[:, k * CHUNK : (k + 1) * CHUNK] * damping
            within = dot(jnp.concatenate(weights, axis=1), stacked)
            beyond = ending * carried_back[:, lanes]
            value_grad = within + beyond
            ends_low[:, lanes] = (stepped * ending).astype(bf16)
            begins_low[:, lanes] = (grad * beginning).astype(bf16)
            behind = state_grad[:, lanes]
            crossing = fold(behind * kept_states[index, :, lanes].astype(f32))
            state_grad[:, lanes] = behind * (carried * last)
            rows_flow = grad * (mix - skip * value) - stepped_low.astype(f32) * within
            level_grad += dot(halves(jnp.concatenate([rows_flow, crossing], axis=0)), pick)
            both = jnp.concatenate([value * value_grad, stepped * beyond], axis=1)
            step_grad += dot(both.astype(bf16), pairs[j])
            pre_grad[at, lanes] = (step_pair * value_grad + skip * grad) * slope[
                at, lanes
            ].astype(f32)
        state_grad[...] += dot_tn(state_c, begins_low[...])
        score_low = jnp.where(seen, score_grad, 0.0).astype(bf16)
        state_pre[at, :LANES] = (
            dot(score_low, state_c) + dot_nt(ends_low[...], state_low)
        ) * state_slope[at, :LANES].astype(f32)
        state_pre[at, LANES:] = (
            dot_tn(score_low, state_b) + dot_nt(begins_low[...], kept_states[index])
        ) * state_slope[at, LANES:].astype(f32)
        sums_over = jnp.concatenate(
            [(place(0) <= place(1)).astype(bf16), (place(0) > place(1)).astype(bf16)], axis=1
        )
        inter_grad = pltpu.roll(step_grad, LANES // 2, 1)
        flows = jnp.concatenate([halves(level_grad[:CHUNK]), halves(inter_grad)], axis=0)
        reach = dot(sums_over, flows)
        across = jnp.sum(level_grad[CHUNK:], axis=0, keepdims=True) * (
            carried * jnp.exp2(levels[CHUNK - 1 : CHUNK, :])
        )
        reach = reach[:, :LANES] + reach[:, LANES:] + across
        own = (place(1) < LANES // 2).astype(f32)
        reach = reach * own
        step_grad = step_grad * own
        rates = heads[2:3, :]
        field_grad = (step_grad + reach * rates) * sigmoid(field)
        small_low[at, 256:] = field_grad.astype(bf16)
        head_sums[0:8, :] += fold(field_grad)
        head_sums[8:16, :] += fold(reach * step_size * rates)
        return carry

    lax.fori_loop(0, chunks, chunk, 0)
    settle(late)

    def unconv(index, carry):
        first_row = pl.multiple_of(index * CHUNK, CHUNK)
        at = pl.ds(first_row, CHUNK)
        left = stand(marks[1:2, pl.ds(pl.multiple_of(block * rows + index * CHUNK, CHUNK), CHUNK)])
        kept = [(left >= k).astype(f32) for k in range(1, 4)]

        def tile(window, value, taps, lanes, totals, line):
            own = window[:CHUNK]
            total = taps[0:1, lanes] * own
            totals[line : line + 8, lanes] += fold(value * own)
            for k in range(1, 4):
                moved = kept[k - 1] * window[k : k + CHUNK]
                total += taps[k : k + 1, lanes] * moved
                totals[line + 8 * k : line + 8 * k + 8, lanes] += fold(value * moved)
            totals[line + 32 : line + 40, lanes] += fold(own)
            return total.astype(bf16)

        for j in range(inner // LANES):
            lanes = slice(j * LANES, (j + 1) * LANES)
            mixer_low[at, lanes] = tile(
                pre_grad[pl.ds(first_row, CHUNK + 8), lanes],
                mixer_raw[at, lanes].astype(f32),
                chan,
                lanes,
                chan_sums,
                8,
            )
        for j in range(2):
            lanes = slice(j * LANES, (j + 1) * LANES)
            small_low[at, lanes] = tile(
                state_pre[pl.ds(first_row, CHUNK + 8), lanes],
                small_raw[at, lanes].astype(f32),
                state_chan,
                lanes,
                state_sums,
                0,
            )
        return carry

    lax.fori_loop(0, chunks, unconv, 0)
    stores = started(
        [(mixer_low, mixer_home.at[here, :]), (small_low, small_home.at[here, :])], store_sems
    )
    for start in range(0, width, 256):
        lanes = slice(start, start + 256)
        normed_grad[:, lanes] = (
            dot_nt(gate_low[...], gate_weight[lanes, :])
            + dot_nt(mixer_low[...], input_weight[lanes, :])
            + dot_nt(small_low[...], state_weight[lanes, :])
        )

    def unnorm(part, index, carry):
        at = pl.ds(pl.multiple_of(index * 16, 16), 16)
        from_row = pl.ds(pl.multiple_of(part * part_rows + index * 16, 16), 16)
        values = tokens[from_row, :].astype(f32)
        inverse = lax.rsqrt(jnp.mean(values * values, axis=-1, keepdims=True) + epsilon)
        unit = values * inverse
        grad = normed_grad[from_row, :]
        gain_sums[...] += fold(grad * unit)
        grad = grad * gain[...]
        out = partials[part]
        out[at, :] = (
            inverse * (grad - unit * jnp.mean(grad * unit, axis=-1, keepdims=True))
        ).astype(bf16)
        return carry

    part_rows = partials[0].shape[0]
    for part in range(len(partials)):
        lax.fori_loop(0, part_rows // 16, functools.partial(unnorm, part), 0, unroll=2)
    halo_out[:, :inner] = pre_grad[0:8, :]
    halo_out[:, inner:] = state_pre[0:8, :]
    settle(stores)


def backward(block, starts, marks, tokens, params, saved, grads, carry, earlier, after, parts):
    gain, gate_weight, input_weight, small_weight, *tables, _ = params
    tables = [gain, *tables]
    length, width = tokens.shape
    inner = gate_weight.shape[1]
    chunks = ROWS // CHUNK
    (gate_raw, mixer_raw, small_raw, mixer_in, slope, states, state_slope, mixed, _, kept) = saved
    mixer_grad, gate_low = grads
    sources = [
        mixed,
        mixer_grad,
        mixer_in,
        slope,
        small_raw,
        states,
        state_slope,
        kept,
        mixer_raw,
        gate_low,
        gate_weight,
        input_weight,
        small_weight,
        tokens,
    ]
    operands = [starts, marks, *tables, *sources, *carry]
    in_specs = [SMEM, *wholes([marks, *tables]), *[HBM] * len(sources), *wholes(carry)]
    aliases = {}
    if earlier is not None:
        aliases = {len(operands) + k: k for k in range(2)}
        in_specs += [HBM] * 2
        operands += list(earlier)
    operands += list(after)
    in_specs += [ANY] * len(after)
    results = [
        (LANES, inner),
        (8, inner + 256),
        (48, inner),
        (40, 256),
        (16, LANES),
        (8, width),
    ]
    outs = pl.pallas_call(
        functools.partial(
            backward_kernel,
            block=block,
            first=not carry,
            unread=len(aliases) + len(after),
            parts=parts,
        ),
        grid=(1,),
        in_specs=in_specs,
        out_specs=[HBM] * 2
        + [whole((ROWS // parts, width))] * parts
        + [whole(shape) for shape in results],
        out_shape=[
            jax.ShapeDtypeStruct((length, inner), bf16),
            jax.ShapeDtypeStruct((length, 384), bf16),
            *[jax.ShapeDtypeStruct((ROWS // parts, width), bf16)] * parts,
            *[jax.ShapeDtypeStruct(shape, f32) for shape in results],
        ],
        scratch_shapes=[
            *[
                pltpu.VMEM((chunks, LANES, inner), bf16)
                if source.ndim == 3
                else pltpu.VMEM(
                    (ROWS if source.shape[0] == length else source.shape[0], source.shape[1]),
                    source.dtype,
                )
                for source in sources
            ],
            pltpu.VMEM((ROWS, inner), bf16),
            pltpu.VMEM((ROWS, 384), bf16),
            pltpu.VMEM((ROWS + 8, inner), f32),
            pltpu.VMEM((ROWS + 8, 256), f32),
            pltpu.VMEM((CHUNK, inner), bf16),
            pltpu.VMEM((CHUNK, inner), bf16),
            pltpu.VMEM((ROWS, width), f32),
            *[pltpu.VMEM((inner // LANES, 2 * LANES, LANES), bf16)] * 2,
            pltpu.VMEM((CHUNK, inner), f32),
            pltpu.VMEM((3 * CHUNK + 8, inner), f32),
            pltpu.SemaphoreType.DMA((22,)),
            pltpu.SemaphoreType.DMA((2,)),
        ],
        input_output_aliases=aliases,
        compiler_params=pltpu.CompilerParams(vmem_limit_bytes=VMEM_BYTES),
        cost_estimate=LONG,
        name="backward_mix",
    )(*operands)
    return outs[:2], outs[2 : 2 + parts], outs[2 + parts :]


def pack(packed, chan_sums, gate_sums, head_sums, state_sums, gain_sums, small_total):
    inner = chan_sums.shape[1]
    packed[...] = jnp.zeros_like(packed)
    total = lambda values: jnp.sum(values, axis=0, keepdims=True)
    for k in range(6):
        packed[k : k + 1, :inner] = total(chan_sums[8 * k : 8 * k + 8, :])
    packed[6:7, :inner] = total(gate_sums[...])
    for k in range(2):
        packed[7:8, k * LANES : (k + 1) * LANES] = total(head_sums[8 * k : 8 * k + 8, :])
    for k in range(5):
        packed[8 + k : 9 + k, :256] = total(state_sums[8 * k : 8 * k + 8, :])
    packed[13:14, :] = total(gain_sums[...])
    for start in range(0, packed.shape[1], LANES):
        lanes = slice(start, start + LANES)
        packed[16:32, lanes] = jnp.transpose(small_total[lanes, 256:])[0:16]


def weight_kernel(left, *rest, rights, unread, packs):
    right, rest = rest[:rights], rest[rights:]
    sums, rest = rest[:packs], rest[packs + unread :]
    outs, totals = rest[: rights + bool(packs)], rest[rights + bool(packs) :]
    step = pl.program_id(0)

    @pl.when(step == 0)
    def _():
        for total in totals:
            total[...] = jnp.zeros_like(total)

    for start in range(0, left.shape[1], 256):
        columns = slice(start, start + 256)
        for item, total in zip(right, totals):
            total[columns, :] += dot_tn(left[:, columns], item[...])

    @pl.when(step == pl.num_programs(0) - 1)
    def _():
        if packs:
            packed = totals[rights]
            pack(packed, *sums, totals[rights - 1])
            outs[rights][...] = packed[...].astype(bf16)
        for out, total in zip(outs[:rights], totals):
            out[...] = total[:, : out.shape[1]].astype(bf16)


def weight_grads(left, rights, after, sums=()):
    length, height = left.shape
    rows_of = lambda columns: pl.BlockSpec((ROWS, columns), lambda i: (i, 0))
    shapes = [(height, item.shape[1]) for item in rights]
    outs, scratch = list(shapes), list(shapes)
    if sums:
        outs[-1] = (height, 256)
        outs.append((32, height))
        scratch.append((32, height))
    return pl.pallas_call(
        functools.partial(
            weight_kernel, rights=len(rights), unread=len(after), packs=len(sums)
        ),
        grid=(length // ROWS,),
        in_specs=[rows_of(height)]
        + [rows_of(item.shape[1]) for item in rights]
        + wholes(sums)
        + [ANY] * len(after),
        out_specs=[held(shape) for shape in outs],
        out_shape=[jax.ShapeDtypeStruct(shape, bf16) for shape in outs],
        scratch_shapes=[pltpu.VMEM(shape, f32) for shape in scratch],
        compiler_params=compiler_params(),
        cost_estimate=BRIEF,
        name="weight_grads",
    )(left, *rights, *sums, *after)


def land_kernel(take, total_home, moved_home, *rest, mode, unread):
    out_home, total, moved, out, load_sems, store_sems = rest[unread:]
    tiles = total.shape[0] // CHUNK
    part = [pl.ds(k * CHUNK, CHUNK) for k in range(tiles)]
    loads = [
        started(
            [
                (total_home.at[part[k], :], total.at[part[k], :]),
                (moved_home.at[part[k], :], moved.at[part[k], :]),
            ],
            load_sems,
            2 * k,
        )
        for k in range(tiles)
    ]
    stores = []
    for k in range(tiles):
        settle(loads[k])
        at = slice(k * CHUNK, (k + 1) * CHUNK)
        if mode == "add":
            out[at, :] = total[at, :] + moved[at, :]
        else:
            out[at, :] = jnp.where(take[0] > 0, moved[at, :], total[at, :])
        stores += started([(out.at[part[k], :], out_home.at[part[k], :])], store_sems, k)
    settle(stores)


def finish_kernel(
    take, total_home, moved_home, base_home, sums, *rest, adds, inner, row, unread
):
    out_home, total, moved, base, out, load_sems, store_sems = rest[unread:]
    rows = total.shape[0]
    tiles = rows // CHUNK
    at_home = lambda k: pl.ds(row + k * CHUNK, CHUNK)
    at_here = lambda k: pl.ds(k * CHUNK, CHUNK)

    def run(pairs):
        loads = [
            started(
                [(home.at[at_here(k), :], here.at[at_here(k), :]) for home, here in pairs]
                + [(base_home.at[at_home(k), :], base.at[at_here(k), :])],
                load_sems,
                3 * k,
            )
            for k in range(tiles)
        ]
        stores = []
        for k in range(tiles):
            at = slice(k * CHUNK, (k + 1) * CHUNK)
            if inner:
                scale = stand(
                    lax.rsqrt(
                        sums[0:1, row + k * CHUNK : row + (k + 1) * CHUNK] / inner + epsilon
                    )
                )
            settle(loads[k])
            for start in range(0, total.shape[1], LANES):
                lanes = slice(start, start + LANES)
                value = pairs[0][1][at, lanes].astype(f32)
                for _, here in pairs[1:]:
                    value += here[at, lanes].astype(f32)
                if inner:
                    value = value * scale
                out[at, lanes] = (value + base[at, lanes].astype(f32)).astype(bf16)
            stores += started(
                [(out.at[at_here(k), :], out_home.at[at_home(k), :])], store_sems, k
            )
        settle(stores)

    if adds:
        run([(moved_home, moved), (total_home, total)])
        return

    @pl.when(take[0] > 0)
    def _():
        run([(moved_home, moved)])

    @pl.when(take[0] <= 0)
    def _():
        run([(total_home, total)])


def land(take, total, moved, mode, after):
    rows, width = total.shape
    return pl.pallas_call(
        functools.partial(land_kernel, mode=mode, unread=len(after)),
        in_specs=[SMEM, HBM, HBM] + [ANY] * len(after),
        out_specs=HBM,
        out_shape=jax.ShapeDtypeStruct((rows, width), bf16),
        scratch_shapes=[
            *[pltpu.VMEM((rows, width), bf16)] * 3,
            pltpu.SemaphoreType.DMA((2 * rows // CHUNK,)),
            pltpu.SemaphoreType.DMA((rows // CHUNK,)),
        ],
        compiler_params=pltpu.CompilerParams(vmem_limit_bytes=VMEM_BYTES),
        cost_estimate=BRIEF,
        name="line_land",
    )(take, total, moved, *after)


def turn_kernel(take, total_home, moved_home, next_home, *rest, unread):
    out_home, total, moved, out, load_sems, store_sems = rest[unread:]
    land_refs = (out_home, total, moved, out, load_sems, store_sems)

    @pl.when(take[0] > 0)
    def _():
        tiles = out.shape[0] // CHUNK
        part = [pl.ds(k * CHUNK, CHUNK) for k in range(tiles)]
        loads = started([(next_home.at[at, :], out.at[at, :]) for at in part], load_sems)
        stores = []
        for k, at in enumerate(part):
            settle(loads[k : k + 1])
            stores += started([(out.at[at, :], out_home.at[at, :])], store_sems, k)
        settle(stores)

    @pl.when(take[0] <= 0)
    def _():
        land_kernel(take, total_home, moved_home, *land_refs, mode="add", unread=0)


def turn(take, total, moved, following, after):
    rows, width = total.shape
    return pl.pallas_call(
        functools.partial(turn_kernel, unread=len(after)),
        in_specs=[SMEM, HBM, HBM, HBM] + [ANY] * len(after),
        out_specs=HBM,
        out_shape=jax.ShapeDtypeStruct((rows, width), bf16),
        scratch_shapes=[
            *[pltpu.VMEM((rows, width), bf16)] * 3,
            pltpu.SemaphoreType.DMA((2 * rows // CHUNK,)),
            pltpu.SemaphoreType.DMA((rows // CHUNK,)),
        ],
        compiler_params=pltpu.CompilerParams(vmem_limit_bytes=VMEM_BYTES),
        cost_estimate=BRIEF,
        name="line_turn",
    )(take, total, moved, following, *after)


def finish(take, total, moved, adds, base, sums, inner, row, earlier, after, cost):
    rows, width = total.shape
    operands = [take, total, moved, base, sums]
    in_specs = [SMEM, HBM, HBM, HBM, whole(sums.shape)]
    aliases = {}
    if earlier is not None:
        aliases = {len(operands): 0}
        operands += [earlier]
        in_specs += [HBM]
    after = [item for item in after if item is not earlier]
    operands += after
    in_specs += [ANY] * len(after)
    return pl.pallas_call(
        functools.partial(
            finish_kernel,
            adds=adds,
            inner=inner,
            row=row,
            unread=len(aliases) + len(after),
        ),
        in_specs=in_specs,
        out_specs=HBM,
        grid=(1,),
        out_shape=jax.ShapeDtypeStruct(base.shape, bf16),
        scratch_shapes=[
            *[pltpu.VMEM((rows, width), bf16)] * 4,
            pltpu.SemaphoreType.DMA((3 * rows // CHUNK,)),
            pltpu.SemaphoreType.DMA((rows // CHUNK,)),
        ],
        input_output_aliases=aliases,
        compiler_params=pltpu.CompilerParams(vmem_limit_bytes=VMEM_BYTES),
        cost_estimate=cost,
        name="line_finish",
    )(*operands)


class Line:
    def __init__(self, members, me):
        middle = members // 2
        self.steps = [
            ("add", [(near, near + 1), (members - 1 - near, members - 2 - near)], near)
            for near in range(middle - 1)
        ]
        self.steps.append(("add", [(middle - 1, middle), (middle, middle - 1)], 0))
        self.steps += [
            ("take", [(near + 1, near), (members - 2 - near, members - 1 - near)], near)
            for near in reversed(range(middle - 1))
        ]
        self.takes = [
            ((me == near) | (me == members - 1 - near)).astype(jnp.int32)[None]
            for _, _, near in self.steps
        ]
        self.flying = [[] for _ in self.steps]
        self.outs = {}
        self.extra = []

    def push(self, total, name, row):
        self.launch(0, total, name, row)

    def launch(self, step, total, name, row):
        moved = lax.ppermute(total, "tensor", self.steps[step][1])
        self.flying[step].append((total, moved, name, row))

    def tick(self, ending, after, first=1, then=1, last=1):
        ready = []
        for step, queue in enumerate(self.flying):
            count = last if step == len(self.flying) - 1 else then if step else first
            for _ in range(min(len(queue), count)):
                ready.append((step, queue.pop(0)))
        for step, (total, moved, name, row) in ready:
            mode = self.steps[step][0]
            if step < len(self.steps) - 1:
                total = land(self.takes[step], total, moved, mode, after)
                self.launch(step + 1, total, name, row)
                after = [total]
            else:
                base, sums, inner = ending[name]
                out = finish(
                    self.takes[step],
                    total,
                    moved,
                    mode == "add",
                    base,
                    sums,
                    inner,
                    row,
                    self.outs.get(name),
                    after,
                    BRIEF,
                )
                self.outs[name] = out
                after = [out]
        return after

    def busy(self):
        return any(self.flying)

    def inward(self, after):
        return self.tick({}, after, then=0, last=0)

    def outward(self, ending, after):
        return self.tick(ending, after, first=0)

    def round(self, ending, after):
        return self.tick(ending, after)


class CrossLine:
    def __init__(self, me):
        self.take = ((me == 0) | (me == 3)).astype(jnp.int32)[None]
        self.crossing, self.meeting, self.ready, self.waiting = [], [], [], []
        self.arrived = None
        self.cost, self.extra = BRIEF, []
        self.outs = {}

    def push(self, total, name, row):
        self.waiting.append((total, name, row))

    def launch(self, total, inbound, outbound):
        moved = lax.ppermute(total, "tensor", [(0, 1), (1, 0), (2, 3), (3, 2)])
        self.crossing.append((moved, inbound, outbound))

    def send(self):
        item = self.waiting.pop(0)
        self.launch(item[0], item, None)

    def arrive(self, after):
        self.arrived = self.crossing.pop(0) if self.crossing else None
        if self.arrived and self.arrived[1]:
            moved, (total, name, row), _ = self.arrived
            total = land(self.take, total, moved, "add", after)
            met = lax.ppermute(total, "tensor", [(1, 2), (2, 1)])
            self.meeting.append((total, met, name, row))
            after = [total]
        return after

    def depart(self, after):
        if self.ready:
            ((total, met, name, row),) = self.ready
            following = self.waiting.pop(0) if self.waiting else None
            if following:
                total = turn(self.take, total, met, following[0], after)
            else:
                total = land(self.take, total, met, "add", after)
            self.launch(total, following, (total, name, row))
            self.ready = []
            after = [total]
        elif self.waiting:
            self.send()
        return after

    def complete(self, ending, after):
        if self.arrived and self.arrived[2]:
            moved, _, (total, name, row) = self.arrived
            base, sums, inner = ending[name]
            earlier = self.outs.get(name)
            after = [*after, *self.extra]
            out = finish(
                self.take, total, moved, False, base, sums, inner, row, earlier, after, self.cost
            )
            self.outs[name] = out
            after = [out]
        return after

    def inward(self, after):
        self.ready, self.meeting = self.meeting, []
        return self.arrive(after)

    def outward(self, ending, after):
        return self.complete(ending, self.depart(after))

    def round(self, ending, after):
        self.ready, self.meeting = self.meeting, []
        return self.complete(ending, self.arrive(self.depart(after)))

    def busy(self):
        return bool(self.crossing or self.meeting or self.waiting)


def sum_over(values, axis, size):
    parts = [values]
    for k in range(1, size):
        parts.append(lax.ppermute(values, axis, [(i, i ^ k) for i in range(size)]))
    while len(parts) > 1:
        parts = [parts[k] + parts[k + 1] for k in range(0, len(parts), 2)]
    return parts[0]


def part_kernel(me, lines, values, *rest, size, unread):
    outs = rest[unread:]
    rows = values.shape[0] // size
    for k in range(size):
        first = pl.multiple_of((me[0] ^ k) * rows, 32)
        outs[k][:rows, :] = values[pl.ds(first, rows), :]
        for j in range(lines.shape[1] // 256):
            at = slice(rows + 16 * j, rows + 16 * j + 16)
            outs[k][at, :] = lines[0:16, 256 * j : 256 * j + 256]


def join_kernel(*refs):
    parts, (line_sums, value_sums) = list(refs[:-2]), refs[-2:]
    rows = value_sums.shape[0]
    for out, at in [(value_sums, slice(0, rows)), (line_sums, slice(rows, None))]:
        totals = [part[at, :].astype(f32) for part in parts]
        while len(totals) > 1:
            totals = [totals[k] + totals[k + 1] for k in range(0, len(totals), 2)]
        out[...] = totals[0]


def sum_pieces(lines, values, axis, size, me, after):
    rows = values.shape[0] // size
    height = rows + 16 * (lines.shape[1] // 256)
    shape = jax.ShapeDtypeStruct((height, 256), bf16)
    own, *sent = pl.pallas_call(
        functools.partial(part_kernel, size=size, unread=len(after)),
        grid=(1,),
        in_specs=[SMEM, *wholes([lines, values]), *[ANY] * len(after)],
        out_specs=[whole(shape.shape)] * size,
        out_shape=[shape] * size,
        compiler_params=compiler_params(),
        cost_estimate=BRIEF,
        name="part_pieces",
    )(me[None], lines, values, *after)
    parts = [own] + [
        lax.ppermute(sent[k - 1], axis, [(i, i ^ k) for i in range(size)])
        for k in range(1, size)
    ]
    outs = [(height - rows, 256), (rows, 256)]
    line_sums, value_sums = pl.pallas_call(
        join_kernel,
        grid=(1,),
        in_specs=wholes(parts),
        out_specs=[whole(item) for item in outs],
        out_shape=[jax.ShapeDtypeStruct(item, f32) for item in outs],
        compiler_params=compiler_params(),
        cost_estimate=BRIEF,
        name="join_pieces",
    )(*parts)
    return line_sums.reshape(-1, 16, 256), value_sums


def on_device(
    block_input,
    segment_ids,
    norm_gain,
    gate_weight,
    input_weight,
    state_weight,
    step_weight,
    mixer_conv,
    mixer_shift,
    state_conv,
    state_shift,
    step_bias,
    decay_log,
    skip_gain,
    gate_gain,
    out_weight,
    out_grad,
):
    length, width = block_input.shape
    inner = gate_weight.shape[1]
    heads_local = step_weight.shape[1]
    groups = lax.axis_size("tensor")
    member = lax.axis_index("tensor")
    columns = width // groups
    total_inner = inner * groups

    gain, marks, chan, state_chan, heads, small_weight, owners = prepare(
        length,
        width,
        inner,
        (
            segment_ids,
            norm_gain,
            mixer_conv,
            mixer_shift,
            state_conv,
            state_shift,
            step_bias,
            decay_log,
            skip_gain,
            gate_gain,
            state_weight,
            step_weight,
        ),
    )
    params = (
        gain,
        gate_weight,
        input_weight,
        small_weight,
        chan,
        state_chan,
        heads,
        owners,
        out_weight,
    )
    blocks = length // ROWS
    line = CrossLine(member) if groups == 4 else Line(groups, member)
    saved, carry, after = None, [], []
    block_sums, waiting = [], []
    for block in range(blocks):
        early = block < blocks // 2
        saved, partial, sums, carry = forward(
            block,
            segment_ids,
            marks,
            block_input,
            out_grad,
            params,
            carry,
            saved,
            after,
            early,
        )
        block_sums.append(sums)
        after = [partial]
        if early:
            line.push(partial, "output", block * ROWS)
            if groups == 4:
                line.send()
        else:
            waiting.append(partial)
        if block == blocks // 2:
            after = line.inward(after)
    sums = jnp.concatenate(block_sums, axis=1)
    after = line.inward([sums])
    sums = sum_over(sums, "tensor", groups)
    ending = {
        "output": (block_input, sums, total_inner),
        "input": (out_grad, sums, 0),
    }
    partials = project_rows(waiting, out_weight, [*after, sums])
    for k, partial in enumerate(partials):
        line.push(partial, "output", (blocks // 2 + k) * ROWS)
    after = line.outward(ending, [partials[0]])
    normed, *saved = saved
    grad_low, gate_low, gate_out, gate_sums = gate_grads(
        total_inner, sums, saved[7], saved[0], saved[8], chan, after
    )
    (gate_weight_grad,) = weight_grads(normed, [gate_low], [grad_low])
    (out_weight_grad,) = weight_grads(gate_out, [out_grad], [gate_weight_grad])
    after = [out_weight_grad]
    gate_weight_grad, out_weight_grad = lax.psum((gate_weight_grad, out_weight_grad), "dp")
    after = line.round(ending, after)
    lows, carry = None, []
    for block in reversed(range(blocks)):
        lows, partials, carry = backward(
            block,
            segment_ids,
            marks,
            block_input,
            params,
            saved,
            (grad_low, gate_low),
            carry,
            lows,
            after + [gate_weight_grad, out_weight_grad] if block == 0 else after,
            1,
        )
        after = [partials[0]]
        for k, partial in enumerate(partials):
            line.push(partial, "input", block * ROWS + k * partial.shape[0])
        after = line.round(ending, after)
    mixer_low, small_low = lows
    chan_sums, state_sums, head_sums, gain_sums = carry[2:]
    weight_sums = weight_grads(
        normed,
        [mixer_low, small_low],
        after,
        (chan_sums, gate_sums, head_sums, state_sums, gain_sums),
    )
    after = [weight_sums[0]]
    input_weight_grad, state_weight_grad, packed = lax.psum(tuple(weight_sums), "dp")
    line.cost = LONG
    after = line.round(ending, after)
    line.extra = [input_weight_grad]
    after = line.round(ending, after)
    line_sums, state_weight_grad = sum_pieces(
        packed, state_weight_grad, "tensor", groups, member, after
    )
    while line.busy():
        after = line.round(ending, after)
    block_output = line.outs["output"]
    input_grad = line.outs["input"]
    packed = packed.astype(f32)
    return (
        block_output,
        input_grad,
        lax.dynamic_slice_in_dim(line_sums[:, 13].reshape(-1), member * columns, columns, 0),
        gate_weight_grad.astype(f32),
        input_weight_grad.astype(f32),
        state_weight_grad,
        packed[16 : 16 + heads_local].T,
        packed[1:5, :inner],
        packed[5, :inner],
        line_sums[0, 8:12],
        line_sums[0, 12],
        packed[7, :heads_local],
        packed[7, LANES : LANES + heads_local],
        packed[0, :inner].reshape(heads_local, inner // heads_local).sum(axis=1),
        packed[6, :inner],
        out_weight_grad.astype(f32),
    )


def solution(mesh):
    return jax.shard_map(
        on_device,
        mesh=mesh,
        in_specs=(
            P("dp", None),
            P("dp"),
            P(),
            P(None, "tensor"),
            P(None, "tensor"),
            P(),
            P(None, "tensor"),
            P(None, "tensor"),
            P("tensor"),
            P(),
            P(),
            P("tensor"),
            P("tensor"),
            P("tensor"),
            P("tensor"),
            P("tensor", None),
            P("dp", None),
        ),
        out_specs=(
            P("dp", None),
            P("dp", None),
            P("tensor"),
            P(None, "tensor"),
            P(None, "tensor"),
            P("tensor", None),
            P(None, "tensor"),
            P(None, "tensor"),
            P("tensor"),
            P(),
            P(),
            P("tensor"),
            P("tensor"),
            P("tensor"),
            P("tensor"),
            P("tensor", None),
        ),
        check_vma=False,
    )
```
